128 devices in a mesh: dp: 64 (over x, y, z_hi, core), blk: 2 (over z_lo).
Axes of the slice: x: 4, y: 4, z: 4 (z_hi: 2, z_lo: 2; z = z_hi * 2 + z_lo), core: 2. Of those that a mesh axis runs over, the one named last changes fastest.
Arguments:
- inputs: bfloat16 [64, 980, 768], P('dp', 'blk'), may hold values from -6 to 6
- segments: int32 [64, 980], P('dp'), may hold values from 0 to 4, as said below
- cotangent: bfloat16 [64, 980, 768], P('dp', 'blk'), may hold values from -6 to 6
- ln1_gain: float32 [768], replicated, may hold values from 0.5 to 1.5
- ln1_bias: float32 [768], replicated, may hold values from -1 to 1
- w_qkv: bfloat16 [768, 2304], replicated, may hold values from -0.21875 to 0.21875
- q_bias: float32 [768], replicated, may hold values from -1 to 1
- v_bias: float32 [768], replicated, may hold values from -1 to 1
- w_out: bfloat16 [768, 768], replicated, may hold values from -1.75 to 1.75
- out_bias: float32 [768], replicated, may hold values from -1 to 1
- ln2_gain: float32 [768], replicated, may hold values from 0.5 to 1.5
- ln2_bias: float32 [768], replicated, may hold values from -1 to 1
- w_fc1: bfloat16 [768, 3072], replicated, may hold values from -0.21875 to 0.21875
- fc1_bias: float32 [3072], replicated, may hold values from -1.5 to 1.5
- w_fc2: bfloat16 [3072, 768], replicated, may hold values from -0.109375 to 0.109375
- fc2_bias: float32 [768], replicated, may hold values from -1 to 1
Outputs:
- output: bfloat16 [64, 980, 768], P('dp', 'blk')
- input_grad: bfloat16 [64, 980, 768], P('dp', 'blk')
- grad_ln1_gain: float32 [768], replicated
- grad_ln1_bias: float32 [768], replicated
- grad_w_qkv: float32 [768, 2304], replicated
- grad_q_bias: float32 [768], replicated
- grad_v_bias: float32 [768], replicated
- grad_w_out: float32 [768, 768], replicated
- grad_out_bias: float32 [768], replicated
- grad_ln2_gain: float32 [768], replicated
- grad_ln2_bias: float32 [768], replicated
- grad_w_fc1: float32 [768, 3072], replicated
- grad_fc1_bias: float32 [3072], replicated
- grad_w_fc2: float32 [3072, 768], replicated
- grad_fc2_bias: float32 [768], replicated
The draws below stay inside these ranges and needn't reach their ends.
Inputs may be any that keep to these rules, and one draw needn't show every extreme that they name: `segments`: each packed row holds either one image of 784 patches and one of 196 patches (in either order) or five images of 196 patches; a patch's segment is the first patch of its image divided by 196. Among the 1 row of each index of dp one row holds an image of 784 patches.
All inputs are finite; a program needn't handle non-finite values.
Results may differ from the reference program's by a relative error of at most 0.017.
Values may be sent and summed in bfloat16 or wider, within the bound.
No kernel may reach another device: no remote copies, remote signals or barrier semaphores. Data moves between devices by JAX's collectives and lax.ppermute only.
A program may use at most 256 MiB of HBM per device.

```python
import jax
import jax.numpy as jnp
from jax import lax

D = 768
HEADS = 12
HD = 64
FF = 3072
IMG = 196
ROWS_DEV = 1
ROW_LEN = 980
ROWS = 64
N_DP = 64


def draw_segments(key, part):
    key = jax.random.fold_in(key, 7)
    kinds = jax.random.randint(jax.random.fold_in(key, 1), (ROWS,), 0, 3)
    forced = jax.random.randint(jax.random.fold_in(key, 2), (N_DP,), 0, ROWS_DEV)
    sides = jax.random.randint(jax.random.fold_in(key, 3), (N_DP,), 0, 2)
    sides = jnp.where(jnp.arange(N_DP) == 0, 0, sides)
    row_ids = jnp.arange(ROWS)
    groups = row_ids // ROWS_DEV
    chosen = row_ids % ROWS_DEV == forced[groups]
    kinds = jnp.where(chosen, sides[groups], kinds)
    places = jnp.arange(ROW_LEN)
    big_first = jnp.where(places >= 4 * IMG, 4, 0)
    small_first = jnp.where(places >= IMG, 1, 0)
    all_small = places // IMG
    table = jnp.stack([big_first, small_first, all_small])
    return table[kinds].astype(jnp.int32)


def block_scale(key, shape, shards, least, high):
    def one(position, parts):
        draws = jax.random.uniform(jax.random.fold_in(jax.random.fold_in(key, 6), position), (parts,), jnp.float32, least / len(shards), high / len(shards))
        return jnp.repeat(jnp.exp(draws), shape[position] // parts).reshape((-1,) + (1,) * (len(shape) - position - 1))

    loudness = one(*shards[0])
    for cut in shards[1:]:
        loudness = loudness * one(*cut)
    return loudness


def bell_draw(rng, shape, scale, most, split=(), dtype=jnp.bfloat16):
    level = block_scale(rng, shape, split, -0.22, 0.18) if split else 1.0
    entries = jax.random.normal(rng, shape, jnp.float32) * scale * level
    return jnp.minimum(jnp.maximum(entries, -most), most).astype(dtype)


def setup_inputs(seed: int = 0) -> dict:
    splits = jax.random.split(jax.random.key(seed), 17)
    return {
        "inputs": bell_draw(splits[0], (ROWS, ROW_LEN, D), 1.0, 6.0, ((0, 64), (1, 2))),
        "segments": draw_segments(jax.random.fold_in(splits[16], 71), 0),
        "cotangent": bell_draw(splits[2], (ROWS, ROW_LEN, D), 1.0, 6.0, ((0, 64), (1, 2))),
        "ln1_gain": jnp.clip(1.0 + 0.1 * jax.random.normal(splits[3], (D,), jnp.float32), 0.5, 1.5),
        "ln1_bias": bell_draw(splits[4], (D,), 0.2, 1.0, (), jnp.float32),
        "w_qkv": bell_draw(splits[5], (D, 3 * D), D ** -0.5, 0.21875),
        "q_bias": bell_draw(splits[6], (D,), 0.2, 1.0, (), jnp.float32),
        "v_bias": bell_draw(splits[7], (D,), 0.2, 1.0, (), jnp.float32),
        "w_out": bell_draw(splits[8], (D, D), (D // 64) ** -0.5, 1.75),
        "out_bias": bell_draw(splits[9], (D,), 0.2, 1.0, (), jnp.float32),
        "ln2_gain": jnp.clip(1.0 + 0.1 * jax.random.normal(splits[10], (D,), jnp.float32), 0.5, 1.5),
        "ln2_bias": bell_draw(splits[11], (D,), 0.2, 1.0, (), jnp.float32),
        "w_fc1": bell_draw(splits[12], (D, FF), D ** -0.5, 0.21875),
        "fc1_bias": bell_draw(splits[13], (FF,), 0.3, 1.5, (), jnp.float32),
        "w_fc2": bell_draw(splits[14], (FF, D), FF ** -0.5, 0.109375),
        "fc2_bias": bell_draw(splits[15], (D,), 0.2, 1.0, (), jnp.float32),
    }


@jax.custom_vjp
def low(v):
    return lax.optimization_barrier(v.astype(jnp.bfloat16)).astype(jnp.float32)

@jax.custom_vjp
def low_back(v):
    return v

def low_keep(v):
    return (low(v), None)

def low_pass(kept, grad):
    return (grad,)

def back_keep(v):
    return (v, None)

def back_low(kept, grad):
    return (low(grad),)
low.defvjp(low_keep, low_pass)
low_back.defvjp(back_keep, back_low)

def matmul(left, right):
    return jnp.dot(left, right, precision=lax.Precision.HIGHEST)

def layer_norm(values, gain, shift):
    center = values - lax.optimization_barrier(jnp.mean(values, axis=-1, keepdims=True))
    spread = lax.optimization_barrier(jnp.mean(center * center, axis=-1, keepdims=True))
    return center * lax.rsqrt(spread + 1e-06) * gain + shift

def row_forward(params, row_input, row_segments):
    ln1_gain, ln1_bias, w_qkv, q_bias, v_bias, w_out, out_bias, ln2_gain, ln2_bias, w_fc1, fc1_bias, w_fc2, fc2_bias = params
    count, width = row_input.shape
    normed = low(layer_norm(row_input, ln1_gain, ln1_bias))
    packed = matmul(normed, w_qkv)
    query = low(low_back(packed[:, :width] + q_bias))
    key = low(low_back(packed[:, width:2 * width]))
    value = low(low_back(packed[:, 2 * width:] + v_bias))
    query_heads = query.reshape(count, HEADS, HD)
    key_heads = key.reshape(count, HEADS, HD)
    value_heads = value.reshape(count, HEADS, HD)
    scores = jnp.einsum('qhd,khd->hqk', query_heads, key_heads, precision=lax.Precision.HIGHEST) * HD ** (-0.5)
    same = row_segments[:, None] == row_segments[None, :]
    scores = low_back(jnp.where(same[None], scores, -1e+30))
    probs = low(jax.nn.softmax(scores, axis=-1))
    mixed = jnp.einsum('hqk,khd->qhd', probs, value_heads, precision=lax.Precision.HIGHEST).reshape(count, width)
    mixed = low(low_back(mixed))
    branch = low_back(matmul(mixed, w_out) + out_bias)
    middle = row_input + branch
    normed_two = low(layer_norm(middle, ln2_gain, ln2_bias))
    hidden = low_back(matmul(normed_two, w_fc1) + fc1_bias)
    active = low(jax.nn.gelu(hidden, approximate=False))
    return middle + low_back(matmul(active, w_fc2) + fc2_bias)

def reference(inputs, segments, cotangent, ln1_gain, ln1_bias, w_qkv, q_bias, v_bias, w_out, out_bias, ln2_gain, ln2_bias, w_fc1, fc1_bias, w_fc2, fc2_bias):
    params = tuple((p.astype(jnp.float32) for p in (ln1_gain, ln1_bias, w_qkv, q_bias, v_bias, w_out, out_bias, ln2_gain, ln2_bias, w_fc1, fc1_bias, w_fc2, fc2_bias)))

    def one_row(totals, row):
        row_input, row_segments, row_grad = row

        def forward(values, weights):
            return row_forward(weights, values, row_segments)
        result, pull = jax.vjp(forward, row_input.astype(jnp.float32), params)
        grad_input, grad_params = pull(row_grad.astype(jnp.float32))
        totals = jax.tree.map(lambda a, b: a + b, totals, grad_params)
        return (totals, (result.astype(jnp.bfloat16), grad_input.astype(jnp.bfloat16)))
    zeros = jax.tree.map(jnp.zeros_like, params)
    totals, (outputs, input_grads) = lax.scan(one_row, zeros, (inputs, segments, cotangent))
    return (outputs, input_grads, totals[0], totals[1], totals[2], totals[3], totals[4], totals[5], totals[6], totals[7], totals[8], totals[9], totals[10], totals[11], totals[12])
```

```python
import jax
import jax.numpy as jnp
from jax import lax
from jax.experimental import pallas as pl
from jax.experimental.pallas import tpu as pltpu
from jax.sharding import Mesh
from jax.sharding import PartitionSpec as P


HALF = 496
TOK = 2 * HALF
REAL = 490
PAIR = 128
BIG_Q, BIG_K, BIG_STEP = 800, 896, 160
SMALL_Q, SMALL_K = 208, 256
OFF = -1e30
F32, BF16 = jnp.float32, jnp.bfloat16
NT = (((1,), (1,)), ((), ()))
TN = (((0,), (0,)), ((), ()))


def windows(small_first):
    big = (
        pl.multiple_of(small_first * 192, 32),
        pl.multiple_of(small_first * 96, 32),
        small_first * 196,
        790 + small_first * 196,
    )
    small = (
        pl.multiple_of((1 - small_first) * 784, 16),
        pl.multiple_of((1 - small_first) * 736, 32),
        (1 - small_first) * 790,
        196 + (1 - small_first) * 790,
    )
    return big, small


def in_image(start, count, first, end):
    rows = start + lax.broadcasted_iota(jnp.int32, (count, PAIR), 0)
    return (rows >= first) & (rows < end) & ((rows < REAL) | (rows >= HALF))


def lanes(count):
    return lax.broadcasted_iota(jnp.int32, (count, PAIR), 1)


def own(lane, head):
    return lane < 64 if head == 0 else lane >= 64


def forward_kernel(flag, q_ref, k_ref, v_ref, mixed_ref, lse_ref):
    small_first = flag[0]
    big, small = windows(small_first)

    def image(window, queries, step, keys, merge):
        q_start, k_start, first, end = window
        lane_k = lanes(keys)
        bias = jnp.where(in_image(k_start, keys, first, end), 0.0, OFF)
        k_all = k_ref[pl.ds(k_start, keys), :].astype(F32)
        v_all = v_ref[pl.ds(k_start, keys), :].astype(F32)
        k_heads, v_heads = [], []
        for head in range(2):
            spare = 64 - 64 * head
            k_heads.append(
                jnp.where(own(lane_k, head), k_all, jnp.where(lane_k == spare, bias, 0.0)).astype(BF16)
            )
            v_heads.append(
                jnp.where(own(lane_k, head), v_all, jnp.where(lane_k == spare, 1.0, 0.0)).astype(BF16)
            )
        lane = lanes(step)
        for part in range(queries // step):
            start = pl.multiple_of(q_start + part * step, 16)
            here = pl.ds(start, step)
            q_part = q_ref[here, :].astype(F32) * 0.125
            outs, sums = [], []
            for head in range(2):
                spare = 64 - 64 * head
                q_head = jnp.where(
                    own(lane, head), q_part, jnp.where(lane == spare, 1.0, 0.0)
                ).astype(BF16)
                scores = lax.dot_general(q_head, k_heads[head], NT, preferred_element_type=F32)
                top = jnp.max(scores, axis=1, keepdims=True)
                weights = jnp.exp(scores - top).astype(BF16)
                out = jnp.dot(weights, v_heads[head], preferred_element_type=F32)
                total = out[:, spare : spare + 1]
                outs.append(out * (1.0 / total))
                sums.append(top + jnp.log(total))
            mixed = jnp.where(lane < 64, outs[0], outs[1])
            lse = jnp.where(lane < 64, sums[1], sums[0])
            if merge:
                rows = start + lax.broadcasted_iota(jnp.int32, (step, PAIR), 0)
                keep = (rows >= small[2]) & ((rows < 196) | (small_first == 0))
                mixed = jnp.where(keep, mixed_ref[here, :].astype(F32), mixed)
                lse = jnp.where(keep, lse_ref[here, :], lse)
            mixed_ref[here, :] = mixed.astype(BF16)
            lse_ref[here, :] = lse

    image(small, SMALL_Q, SMALL_Q, SMALL_K, False)
    image(big, BIG_Q, BIG_STEP, BIG_K, True)


def block(first):
    return pl.BlockSpec((TOK, PAIR), lambda i, flag: (0, first + i))


def attention_forward(flag, packed):
    return pl.pallas_call(
        forward_kernel,
        grid_spec=pltpu.PrefetchScalarGridSpec(
            num_scalar_prefetch=1,
            grid=(3,),
            in_specs=[block(0), block(3), block(6)],
            out_specs=[block(0), block(0)],
        ),
        out_shape=[
            jax.ShapeDtypeStruct((TOK, 3 * PAIR), BF16),
            jax.ShapeDtypeStruct((TOK, 3 * PAIR), F32),
        ],
        compiler_params=pltpu.CompilerParams(vmem_limit_bytes=40 * 2**20),
        cost_estimate=pl.CostEstimate(flops=6_000_000_000, bytes_accessed=5_000_000, transcendentals=4_000_000),
        name="attention_forward",
    )(flag, packed, packed, packed)


def split(values):
    high = values.astype(BF16).astype(F32)
    return high, values - high


def backward_kernel(flag, q_ref, k_ref, v_ref, grad_ref, mixed_ref, lse_ref, out_ref, scores_ref):
    pair = pl.program_id(0)
    big, small = windows(flag[0])

    def lanes_of(kind):
        return pl.ds(pl.multiple_of((3 * kind + pair) * PAIR, PAIR), PAIR)

    def image(window, keys, step, queries, add):
        k_start, q_start, first, end = window
        here = pl.ds(q_start, queries)
        lane = lanes(queries)
        bias = jnp.where(in_image(q_start, queries, first, end), 0.0, OFF)
        q_all = q_ref[here, :].astype(F32) * 0.125
        q_low = q_all.astype(BF16)
        grad_low = grad_ref[here, :]
        grad_all = grad_low.astype(F32)
        products = grad_all * mixed_ref[here, :].astype(F32)
        lse_high, lse_rest = split(lse_ref[here, :])
        lse_mid, lse_low = split(lse_rest)
        q_heads, grad_heads = [], []
        for head in range(2):
            spare = 64 - 64 * head
            mine = own(lane, head)
            q_head = jnp.where(mine, q_all, 0.0)
            for at, extra in enumerate((1.0, -lse_high, -lse_mid, -lse_low, bias)):
                q_head = jnp.where(lane == spare + at, extra, q_head)
            q_heads.append(q_head.astype(BF16))
            row_term = jnp.sum(jnp.where(mine, products, 0.0), axis=1, keepdims=True)
            term_high, term_low = split(row_term)
            grad_head = jnp.where(mine, grad_all, 0.0)
            grad_head = jnp.where(lane == spare + 1, -term_high, grad_head)
            grad_head = jnp.where(lane == spare + 2, -term_low, grad_head)
            grad_heads.append(grad_head.astype(BF16))
        lane = lanes(step)
        for part in range(keys // step):
            start = pl.multiple_of(k_start + part * step, 16)
            rows = pl.ds(start, step)
            k_part = k_ref[rows, :].astype(F32)
            v_part = v_ref[rows, :].astype(F32)
            key_bias = jnp.where(in_image(start, step, first, end), 0.0, OFF)
            keys_grad, values_grad = [], []
            for head in range(2):
                spare = 64 - 64 * head
                mine = own(lane, head)
                ones = (lane >= spare + 1) & (lane <= spare + 4)
                k_head = jnp.where(mine, k_part, jnp.where(ones, 1.0, 0.0))
                k_head = jnp.where(lane == spare, key_bias, k_head).astype(BF16)
                v_head = jnp.where(mine, v_part, jnp.where(ones, 1.0, 0.0)).astype(BF16)
                probs = jnp.exp(
                    lax.dot_general(k_head, q_heads[head], NT, preferred_element_type=F32)
                )
                change = lax.dot_general(v_head, grad_heads[head], NT, preferred_element_type=F32)
                grad_scores = (probs * change).astype(BF16)
                values_grad.append(
                    jnp.dot(probs.astype(BF16), grad_low, preferred_element_type=F32)
                )
                keys_grad.append(jnp.dot(grad_scores, q_low, preferred_element_type=F32))
                scores_ref[head, part * step : (part + 1) * step, :queries] = grad_scores
            key_out = jnp.where(lane < 64, keys_grad[0], keys_grad[1]).astype(BF16)
            value_out = jnp.where(lane < 64, values_grad[0], values_grad[1]).astype(BF16)
            if add:
                key_out = key_out + out_ref[rows, lanes_of(1)]
                value_out = value_out + out_ref[rows, lanes_of(2)]
            out_ref[rows, lanes_of(1)] = key_out
            out_ref[rows, lanes_of(2)] = value_out
        k_all = k_ref[pl.ds(k_start, keys), :]
        turned = [
            lax.dot_general(k_all, scores_ref[head, :keys, :queries], TN, preferred_element_type=F32)
            for head in range(2)
        ]
        row = lax.broadcasted_iota(jnp.int32, (PAIR, queries), 0)
        query_out = jnp.transpose(jnp.where(row < 64, turned[0], turned[1]) * 0.125).astype(BF16)
        if add:
            query_out = query_out + out_ref[here, lanes_of(0)]
        out_ref[here, lanes_of(0)] = query_out

    out_ref[pl.ds(small[0], SMALL_Q), lanes_of(1)] = jnp.zeros((SMALL_Q, PAIR), BF16)
    out_ref[pl.ds(small[0], SMALL_Q), lanes_of(2)] = jnp.zeros((SMALL_Q, PAIR), BF16)
    out_ref[pl.ds(small[1], SMALL_K), lanes_of(0)] = jnp.zeros((SMALL_K, PAIR), BF16)
    image(big, BIG_Q, BIG_STEP, BIG_K, False)
    image(small, SMALL_Q, SMALL_Q, SMALL_K, True)


def attention_backward(flag, packed, grad_mixed, mixed, lse):
    return pl.pallas_call(
        backward_kernel,
        grid_spec=pltpu.PrefetchScalarGridSpec(
            num_scalar_prefetch=1,
            grid=(3,),
            in_specs=[block(0), block(3), block(6), block(0), block(0), block(0)],
            out_specs=pl.BlockSpec((TOK, 9 * PAIR), lambda i, flag: (0, 0)),
            scratch_shapes=[pltpu.VMEM((2, BIG_Q, BIG_K), BF16)],
        ),
        out_shape=jax.ShapeDtypeStruct((TOK, 9 * PAIR), BF16),
        compiler_params=pltpu.CompilerParams(vmem_limit_bytes=48 * 2**20),
        cost_estimate=pl.CostEstimate(flops=15_000_000_000, bytes_accessed=9_000_000, transcendentals=4_000_000),
        name="attention_backward",
    )(flag, packed, packed, packed, grad_mixed, mixed, lse)


WIDTH = 768
SHARE = 384
FF_SHARE = 1536
PEERS = 64
CHIPS = ("x", "y", "zh", "zl")
ROWS = ("x", "y", "zh", "c")


def norm_parts(values):
    center = values - jnp.mean(values, axis=-1, keepdims=True)
    inverse = lax.rsqrt(jnp.mean(center * center, axis=-1, keepdims=True) + 1e-06)
    return (center * inverse, inverse)


def norm_back(grad_normed, normed, inverse):
    return inverse * (
        grad_normed
        - jnp.mean(grad_normed, axis=-1, keepdims=True)
        - normed * jnp.mean(grad_normed * normed, axis=-1, keepdims=True)
    )


def matmul(left, right):
    return jnp.dot(left, right, preferred_element_type=F32)


def other_core(values):
    return lax.ppermute(values, "c", [(0, 1), (1, 0)])


def swap_home(values):
    return lax.ppermute(values, ("c", "zl"), [(1, 2), (2, 1)])


def body(
    inputs,
    segments,
    cotangent,
    ln1_gain,
    ln1_bias,
    w_qkv,
    q_bias,
    v_bias,
    w_out,
    out_bias,
    ln2_gain,
    ln2_bias,
    w_fc1,
    fc1_bias,
    w_fc2,
    fc2_bias,
):
    core = lax.axis_index("c")
    home = core == lax.axis_index("zl")
    first = core == 0

    def pair(mine, other, axis):
        return jnp.concatenate(
            [jnp.where(first, mine, other), jnp.where(first, other, mine)], axis=axis
        )

    def columns(array, size, start=0):
        return lax.dynamic_slice_in_dim(array, start + core * size, size, array.ndim - 1)

    def half(array, which):
        return lax.dynamic_slice_in_dim(array, which * HALF, HALF, 0)

    small_first = (segments[0, 196] != segments[0, 0]).astype(BF16)
    tail = jnp.broadcast_to(small_first, (HALF - REAL, WIDTH))
    sent = jnp.concatenate([inputs[0], tail], axis=0)
    x_half = jnp.where(home, sent, swap_home(sent))
    x_all = pair(x_half, other_core(x_half), 0)
    flag = x_all[REAL : REAL + 1, 0].astype(jnp.int32)
    rows = lax.broadcasted_iota(jnp.int32, (TOK, 1), 0)
    real = (rows < REAL) | ((rows >= HALF) & (rows < HALF + REAL))
    x_all = jnp.where(real, x_all, 0).astype(F32)

    grad_sent = jnp.pad(cotangent[0], ((0, HALF - REAL), (0, 0)))
    grad_half = jnp.where(home, grad_sent, swap_home(grad_sent))
    grad_top = pair(grad_half, other_core(grad_half), 0)

    w_packed = jnp.concatenate([columns(w_qkv, SHARE, i * WIDTH) for i in range(3)], axis=1)
    packed_bias = jnp.concatenate(
        [columns(q_bias, SHARE), jnp.zeros((SHARE,), F32), columns(v_bias, SHARE)]
    )
    w_out_mine = lax.dynamic_slice_in_dim(w_out, core * SHARE, SHARE, 0)
    w_in = columns(w_fc1, FF_SHARE)
    in_bias = columns(fc1_bias, FF_SHARE)
    w_back = lax.dynamic_slice_in_dim(w_fc2, core * FF_SHARE, FF_SHARE, 0)

    normed_one, inverse_one = norm_parts(x_all)
    first_in = (normed_one * ln1_gain + ln1_bias).astype(BF16)
    packed = (matmul(first_in, w_packed) + packed_bias).astype(BF16)
    mixed_mine, lse = attention_forward(flag, packed)
    mixed = pair(mixed_mine, other_core(mixed_mine), 1)
    middle = x_all + matmul(mixed, w_out) + out_bias
    normed_two, inverse_two = norm_parts(middle)
    second_in = (normed_two * ln2_gain + ln2_bias).astype(BF16)
    hidden = matmul(second_in, w_in) + in_bias
    active_full, gelu_pull = jax.vjp(lambda h: jax.nn.gelu(h, approximate=False), hidden)
    active = active_full.astype(BF16)
    grad_active = matmul(grad_top, w_back.T)
    grad_hidden = gelu_pull(grad_active)[0].astype(BF16)
    grad_back = matmul(active.T, grad_top)
    grad_in = matmul(second_in.T, grad_hidden)
    grad_in_bias = jnp.sum(grad_hidden.astype(F32), axis=0)
    grad_back_bias = jnp.sum(grad_top.astype(F32), axis=0)
    early_small = jnp.concatenate([grad_in_bias, grad_back_bias]).reshape(3, WIDTH)
    early_back = jnp.concatenate(
        [grad_back.astype(BF16), jnp.pad(early_small.astype(BF16), ((0, 61), (0, 0)))], axis=0
    )
    early = lax.psum((early_back, grad_in.astype(BF16)), CHIPS)

    product = matmul(active, w_back)
    result = (
        half(middle, core)
        + half(product, core)
        + other_core(half(product, 1 - core))
        + fc2_bias
    ).astype(BF16)
    output = jnp.where(home, result, swap_home(result))[None, :REAL]

    second_part = matmul(grad_hidden, w_in.T)
    grad_second_in = second_part + other_core(second_part)
    grad_ln2_gain = jnp.sum(grad_second_in * normed_two, axis=0)
    grad_ln2_bias = jnp.sum(grad_second_in, axis=0)
    grad_middle = grad_top.astype(F32) + norm_back(
        grad_second_in * ln2_gain, normed_two, inverse_two
    )
    grad_branch = grad_middle.astype(BF16)
    grad_w_out = matmul(mixed_mine.T, grad_branch)
    grad_out_bias = jnp.sum(grad_branch.astype(F32), axis=0)
    grad_mixed = matmul(grad_branch, w_out_mine.T).astype(BF16)
    grad_packed = attention_backward(flag, packed, grad_mixed, mixed_mine, lse)
    grad_w_packed = matmul(first_in.T, grad_packed)
    packed_sums = jnp.sum(grad_packed.astype(F32), axis=0)
    first_part = matmul(grad_packed, w_packed.T)

    small = jnp.concatenate(
        [
            grad_out_bias,
            grad_ln2_gain,
            grad_ln2_bias,
            jnp.sum(first_part * normed_one, axis=0),
            jnp.sum(first_part, axis=0),
            packed_sums[:SHARE],
            packed_sums[2 * SHARE :],
        ]
    ).astype(BF16)
    late = jnp.concatenate(
        [
            grad_w_packed.astype(BF16).reshape(PEERS, 12, 3 * SHARE),
            grad_w_out.astype(BF16).reshape(PEERS, 4, 3 * SHARE),
        ],
        axis=1,
    )
    late_small = jnp.pad(small.reshape(PEERS, 1, 72), ((0, 0), (0, 15), (0, 56)))
    late = jnp.concatenate([late, late_small], axis=2)
    parts = lax.all_to_all(late, CHIPS, 0, 0, tiled=True)
    share = jnp.sum(parts.astype(F32), axis=0, keepdims=True).astype(BF16)
    mine = lax.all_to_all(
        jnp.broadcast_to(share, (PEERS,) + share.shape[1:]), CHIPS, 0, 0, tiled=True
    )
    other = other_core(mine)

    grad_first_in = half(first_part, core) + other_core(half(first_part, 1 - core))
    grad_input = half(grad_middle, core) + norm_back(
        grad_first_in * ln1_gain, half(normed_one, core), half(inverse_one, core)
    )
    grad_input = grad_input.astype(BF16)
    input_grad = jnp.where(home, grad_input, swap_home(grad_input))[None, :REAL]

    def both(mine, other, axis):
        return pair(mine.astype(F32), other.astype(F32), axis)

    back, inner = early
    back_other, inner_other = (other_core(a) for a in early)
    total_back = both(back[:FF_SHARE], back_other[:FF_SHARE], 0)
    total_in = both(inner, inner_other, 1)
    early_small, small_other = back[FF_SHARE:], back_other[FF_SHARE:]
    total_in_bias = both(early_small[:2].reshape(-1), small_other[:2].reshape(-1), 0)
    total_back_bias = early_small[2].astype(F32)

    def unpack(late):
        late = late.astype(F32)
        small = late[:, 0, 3 * SHARE : 3 * SHARE + 72].reshape(-1)
        return (
            late[:, :12, : 3 * SHARE].reshape(WIDTH, 3 * SHARE),
            late[:, 12:, : 3 * SHARE].reshape(SHARE, WIDTH),
            small,
        )

    packed_mine, out_mine, small_mine = unpack(mine)
    packed_other, out_other, small_other = unpack(other)
    total_packed = jnp.concatenate(
        [
            pair(
                packed_mine[:, i * SHARE : (i + 1) * SHARE],
                packed_other[:, i * SHARE : (i + 1) * SHARE],
                1,
            )
            for i in range(3)
        ],
        axis=1,
    )
    total_out = pair(out_mine, out_other, 0)

    def vector(i):
        return small_mine[i * WIDTH : (i + 1) * WIDTH]

    def vector_other(i):
        return small_other[i * WIDTH : (i + 1) * WIDTH]

    at = 5 * WIDTH
    total_q_bias = pair(small_mine[at : at + SHARE], small_other[at : at + SHARE], 0)
    total_v_bias = pair(small_mine[at + SHARE :], small_other[at + SHARE :], 0)
    return (
        output,
        input_grad,
        vector(3) + vector_other(3),
        vector(4) + vector_other(4),
        total_packed,
        total_q_bias,
        total_v_bias,
        total_out,
        vector(0),
        vector(1),
        vector(2),
        total_in,
        total_in_bias,
        total_back,
        total_back_bias,
    )


def solution(mesh):
    fine = Mesh(mesh.devices.reshape(4, 4, 2, 2, 2), ("x", "y", "zh", "c", "zl"))
    tokens = P(ROWS, "zl", None)
    return jax.shard_map(
        body,
        mesh=fine,
        in_specs=(tokens, P(ROWS, None), tokens) + (P(),) * 13,
        out_specs=(tokens, tokens) + (P(),) * 13,
        check_vma=False,
    )
```

```python
import jax
import jax.numpy as jnp
from jax import lax
from jax.experimental import pallas as pl
from jax.experimental.pallas import tpu as pltpu
from jax.sharding import Mesh
from jax.sharding import PartitionSpec as P


HALF = 496
TOK = 2 * HALF
REAL = 490
PAIR = 128
BIG_Q, BIG_K, BIG_STEP = 800, 896, 160
SMALL_Q, SMALL_K = 208, 256
OFF = -1e30
F32, BF16 = jnp.float32, jnp.bfloat16
NT = (((1,), (1,)), ((), ()))
TN = (((0,), (0,)), ((), ()))


def windows(small_first):
    big = (
        pl.multiple_of(small_first * 192, 32),
        pl.multiple_of(small_first * 96, 32),
        small_first * 196,
        790 + small_first * 196,
    )
    small = (
        pl.multiple_of((1 - small_first) * 784, 16),
        pl.multiple_of((1 - small_first) * 736, 32),
        (1 - small_first) * 790,
        196 + (1 - small_first) * 790,
    )
    return big, small


def in_image(start, count, first, end):
    rows = start + lax.broadcasted_iota(jnp.int32, (count, PAIR), 0)
    return (rows >= first) & (rows < end) & ((rows < REAL) | (rows >= HALF))


def lanes(count):
    return lax.broadcasted_iota(jnp.int32, (count, PAIR), 1)


def own(lane, head):
    return lane < 64 if head == 0 else lane >= 64


def forward_kernel(flag, q_ref, k_ref, v_ref, mixed_ref, lse_ref):
    small_first = flag[0]
    big, small = windows(small_first)

    def image(window, queries, step, keys, merge):
        q_start, k_start, first, end = window
        lane_k = lanes(keys)
        bias = jnp.where(in_image(k_start, keys, first, end), 0.0, OFF)
        k_all = k_ref[pl.ds(k_start, keys), :].astype(F32)
        v_all = v_ref[pl.ds(k_start, keys), :].astype(F32)
        k_heads, v_heads = [], []
        for head in range(2):
            spare = 64 - 64 * head
            k_heads.append(
                jnp.where(own(lane_k, head), k_all, jnp.where(lane_k == spare, bias, 0.0)).astype(BF16)
            )
            v_heads.append(
                jnp.where(own(lane_k, head), v_all, jnp.where(lane_k == spare, 1.0, 0.0)).astype(BF16)
            )
        lane = lanes(step)
        for part in range(queries // step):
            start = pl.multiple_of(q_start + part * step, 16)
            here = pl.ds(start, step)
            q_part = q_ref[here, :].astype(F32) * 0.125
            outs, sums = [], []
            for head in range(2):
                spare = 64 - 64 * head
                q_head = jnp.where(
                    own(lane, head), q_part, jnp.where(lane == spare, 1.0, 0.0)
                ).astype(BF16)
                scores = lax.dot_general(q_head, k_heads[head], NT, preferred_element_type=F32)
                top = jnp.max(scores, axis=1, keepdims=True)
                weights = jnp.exp(scores - top).astype(BF16)
                out = jnp.dot(weights, v_heads[head], preferred_element_type=F32)
                total = out[:, spare : spare + 1]
                outs.append(out * (1.0 / total))
                sums.append(top + jnp.log(total))
            mixed = jnp.where(lane < 64, outs[0], outs[1])
            lse = jnp.where(lane < 64, sums[1], sums[0])
            if merge:
                rows = start + lax.broadcasted_iota(jnp.int32, (step, PAIR), 0)
                keep = (rows >= small[2]) & ((rows < 196) | (small_first == 0))
                mixed = jnp.where(keep, mixed_ref[here, :].astype(F32), mixed)
                lse = jnp.where(keep, lse_ref[here, :], lse)
            mixed_ref[here, :] = mixed.astype(BF16)
            lse_ref[here, :] = lse

    image(small, SMALL_Q, SMALL_Q, SMALL_K, False)
    image(big, BIG_Q, BIG_STEP, BIG_K, True)


def block(first):
    return pl.BlockSpec((TOK, PAIR), lambda i, flag: (0, first + i))


def attention_forward(flag, packed):
    return pl.pallas_call(
        forward_kernel,
        grid_spec=pltpu.PrefetchScalarGridSpec(
            num_scalar_prefetch=1,
            grid=(3,),
            in_specs=[block(0), block(3), block(6)],
            out_specs=[block(0), block(0)],
        ),
        out_shape=[
            jax.ShapeDtypeStruct((TOK, 3 * PAIR), BF16),
            jax.ShapeDtypeStruct((TOK, 3 * PAIR), F32),
        ],
        compiler_params=pltpu.CompilerParams(vmem_limit_bytes=40 * 2**20),
        cost_estimate=pl.CostEstimate(flops=6_000_000_000, bytes_accessed=5_000_000, transcendentals=4_000_000),
        name="attention_forward",
    )(flag, packed, packed, packed)


def split(values):
    high = values.astype(BF16).astype(F32)
    return high, values - high


def backward_kernel(flag, q_ref, k_ref, v_ref, grad_ref, mixed_ref, lse_ref, out_ref, scores_ref):
    pair = pl.program_id(0)
    big, small = windows(flag[0])

    def lanes_of(kind):
        return pl.ds(pl.multiple_of((3 * kind + pair) * PAIR, PAIR), PAIR)

    def image(window, keys, step, queries, add):
        k_start, q_start, first, end = window
        here = pl.ds(q_start, queries)
        lane = lanes(queries)
        bias = jnp.where(in_image(q_start, queries, first, end), 0.0, OFF)
        q_all = q_ref[here, :].astype(F32) * 0.125
        q_low = q_all.astype(BF16)
        grad_low = grad_ref[here, :]
        grad_all = grad_low.astype(F32)
        products = grad_all * mixed_ref[here, :].astype(F32)
        lse_high, lse_rest = split(lse_ref[here, :])
        lse_mid, lse_low = split(lse_rest)
        q_heads, grad_heads = [], []
        for head in range(2):
            spare = 64 - 64 * head
            mine = own(lane, head)
            q_head = jnp.where(mine, q_all, 0.0)
            for at, extra in enumerate((1.0, -lse_high, -lse_mid, -lse_low, bias)):
                q_head = jnp.where(lane == spare + at, extra, q_head)
            q_heads.append(q_head.astype(BF16))
            row_term = jnp.sum(jnp.where(mine, products, 0.0), axis=1, keepdims=True)
            term_high, term_low = split(row_term)
            grad_head = jnp.where(mine, grad_all, 0.0)
            grad_head = jnp.where(lane == spare + 1, -term_high, grad_head)
            grad_head = jnp.where(lane == spare + 2, -term_low, grad_head)
            grad_heads.append(grad_head.astype(BF16))
        lane = lanes(step)
        for part in range(keys // step):
            start = pl.multiple_of(k_start + part * step, 16)
            rows = pl.ds(start, step)
            k_part = k_ref[rows, :].astype(F32)
            v_part = v_ref[rows, :].astype(F32)
            key_bias = jnp.where(in_image(start, step, first, end), 0.0, OFF)
            keys_grad, values_grad = [], []
            for head in range(2):
                spare = 64 - 64 * head
                mine = own(lane, head)
                ones = (lane >= spare + 1) & (lane <= spare + 4)
                k_head = jnp.where(mine, k_part, jnp.where(ones, 1.0, 0.0))
                k_head = jnp.where(lane == spare, key_bias, k_head).astype(BF16)
                v_head = jnp.where(mine, v_part, jnp.where(ones, 1.0, 0.0)).astype(BF16)
                probs = jnp.exp(
                    lax.dot_general(k_head, q_heads[head], NT, preferred_element_type=F32)
                )
                change = lax.dot_general(v_head, grad_heads[head], NT, preferred_element_type=F32)
                grad_scores = (probs * change).astype(BF16)
                values_grad.append(
                    jnp.dot(probs.astype(BF16), grad_low, preferred_element_type=F32)
                )
                keys_grad.append(jnp.dot(grad_scores, q_low, preferred_element_type=F32))
                scores_ref[head, part * step : (part + 1) * step, :queries] = grad_scores
            key_out = jnp.where(lane < 64, keys_grad[0], keys_grad[1]).astype(BF16)
            value_out = jnp.where(lane < 64, values_grad[0], values_grad[1]).astype(BF16)
            if add:
                key_out = key_out + out_ref[rows, lanes_of(1)]
                value_out = value_out + out_ref[rows, lanes_of(2)]
            out_ref[rows, lanes_of(1)] = key_out
            out_ref[rows, lanes_of(2)] = value_out
        k_all = k_ref[pl.ds(k_start, keys), :]
        turned = [
            lax.dot_general(k_all, scores_ref[head, :keys, :queries], TN, preferred_element_type=F32)
            for head in range(2)
        ]
        row = lax.broadcasted_iota(jnp.int32, (PAIR, queries), 0)
        query_out = jnp.transpose(jnp.where(row < 64, turned[0], turned[1]) * 0.125).astype(BF16)
        if add:
            query_out = query_out + out_ref[here, lanes_of(0)]
        out_ref[here, lanes_of(0)] = query_out

    out_ref[pl.ds(small[0], SMALL_Q), lanes_of(1)] = jnp.zeros((SMALL_Q, PAIR), BF16)
    out_ref[pl.ds(small[0], SMALL_Q), lanes_of(2)] = jnp.zeros((SMALL_Q, PAIR), BF16)
    out_ref[pl.ds(small[1], SMALL_K), lanes_of(0)] = jnp.zeros((SMALL_K, PAIR), BF16)
    image(big, BIG_Q, BIG_STEP, BIG_K, False)
    image(small, SMALL_Q, SMALL_Q, SMALL_K, True)


def attention_backward(flag, packed, grad_mixed, mixed, lse):
    return pl.pallas_call(
        backward_kernel,
        grid_spec=pltpu.PrefetchScalarGridSpec(
            num_scalar_prefetch=1,
            grid=(3,),
            in_specs=[block(0), block(3), block(6), block(0), block(0), block(0)],
            out_specs=pl.BlockSpec((TOK, 9 * PAIR), lambda i, flag: (0, 0)),
            scratch_shapes=[pltpu.VMEM((2, BIG_Q, BIG_K), BF16)],
        ),
        out_shape=jax.ShapeDtypeStruct((TOK, 9 * PAIR), BF16),
        compiler_params=pltpu.CompilerParams(vmem_limit_bytes=48 * 2**20),
        cost_estimate=pl.CostEstimate(flops=1_000_000_000, bytes_accessed=4_000_000, transcendentals=0),
        name="attention_backward",
    )(flag, packed, packed, packed, grad_mixed, mixed, lse)


WIDTH = 768
FF_SHARE = 1536
SUB = 256
PARTS = ((0, 256), (256, 512), (512, 768), (768, TOK))
SHARE = 384
PEERS = 64
LATE = 3 * SHARE + 128
CHIPS = ("x", "y", "zh", "zl")
ROWS = ("x", "y", "zh", "c")
WHOLE = pl.BlockSpec(memory_space=pltpu.VMEM)
HBM = pl.BlockSpec(memory_space=pl.ANY)


def params(mib):
    return pltpu.CompilerParams(vmem_limit_bytes=mib * 2**20)


def cost(flops, traffic, transcendentals=0):
    return pl.CostEstimate(
        flops=int(flops), bytes_accessed=int(traffic), transcendentals=int(transcendentals)
    )


def norm_rows(values):
    center = values - jnp.mean(values, axis=-1, keepdims=True)
    inverse = lax.rsqrt(jnp.mean(center * center, axis=-1, keepdims=True) + 1e-06)
    return center * inverse, inverse


def middle_kernel(
    core,
    mixed_ref,
    other_ref,
    x_ref,
    w_out_ref,
    out_bias_ref,
    gain_ref,
    bias_ref,
    grad_ref,
    w_in_ref,
    in_bias_ref,
    w_back_ref,
    middle_ref,
    active_ref,
    grad_hidden_ref,
    early_ref,
    sums_ref,
    second_ref,
    turned_ref,
):
    @pl.when(pl.program_id(0) == 0)
    def _():
        mine = w_out_ref[pl.ds(pl.multiple_of(core[0] * SHARE, 128), SHARE), :]
        other = w_out_ref[pl.ds(pl.multiple_of((1 - core[0]) * SHARE, 128), SHARE), :]
        for begin, end in PARTS:
            rows = slice(begin, end)
            branch = jnp.dot(mixed_ref[rows, :], mine, preferred_element_type=F32)
            branch += jnp.dot(other_ref[rows, :], other, preferred_element_type=F32)
            middle = x_ref[rows, :].astype(F32) + branch + out_bias_ref[...]
            middle_ref[rows, :] = middle
            second = norm_rows(middle)[0] * gain_ref[...] + bias_ref[...]
            second_ref[rows, :] = second.astype(BF16)
        turned_ref[...] = jnp.transpose(second_ref[...])

    def back(begin):
        here = active_ref[:, begin : begin + SHARE]
        total = lax.dot_general(here, grad_ref[...], TN, preferred_element_type=F32).astype(BF16)
        for group in range(8):
            for side in range(2):
                early_ref[begin // 24 + 2 * group + side, :, :SHARE] = total[
                    48 * group : 48 * group + 48, SHARE * side : SHARE * (side + 1)
                ]

    for sub in range(3):
        columns = slice(SUB * sub, SUB * (sub + 1))
        column_sums = 0.0
        for part in range(2):
            rows = slice(part * HALF, (part + 1) * HALF)
            hidden = jnp.dot(second_ref[rows, :], w_in_ref[:, columns], preferred_element_type=F32)
            hidden += in_bias_ref[:, columns]
            grad_active = lax.dot_general(
                grad_ref[rows, :], w_back_ref[columns, :], NT, preferred_element_type=F32
            )
            below = 0.5 + 0.5 * lax.erf(hidden * 0.7071067811865476)
            active_ref[rows, columns] = (hidden * below).astype(BF16)
            slope = below + hidden * jnp.exp(hidden * hidden * -0.5) * 0.3989422804014327
            grad_hidden = (grad_active * slope).astype(BF16)
            grad_hidden_ref[rows, columns] = grad_hidden
            column_sums += jnp.sum(grad_hidden.astype(F32), axis=0, keepdims=True)
        sums_ref[:, columns] = jnp.broadcast_to(column_sums, (8, SUB))
        total = jnp.dot(
            turned_ref[...], grad_hidden_ref[:, columns], preferred_element_type=F32
        ).astype(BF16)
        for tile in range(2):
            at = SUB * sub + 128 * tile
            side, lane = at // SHARE, at % SHARE
            for group in range(16):
                early_ref[2 * group + side, :, SHARE + lane : SHARE + lane + 128] = total[
                    48 * group : 48 * group + 48, 128 * tile : 128 * (tile + 1)
                ]
        if sub:
            back(SHARE * (sub - 1))


def middle_part(core, mixed, other, x, w_out, out_bias, gain, bias, grad, w_fc1, fc1_bias, w_fc2):
    def whole(shape):
        return pl.BlockSpec(shape, lambda i, core: (0, 0))

    tokens = whole((TOK, WIDTH))
    heads = whole((TOK, SHARE))
    vector = whole((1, WIDTH))
    ff_columns = pl.BlockSpec((TOK, WIDTH), lambda i, core: (0, i))
    return pl.pallas_call(
        middle_kernel,
        grid_spec=pltpu.PrefetchScalarGridSpec(
            num_scalar_prefetch=1,
            grid=(2,),
            in_specs=[
                heads,
                heads,
                tokens,
                whole((WIDTH, WIDTH)),
                vector,
                vector,
                vector,
                tokens,
                pl.BlockSpec((WIDTH, WIDTH), lambda i, core: (0, core[0] * 2 + i)),
                pl.BlockSpec((1, WIDTH), lambda i, core: (0, core[0] * 2 + i)),
                pl.BlockSpec((WIDTH, WIDTH), lambda i, core: (core[0] * 2 + i, 0)),
            ],
            out_specs=[
                tokens,
                ff_columns,
                ff_columns,
                pl.BlockSpec((32, 48, WIDTH), lambda i, core: (i, 0, 0)),
                pl.BlockSpec((8, WIDTH), lambda i, core: (0, i)),
            ],
            scratch_shapes=[pltpu.VMEM((TOK, WIDTH), BF16), pltpu.VMEM((WIDTH, TOK), BF16)],
        ),
        out_shape=[
            jax.ShapeDtypeStruct((TOK, WIDTH), F32),
            jax.ShapeDtypeStruct((TOK, FF_SHARE), BF16),
            jax.ShapeDtypeStruct((TOK, FF_SHARE), BF16),
            jax.ShapeDtypeStruct((PEERS, 48, WIDTH), BF16),
            jax.ShapeDtypeStruct((8, FF_SHARE), F32),
        ],
        compiler_params=params(48),
        cost_estimate=cost(10.5e9, 30e6, 3e6),
        name="middle_part",
    )(
        core,
        mixed,
        other,
        x,
        w_out,
        out_bias.reshape(1, WIDTH),
        gain.reshape(1, WIDTH),
        bias.reshape(1, WIDTH),
        grad,
        w_fc1,
        fc1_bias.reshape(1, 2 * FF_SHARE),
        w_fc2,
    )


def ff_products_kernel(core, active_ref, grad_ref, w_back_ref, w_in_ref, product_ref, second_ref, low_ref):
    product = jnp.dot(active_ref[...], w_back_ref[...], preferred_element_type=F32)
    second = lax.dot_general(grad_ref[...], w_in_ref[...], NT, preferred_element_type=F32)

    @pl.when(pl.program_id(0) == 0)
    def _():
        product_ref[...] = product
        second_ref[...] = second

    @pl.when(pl.program_id(0) == 1)
    def _():
        product_ref[...] += product
        total = second_ref[...] + second
        second_ref[...] = total
        low_ref[...] = total.astype(BF16)


def ff_products(core, active, grad_hidden, w_fc2, w_fc1):
    tokens = pl.BlockSpec((TOK, WIDTH), lambda i, core: (0, 0))
    ff_columns = pl.BlockSpec((TOK, WIDTH), lambda i, core: (0, i))
    return pl.pallas_call(
        ff_products_kernel,
        grid_spec=pltpu.PrefetchScalarGridSpec(
            num_scalar_prefetch=1,
            grid=(2,),
            in_specs=[
                ff_columns,
                ff_columns,
                pl.BlockSpec((WIDTH, WIDTH), lambda i, core: (core[0] * 2 + i, 0)),
                pl.BlockSpec((WIDTH, WIDTH), lambda i, core: (0, core[0] * 2 + i)),
            ],
            out_specs=[tokens, tokens, tokens],
        ),
        out_shape=[
            jax.ShapeDtypeStruct((TOK, WIDTH), F32),
            jax.ShapeDtypeStruct((TOK, WIDTH), F32),
            jax.ShapeDtypeStruct((TOK, WIDTH), BF16),
        ],
        compiler_params=params(40),
        cost_estimate=cost(1e9, 4e6),
        name="ff_products",
    )(core, active, grad_hidden, w_fc2, w_fc1)


def second_back_kernel(
    core,
    second_ref,
    other_ref,
    middle_ref,
    top_ref,
    mixed_ref,
    w_out_ref,
    gain_ref,
    grad_middle_ref,
    grad_mixed_ref,
    late_ref,
    sums_ref,
    branch_ref,
):
    sums = [0.0, 0.0, 0.0, 0.0]
    for begin, end in PARTS:
        rows = slice(begin, end)
        grad = second_ref[rows, :] + other_ref[rows, :].astype(F32)
        normed, inverse = norm_rows(middle_ref[rows, :])
        product = grad * normed
        scaled = grad * gain_ref[...]
        top = top_ref[rows, :].astype(F32)
        grad_middle = top + inverse * (
            scaled
            - jnp.mean(scaled, axis=-1, keepdims=True)
            - normed * jnp.mean(product * gain_ref[...], axis=-1, keepdims=True)
        )
        grad_middle_ref[rows, :] = grad_middle
        branch = grad_middle.astype(BF16)
        branch_ref[rows, :] = branch
        grad_mixed_ref[rows, :] = lax.dot_general(
            branch, w_out_ref[...], NT, preferred_element_type=F32
        ).astype(BF16)
        for i, values in enumerate((branch.astype(F32), product, grad, top)):
            sums[i] += jnp.sum(values, axis=0, keepdims=True)
    row = lax.broadcasted_iota(jnp.int32, (8, WIDTH), 0)
    out = jnp.broadcast_to(sums[0], (8, WIDTH))
    for i in range(1, 4):
        out = jnp.where(row == i, sums[i], out)
    sums_ref[...] = out
    total = lax.dot_general(mixed_ref[...], branch_ref[...], TN, preferred_element_type=F32)
    total = total.astype(BF16)
    for a in range(8):
        for b in range(2):
            for s in range(3):
                late_ref[16 * (2 * a + b) : 16 * (2 * a + b) + 16, SHARE * s : SHARE * (s + 1)] = total[
                    48 * a + 16 * s : 48 * a + 16 * s + 16, SHARE * b : SHARE * (b + 1)
                ]


def second_back(core, second, other, middle, top, mixed, w_out, gain):
    def whole(shape):
        return pl.BlockSpec(shape, lambda i, core: (0, 0))

    tokens = whole((TOK, WIDTH))
    return pl.pallas_call(
        second_back_kernel,
        grid_spec=pltpu.PrefetchScalarGridSpec(
            num_scalar_prefetch=1,
            grid=(1,),
            in_specs=[
                tokens,
                tokens,
                tokens,
                tokens,
                whole((TOK, SHARE)),
                pl.BlockSpec((SHARE, WIDTH), lambda i, core: (core[0], 0)),
                whole((1, WIDTH)),
            ],
            out_specs=[tokens, whole((TOK, SHARE)), whole((256, 3 * SHARE)), whole((8, WIDTH))],
            scratch_shapes=[pltpu.VMEM((TOK, WIDTH), BF16)],
        ),
        out_shape=[
            jax.ShapeDtypeStruct((TOK, WIDTH), F32),
            jax.ShapeDtypeStruct((TOK, SHARE), BF16),
            jax.ShapeDtypeStruct((256, 3 * SHARE), BF16),
            jax.ShapeDtypeStruct((8, WIDTH), F32),
        ],
        compiler_params=params(40),
        cost_estimate=cost(1e9, 4e6),
        name="second_back",
    )(core, second, other, middle, top, mixed, w_out, gain.reshape(1, WIDTH))


def first_back_kernel(
    x_ref, first_ref, grad_ref, w_ref, late_out_ref, sums_ref, in_sums_ref, late_ref, part_ref
):
    late_ref[: 3 * 256, : 3 * SHARE] = lax.dot_general(
        first_ref[...], grad_ref[...], TN, preferred_element_type=F32
    ).astype(BF16)
    late_ref[3 * 256 :, : 3 * SHARE] = late_out_ref[...]
    gain, bias, packed = 0.0, 0.0, 0.0
    for begin, end in PARTS:
        rows = slice(begin, end)
        grad = grad_ref[rows, :]
        part = lax.dot_general(grad, w_ref[...], NT, preferred_element_type=F32)
        part_ref[rows, :] = part
        gain += jnp.sum(part * norm_rows(x_ref[rows, :].astype(F32))[0], axis=0, keepdims=True)
        bias += jnp.sum(part, axis=0, keepdims=True)
        packed += jnp.sum(grad.astype(F32), axis=0, keepdims=True)
    vectors = [sums_ref[i : i + 1, :] for i in range(3)] + [gain, bias, sums_ref[3:4, :]]
    vectors += [packed[:, :SHARE], packed[:, 2 * SHARE :], in_sums_ref[:1, :]]
    late_ref[:, 3 * SHARE :] = jnp.zeros((16 * PEERS, 128), BF16)
    at = 0
    for vector in vectors:
        for tile in range(vector.shape[1] // 128):
            late_ref[16 * at : 16 * at + 16, 3 * SHARE :] = jnp.broadcast_to(
                vector[:, 128 * tile : 128 * (tile + 1)], (16, 128)
            ).astype(BF16)
            at += 1


def first_back(x, first, grad, w_packed, late_out, sums, in_sums):
    return pl.pallas_call(
        first_back_kernel,
        in_specs=[WHOLE] * 7,
        out_specs=[WHOLE, WHOLE],
        out_shape=[
            jax.ShapeDtypeStruct((16 * PEERS, LATE), BF16),
            jax.ShapeDtypeStruct((TOK, WIDTH), F32),
        ],
        compiler_params=params(40),
        cost_estimate=cost(1e9, 4e6),
        name="first_back",
    )(x, first, grad, w_packed, late_out, sums, in_sums)


def sum_kernel(parts_ref, *refs):
    total = parts_ref[0].astype(F32)
    for i in range(1, PEERS):
        total += parts_ref[i].astype(F32)
    refs[-1][...] = total.astype(BF16)


def sum_early(parts, after):
    return pl.pallas_call(
        sum_kernel,
        in_specs=[WHOLE] + [HBM] * len(after),
        out_specs=WHOLE,
        out_shape=jax.ShapeDtypeStruct(parts.shape[1:], BF16),
        compiler_params=params(16),
        cost_estimate=cost(0, 5e6),
        name="sum_early",
    )(parts, *after)


def sum_late_kernel(parts_ref, early_ref, *refs):
    share_ref = refs[-1]
    total = parts_ref[0].astype(F32)
    for i in range(1, PEERS):
        total += parts_ref[i].astype(F32)
    total = total.astype(BF16)
    share_ref[:, :WIDTH] = early_ref[...]
    for s in range(3):
        share_ref[16 * s : 16 * s + 16, WIDTH : WIDTH + SHARE] = total[:, SHARE * s : SHARE * (s + 1)]
        share_ref[16 * s : 16 * s + 16, WIDTH + SHARE :] = total[:, 3 * SHARE :]


def sum_late(parts, early, after):
    return pl.pallas_call(
        sum_late_kernel,
        in_specs=[WHOLE, WHOLE] + [HBM] * len(after),
        out_specs=WHOLE,
        out_shape=jax.ShapeDtypeStruct((48, WIDTH + SHARE + 128), BF16),
        compiler_params=params(16),
        cost_estimate=cost(0, 5e6),
        name="sum_late",
    )(parts, early, *after)


def widen_kernel(early_ref, late_ref, small_ref, *refs):
    back_ref, in_ref, packed_ref, out_ref, shared_ref, half_ref = refs[-6:]
    step, core = pl.program_id(0), pl.program_id(1)
    for group in range(8):
        rows = slice(48 * group, 48 * group + 48)
        for side in range(2):
            columns = slice(SHARE * side, SHARE * (side + 1))
            piece = early_ref[2 * group + side, 0]
            back_ref[rows, columns] = piece[:, :SHARE].astype(F32)
            in_ref[rows, columns] = piece[:, SHARE:].astype(F32)

    def packed(side):
        for peer in range(16):
            piece = late_ref[peer, 0].astype(F32)
            for kind in range(3):
                columns = slice(SHARE * (2 * kind + side), SHARE * (2 * kind + side + 1))
                packed_ref[16 * peer : 16 * peer + 16, columns] = piece[16 * kind : 16 * kind + 16]

    @pl.when((step < 3) & (core == 0))
    def _():
        packed(0)

    @pl.when((step < 3) & (core == 1))
    def _():
        packed(1)

    @pl.when(step == 3)
    def _():
        for a in range(8):
            for b in range(2):
                out_ref[48 * a : 48 * a + 48, SHARE * b : SHARE * (b + 1)] = late_ref[
                    2 * a + b, 0
                ].astype(F32)

    @pl.when((step == 0) & (core == 0))
    def _():
        for tile in range(6):
            columns = slice(128 * tile, 128 * (tile + 1))
            for vector in range(6):
                value = small_ref[6 * vector + tile, 0].astype(F32)
                if vector in (3, 4):
                    value += small_ref[6 * vector + tile, 1].astype(F32)
                shared_ref[8 * vector : 8 * vector + 8, columns] = value[:8]
        for side in range(2):
            for tile in range(3):
                columns = slice(128 * (3 * side + tile), 128 * (3 * side + tile + 1))
                for kind in range(2):
                    value = small_ref[36 + 3 * kind + tile, side].astype(F32)
                    half_ref[8 * kind : 8 * kind + 8, columns] = value[:8]
            for tile in range(12):
                columns = slice(128 * (12 * side + tile), 128 * (12 * side + tile + 1))
                half_ref[16:24, columns] = small_ref[42 + tile, side].astype(F32)[:8]


def widen(shares, after):
    block = (SHARE, WIDTH)
    return pl.pallas_call(
        widen_kernel,
        grid=(4, 2),
        in_specs=[
            pl.BlockSpec((16, 1, 48, WIDTH), lambda s, h: (s, h, 0, 0)),
            pl.BlockSpec((16, 1, 48, SHARE), lambda s, h: (s, h, 0, 2)),
            pl.BlockSpec((PEERS, 2, 16, 128), lambda s, h: (0, 0, 0, 9)),
        ]
        + [HBM] * len(after),
        out_specs=[
            pl.BlockSpec(block, lambda s, h: (4 * h + s, 0)),
            pl.BlockSpec(block, lambda s, h: (s % 2, 2 * h + s // 2)),
            pl.BlockSpec((256, 3 * WIDTH), lambda s, h: (jnp.minimum(s, 2), 0)),
            pl.BlockSpec(block, lambda s, h: (jnp.where(s == 3, h, 0), 0)),
            pl.BlockSpec((48, WIDTH), lambda s, h: (0, 0)),
            pl.BlockSpec((24, 2 * FF_SHARE), lambda s, h: (0, 0)),
        ],
        out_shape=[
            jax.ShapeDtypeStruct((2 * FF_SHARE, WIDTH), F32),
            jax.ShapeDtypeStruct((WIDTH, 2 * FF_SHARE), F32),
            jax.ShapeDtypeStruct((WIDTH, 3 * WIDTH), F32),
            jax.ShapeDtypeStruct((WIDTH, WIDTH), F32),
            jax.ShapeDtypeStruct((48, WIDTH), F32),
            jax.ShapeDtypeStruct((24, 2 * FF_SHARE), F32),
        ],
        compiler_params=params(40),
        cost_estimate=cost(0, 43e6),
        name="widen",
    )(shares, shares, shares, *after)


def norm_back(grad_normed, normed, inverse):
    return inverse * (
        grad_normed
        - jnp.mean(grad_normed, axis=-1, keepdims=True)
        - normed * jnp.mean(grad_normed * normed, axis=-1, keepdims=True)
    )


def matmul(left, right):
    return jnp.dot(left, right, preferred_element_type=F32)


def other_core(values):
    return lax.ppermute(values, "c", [(0, 1), (1, 0)])


def swap_home(values):
    return lax.ppermute(values, ("c", "zl"), [(1, 2), (2, 1)])


def body(
    inputs,
    segments,
    cotangent,
    ln1_gain,
    ln1_bias,
    w_qkv,
    q_bias,
    v_bias,
    w_out,
    out_bias,
    ln2_gain,
    ln2_bias,
    w_fc1,
    fc1_bias,
    w_fc2,
    fc2_bias,
):
    core = lax.axis_index("c")
    home = core == lax.axis_index("zl")
    first = core == 0
    which = core.reshape(1)

    def pair(mine, other, axis):
        return jnp.concatenate(
            [jnp.where(first, mine, other), jnp.where(first, other, mine)], axis=axis
        )

    def columns(array, size, start=0):
        return lax.dynamic_slice_in_dim(array, start + core * size, size, array.ndim - 1)

    def half(array, which):
        return lax.dynamic_slice_in_dim(array, which * HALF, HALF, 0)

    filling = jnp.broadcast_to(segments[:, :WIDTH].astype(BF16), (HALF - REAL, WIDTH))
    sent = jnp.concatenate([inputs[0], filling], axis=0)
    x_half = jnp.where(home, sent, swap_home(sent))
    x_all = pair(x_half, other_core(x_half), 0)
    flag = (x_all[REAL, 196:197] != x_all[REAL, :1]).astype(jnp.int32)
    rows = lax.broadcasted_iota(jnp.int32, (TOK, 1), 0)
    real = (rows < REAL) | ((rows >= HALF) & (rows < HALF + REAL))

    w_packed = jnp.concatenate([columns(w_qkv, SHARE, i * WIDTH) for i in range(3)], axis=1)
    packed_bias = jnp.concatenate(
        [columns(q_bias, SHARE), jnp.zeros((SHARE,), F32), columns(v_bias, SHARE)]
    )
    grad_sent = jnp.concatenate([cotangent[0], x_all[REAL:HALF]], axis=0)
    grad_half = jnp.where(home, grad_sent, swap_home(grad_sent))

    x_all = jnp.where(real, x_all, 0)
    normed_one, inverse_one = norm_rows(x_all.astype(F32))
    first_in = (normed_one * ln1_gain + ln1_bias).astype(BF16)
    packed = (matmul(first_in, w_packed) + packed_bias).astype(BF16)
    mixed, lse = attention_forward(flag, packed)
    filling = jnp.concatenate([mixed[REAL:HALF], mixed[REAL:HALF]], axis=1)
    grad_half = jnp.concatenate([grad_half[:REAL], filling], axis=0)
    grad_top = jnp.where(real, pair(grad_half, other_core(grad_half), 0), 0)
    middle, active, grad_hidden, early, in_sums = middle_part(
        which,
        mixed,
        other_core(mixed),
        x_all,
        w_out,
        out_bias,
        ln2_gain,
        ln2_bias,
        grad_top,
        w_fc1,
        fc1_bias,
        w_fc2,
    )
    product, second, second_low = ff_products(which, active, grad_hidden, w_fc2, w_fc1)
    grad_middle, grad_mixed, late_out, sums = second_back(
        which, second, other_core(second_low), middle, grad_top, mixed, w_out, ln2_gain
    )
    grad_packed = attention_backward(flag, packed, grad_mixed, mixed, lse)
    late, first_part = first_back(x_all, first_in, grad_packed, w_packed, late_out, sums, in_sums)
    early = sum_early(lax.all_to_all(early, CHIPS, 0, 0, tiled=True), after=(late,))

    result = (
        half(middle, core)
        + half(product, core)
        + other_core(half(product, 1 - core))
        + fc2_bias
    ).astype(BF16)
    output = jnp.where(home, result, swap_home(result))[None, :REAL]

    grad_first_in = half(first_part, core) + other_core(half(first_part, 1 - core))
    grad_input = half(grad_middle, core) + norm_back(
        grad_first_in * ln1_gain, half(normed_one, core), half(inverse_one, core)
    )
    grad_input = grad_input.astype(BF16)
    input_grad = jnp.where(home, grad_input, swap_home(grad_input))[None, :REAL]

    late = lax.all_to_all(late.reshape(PEERS, 16, LATE), CHIPS, 0, 0, tiled=True)
    share = sum_late(late, early, after=(result, grad_input))
    shares = lax.all_gather(share, CHIPS + ("c",)).reshape((PEERS, 2) + share.shape)
    total_back, total_in, total_packed, total_out, shared, halves = widen(
        shares, after=(output, input_grad)
    )
    return (
        output,
        input_grad,
        shared[24],
        shared[32],
        total_packed,
        halves[0, :WIDTH],
        halves[8, :WIDTH],
        total_out,
        shared[0],
        shared[8],
        shared[16],
        total_in,
        halves[16],
        total_back,
        shared[40],
    )


def solution(mesh):
    fine = Mesh(mesh.devices.reshape(4, 4, 2, 2, 2), ("x", "y", "zh", "c", "zl"))
    tokens = P(ROWS, "zl", None)
    return jax.shard_map(
        body,
        mesh=fine,
        in_specs=(tokens, P(ROWS, None), tokens) + (P(),) * 13,
        out_specs=(tokens, tokens) + (P(),) * 13,
        check_vma=False,
    )
```

```python
import jax
import jax.numpy as jnp
from jax import lax
from jax.experimental import pallas as pl
from jax.experimental.pallas import tpu as pltpu
from jax.sharding import Mesh
from jax.sharding import PartitionSpec as P


HALF = 496
TOK = 2 * HALF
REAL = 490
PAIR = 128
BIG_Q, BIG_K, BIG_STEP = 800, 896, 160
WIDTH = 768
SMALL_Q, SMALL_K = 208, 256
OFF = -1e30
F32, BF16 = jnp.float32, jnp.bfloat16
PARTS = ((0, 256), (256, 512), (512, 768), (768, TOK))
NT = (((1,), (1,)), ((), ()))
TN = (((0,), (0,)), ((), ()))


def windows(small_first):
    big = (
        pl.multiple_of(small_first * 192, 32),
        pl.multiple_of(small_first * 96, 32),
        small_first * 196,
        790 + small_first * 196,
    )
    small = (
        pl.multiple_of((1 - small_first) * 784, 16),
        pl.multiple_of((1 - small_first) * 736, 32),
        (1 - small_first) * 790,
        196 + (1 - small_first) * 790,
    )
    return big, small


def in_image(start, count, first, end):
    rows = start + lax.broadcasted_iota(jnp.int32, (count, PAIR), 0)
    return (rows >= first) & (rows < end) & ((rows < REAL) | (rows >= HALF))


def lanes(count):
    return lax.broadcasted_iota(jnp.int32, (count, PAIR), 1)


def own(lane, head):
    return lane < 64 if head == 0 else lane >= 64


def norm_rows(values):
    center = values - jnp.mean(values, axis=-1, keepdims=True)
    inverse = lax.rsqrt(jnp.mean(center * center, axis=-1, keepdims=True) + 1e-06)
    return center * inverse, inverse


def assemble(place, own_ref, swapped_ref, host_ref, guest_ref, rows_ref):
    core, home = place[0], place[1] == 1
    for half, at_home, away in ((core, own_ref, swapped_ref), (1 - core, guest_ref, host_ref)):
        start = pl.multiple_of(half * HALF, 16)
        rows_ref[pl.ds(pl.multiple_of(start + 488, 8), 8), :] = jnp.zeros((8, WIDTH), F32)

        @pl.when(home)
        def _():
            rows_ref[pl.ds(start, REAL), :] = at_home[...][:REAL].astype(F32)

        @pl.when(jnp.logical_not(home))
        def _():
            rows_ref[pl.ds(start, REAL), :] = away[...][:REAL].astype(F32)


def small_comes_first(place, segments_ref, other_ref):
    mine = segments_ref[0, 196] != segments_ref[0, 0]
    other = other_ref[0, 196] != other_ref[0, 0]
    return jnp.where(place[1] == 1, mine.astype(jnp.int32), other.astype(jnp.int32))


def vector(ref, start=0, size=WIDTH):
    return ref[pl.ds(start, size)].reshape(1, size)


def attend_kernel(
    place,
    segments_ref,
    other_segments_ref,
    own_ref,
    swapped_ref,
    host_ref,
    guest_ref,
    gain_ref,
    bias_ref,
    wq_ref,
    wk_ref,
    wv_ref,
    q_bias_ref,
    v_bias_ref,
    x_ref,
    first_ref,
    q_ref,
    k_ref,
    v_ref,
    mixed_ref,
    lse_ref,
    rows_ref,
):
    pair = pl.program_id(0)

    @pl.when(pair == 0)
    def _():
        assemble(place, own_ref, swapped_ref, host_ref, guest_ref, rows_ref)
        for begin, end in PARTS:
            rows = slice(begin, end)
            values = rows_ref[rows, :]
            x_ref[rows, :] = values.astype(BF16)
            first = norm_rows(values)[0] * vector(gain_ref) + vector(bias_ref)
            first_ref[rows, :] = first.astype(BF16)

    weights = jnp.concatenate([wq_ref[...], wk_ref[...], wv_ref[...]], axis=1)
    start = pl.multiple_of((3 * place[0] + pair) * PAIR, PAIR)
    q_bias, v_bias = vector(q_bias_ref, start, PAIR), vector(v_bias_ref, start, PAIR)
    for begin, end in PARTS:
        rows = slice(begin, end)
        packed = jnp.dot(first_ref[rows, :], weights, preferred_element_type=F32)
        q_ref[rows, :] = (packed[:, :PAIR] + q_bias).astype(BF16)
        k_ref[rows, :] = packed[:, PAIR : 2 * PAIR].astype(BF16)
        v_ref[rows, :] = (packed[:, 2 * PAIR :] + v_bias).astype(BF16)

    small_first = small_comes_first(place, segments_ref, other_segments_ref)
    big, small = windows(small_first)

    def image(window, queries, step, keys, merge):
        q_start, k_start, first, end = window
        lane_k = lanes(keys)
        bias = jnp.where(in_image(k_start, keys, first, end), 0.0, OFF)
        k_all = k_ref[pl.ds(k_start, keys), :].astype(F32)
        v_all = v_ref[pl.ds(k_start, keys), :].astype(F32)
        k_heads, v_heads = [], []
        for head in range(2):
            spare = 64 - 64 * head
            k_heads.append(
                jnp.where(own(lane_k, head), k_all, jnp.where(lane_k == spare, bias, 0.0)).astype(BF16)
            )
            v_heads.append(
                jnp.where(own(lane_k, head), v_all, jnp.where(lane_k == spare, 1.0, 0.0)).astype(BF16)
            )
        lane = lanes(step)
        for part in range(queries // step):
            start = pl.multiple_of(q_start + part * step, 16)
            here = pl.ds(start, step)
            q_part = q_ref[here, :].astype(F32) * 0.125
            outs, sums = [], []
            for head in range(2):
                spare = 64 - 64 * head
                q_head = jnp.where(
                    own(lane, head), q_part, jnp.where(lane == spare, 1.0, 0.0)
                ).astype(BF16)
                scores = lax.dot_general(q_head, k_heads[head], NT, preferred_element_type=F32)
                top = jnp.max(scores, axis=1, keepdims=True)
                weights = jnp.exp(scores - top).astype(BF16)
                out = jnp.dot(weights, v_heads[head], preferred_element_type=F32)
                total = out[:, spare : spare + 1]
                outs.append(out * (1.0 / total))
                sums.append(top + jnp.log(total))
            mixed = jnp.where(lane < 64, outs[0], outs[1])
            lse = jnp.where(lane < 64, sums[1], sums[0])
            if merge:
                rows = start + lax.broadcasted_iota(jnp.int32, (step, PAIR), 0)
                keep = (rows >= small[2]) & ((rows < 196) | (small_first == 0))
                mixed = jnp.where(keep, mixed_ref[here, :].astype(F32), mixed)
                lse = jnp.where(keep, lse_ref[here, :], lse)
            mixed_ref[here, :] = mixed.astype(BF16)
            lse_ref[here, :] = lse

    image(small, SMALL_Q, SMALL_Q, SMALL_K, False)
    image(big, BIG_Q, BIG_Q, BIG_K, True)


WHOLE = pl.BlockSpec(memory_space=pltpu.VMEM)
SCALARS = pl.BlockSpec(memory_space=pltpu.SMEM)
ANYWHERE = pl.BlockSpec(memory_space=pl.ANY)


def params(mib):
    return pltpu.CompilerParams(vmem_limit_bytes=mib * 2**20)


def cost(flops, traffic, transcendentals=0):
    return pl.CostEstimate(
        flops=int(flops), bytes_accessed=int(traffic), transcendentals=int(transcendentals)
    )


def far(array):
    return pltpu.with_memory_space_constraint(array, pltpu.HBM)


def block():
    return pl.BlockSpec((TOK, PAIR), lambda i, place: (0, i))


def whole(shape):
    return pl.BlockSpec(shape, lambda i, place: (0,) * len(shape))


def attend(place, segments, tokens, gain, bias, w_qkv, q_bias, v_bias):
    def weight(kind):
        return pl.BlockSpec((WIDTH, PAIR), lambda i, place: (0, 6 * kind + 3 * place[0] + i))

    all_tokens, received = whole((TOK, WIDTH)), whole((REAL, WIDTH))
    heads = pltpu.HBM((TOK, 3 * PAIR), BF16)
    return pl.pallas_call(
        attend_kernel,
        grid_spec=pltpu.PrefetchScalarGridSpec(
            num_scalar_prefetch=1,
            grid=(3,),
            in_specs=[SCALARS, SCALARS]
            + [received] * 4
            + [WHOLE, WHOLE, weight(0), weight(1), weight(2), WHOLE, WHOLE],
            out_specs=[all_tokens, all_tokens, block(), block(), block(), block(), block()],
            scratch_shapes=[pltpu.VMEM((TOK, WIDTH), F32)],
        ),
        out_shape=[
            pltpu.HBM((TOK, WIDTH), BF16),
            pltpu.HBM((TOK, WIDTH), BF16),
            heads,
            heads,
            heads,
            heads,
            pltpu.HBM((TOK, 3 * PAIR), F32),
        ],
        compiler_params=params(44),
        cost_estimate=cost(8e9, 15e6, 4e6),
        name="attend",
    )(
        place,
        *segments,
        *tokens,
        gain,
        bias,
        far(w_qkv),
        far(w_qkv),
        far(w_qkv),
        q_bias,
        v_bias,
    )


def split(values):
    high = values.astype(BF16).astype(F32)
    return high, values - high


def attention_back(pair, small_first, q_ref, k_ref, v_ref, grad_ref, mixed_ref, lse_ref, out_ref, scores_ref):
    big, small = windows(small_first)
    pair_lanes = pl.ds(pl.multiple_of(pair * PAIR, PAIR), PAIR)

    def lanes_of(kind):
        return pl.ds(pl.multiple_of((3 * kind + pair) * PAIR, PAIR), PAIR)

    def image(window, keys, step, queries, add):
        k_start, q_start, first, end = window
        here = pl.ds(q_start, queries)
        lane = lanes(queries)
        bias = jnp.where(in_image(q_start, queries, first, end), 0.0, OFF)
        q_all = q_ref[here, :].astype(F32) * 0.125
        q_low = q_all.astype(BF16)
        grad_low = grad_ref[here, pair_lanes]
        grad_all = grad_low.astype(F32)
        products = grad_all * mixed_ref[here, pair_lanes].astype(F32)
        lse_high, lse_rest = split(lse_ref[here, :])
        lse_mid, lse_low = split(lse_rest)
        q_heads, grad_heads = [], []
        for head in range(2):
            spare = 64 - 64 * head
            mine = own(lane, head)
            q_head = jnp.where(mine, q_all, 0.0)
            for at, extra in enumerate((1.0, -lse_high, -lse_mid, -lse_low, bias)):
                q_head = jnp.where(lane == spare + at, extra, q_head)
            q_heads.append(q_head.astype(BF16))
            row_term = jnp.sum(jnp.where(mine, products, 0.0), axis=1, keepdims=True)
            term_high, term_low = split(row_term)
            grad_head = jnp.where(mine, grad_all, 0.0)
            grad_head = jnp.where(lane == spare + 1, -term_high, grad_head)
            grad_head = jnp.where(lane == spare + 2, -term_low, grad_head)
            grad_heads.append(grad_head.astype(BF16))
        lane = lanes(step)
        for part in range(keys // step):
            start = pl.multiple_of(k_start + part * step, 16)
            rows = pl.ds(start, step)
            k_part = k_ref[rows, :].astype(F32)
            v_part = v_ref[rows, :].astype(F32)
            key_bias = jnp.where(in_image(start, step, first, end), 0.0, OFF)
            keys_grad, values_grad = [], []
            for head in range(2):
                spare = 64 - 64 * head
                mine = own(lane, head)
                ones = (lane >= spare + 1) & (lane <= spare + 4)
                k_head = jnp.where(mine, k_part, jnp.where(ones, 1.0, 0.0))
                k_head = jnp.where(lane == spare, key_bias, k_head).astype(BF16)
                v_head = jnp.where(mine, v_part, jnp.where(ones, 1.0, 0.0)).astype(BF16)
                probs = jnp.exp(
                    lax.dot_general(k_head, q_heads[head], NT, preferred_element_type=F32)
                )
                change = lax.dot_general(v_head, grad_heads[head], NT, preferred_element_type=F32)
                grad_scores = (probs * change).astype(BF16)
                values_grad.append(
                    jnp.dot(probs.astype(BF16), grad_low, preferred_element_type=F32)
                )
                keys_grad.append(jnp.dot(grad_scores, q_low, preferred_element_type=F32))
                scores_ref[head, part * step : (part + 1) * step, :queries] = grad_scores
            key_out = jnp.where(lane < 64, keys_grad[0], keys_grad[1]).astype(BF16)
            value_out = jnp.where(lane < 64, values_grad[0], values_grad[1]).astype(BF16)
            if add:
                key_out = key_out + out_ref[rows, lanes_of(1)]
                value_out = value_out + out_ref[rows, lanes_of(2)]
            out_ref[rows, lanes_of(1)] = key_out
            out_ref[rows, lanes_of(2)] = value_out
        k_all = k_ref[pl.ds(k_start, keys), :]
        turned = [
            lax.dot_general(k_all, scores_ref[head, :keys, :queries], TN, preferred_element_type=F32)
            for head in range(2)
        ]
        row = lax.broadcasted_iota(jnp.int32, (PAIR, queries), 0)
        query_out = jnp.transpose(jnp.where(row < 64, turned[0], turned[1]) * 0.125).astype(BF16)
        if add:
            query_out = query_out + out_ref[here, lanes_of(0)]
        out_ref[here, lanes_of(0)] = query_out

    out_ref[pl.ds(small[0], SMALL_Q), lanes_of(1)] = jnp.zeros((SMALL_Q, PAIR), BF16)
    out_ref[pl.ds(small[0], SMALL_Q), lanes_of(2)] = jnp.zeros((SMALL_Q, PAIR), BF16)
    out_ref[pl.ds(small[1], SMALL_K), lanes_of(0)] = jnp.zeros((SMALL_K, PAIR), BF16)
    image(big, BIG_Q, BIG_STEP, BIG_K, False)
    image(small, SMALL_Q, SMALL_Q, SMALL_K, True)


FF_SHARE = 1536
SUB = 256
SHARE = 384
PEERS = 64
LATE = 3 * SHARE + 128
LATE_HALF = LATE // 2
CHIPS = ("x", "y", "zh", "zl")
ROWS = ("x", "y", "zh", "c")

def middle_kernel(
    place,
    mixed_ref,
    other_ref,
    x_ref,
    w_out_ref,
    out_bias_ref,
    gain_ref,
    bias_ref,
    own_ref,
    swapped_ref,
    host_ref,
    guest_ref,
    w_in_ref,
    in_bias_ref,
    w_back_ref,
    middle_ref,
    grad_ref,
    active_ref,
    grad_hidden_ref,
    early_ref,
    sums_ref,
    second_ref,
    turned_ref,
    rows_ref,
):
    core, step = place[0], pl.program_id(0)

    @pl.when(step == 0)
    def _():
        mine = w_out_ref[pl.ds(pl.multiple_of(core * SHARE, 128), SHARE), :]
        other = w_out_ref[pl.ds(pl.multiple_of((1 - core) * SHARE, 128), SHARE), :]
        assemble(place, own_ref, swapped_ref, host_ref, guest_ref, rows_ref)
        grad_ref[...] = rows_ref[...].astype(BF16)
        for begin, end in PARTS:
            rows = slice(begin, end)
            branch = jnp.dot(mixed_ref[rows, :], mine, preferred_element_type=F32)
            branch += jnp.dot(other_ref[rows, :], other, preferred_element_type=F32)
            middle = x_ref[rows, :].astype(F32) + branch + vector(out_bias_ref)
            middle_ref[rows, :] = middle
            second = norm_rows(middle)[0] * vector(gain_ref) + vector(bias_ref)
            second_ref[rows, :] = second.astype(BF16)
        turned_ref[...] = jnp.transpose(second_ref[...])

    for sub in range(2):
        columns = slice(SUB * sub, SUB * (sub + 1))
        column_sums = 0.0
        start = pl.multiple_of(core * FF_SHARE + step * 512 + SUB * sub, SUB)
        in_bias = vector(in_bias_ref, start, SUB)
        for part in range(2):
            rows = slice(part * HALF, (part + 1) * HALF)
            hidden = jnp.dot(second_ref[rows, :], w_in_ref[:, columns], preferred_element_type=F32)
            hidden += in_bias
            grad_active = lax.dot_general(
                grad_ref[rows, :], w_back_ref[columns, :], NT, preferred_element_type=F32
            )
            below = 0.5 + 0.5 * lax.erf(hidden * 0.7071067811865476)
            active_ref[rows, columns] = (hidden * below).astype(BF16)
            slope = below + hidden * jnp.exp(hidden * hidden * -0.5) * 0.3989422804014327
            grad_hidden = (grad_active * slope).astype(BF16)
            grad_hidden_ref[rows, columns] = grad_hidden
            column_sums += jnp.sum(grad_hidden.astype(F32), axis=0, keepdims=True)
        sums_ref[:, columns] = jnp.broadcast_to(column_sums, (8, SUB))
        total = jnp.dot(
            turned_ref[...], grad_hidden_ref[:, columns], preferred_element_type=F32
        ).astype(BF16)
        for tile in range(2):
            for group in range(16):
                for third in range(3):
                    row = 48 * group + 16 * third
                    early_ref[4 * group + 2 * sub + tile, :, SHARE + 128 * third : SHARE + 128 * (third + 1)] = (
                        total[row : row + 16, 128 * tile : 128 * (tile + 1)]
                    )
        total = lax.dot_general(
            active_ref[:, columns], grad_ref[...], TN, preferred_element_type=F32
        ).astype(BF16)
        for group in range(16):
            for side in range(2):
                early_ref[32 * sub + 2 * group + side, :, :SHARE] = total[
                    16 * group : 16 * group + 16, SHARE * side : SHARE * (side + 1)
                ]


def middle_part(
    place, mixed, other, x, w_out, out_bias, gain, bias, grads, w_fc1, fc1_bias, w_fc2
):
    tokens, heads = whole((TOK, WIDTH)), whole((TOK, SHARE))
    ff_columns = pl.BlockSpec((TOK, 512), lambda i, place: (0, i))
    return pl.pallas_call(
        middle_kernel,
        grid_spec=pltpu.PrefetchScalarGridSpec(
            num_scalar_prefetch=1,
            grid=(3,),
            in_specs=[heads, heads, tokens, whole((WIDTH, WIDTH)), WHOLE, WHOLE, WHOLE]
            + [whole(a.shape) for a in grads]
            + [
                pl.BlockSpec((WIDTH, 512), lambda i, place: (0, place[0] * 3 + i)),
                WHOLE,
                pl.BlockSpec((512, WIDTH), lambda i, place: (place[0] * 3 + i, 0)),
            ],
            out_specs=[
                tokens,
                tokens,
                ff_columns,
                ff_columns,
                pl.BlockSpec((PEERS, 16, WIDTH), lambda i, place: (0, i, 0)),
                pl.BlockSpec((8, 512), lambda i, place: (0, i)),
            ],
            scratch_shapes=[
                pltpu.VMEM((TOK, WIDTH), BF16),
                pltpu.VMEM((WIDTH, TOK), BF16),
                pltpu.VMEM((TOK, WIDTH), F32),
            ],
        ),
        out_shape=[
            pltpu.HBM((TOK, WIDTH), F32),
            pltpu.HBM((TOK, WIDTH), BF16),
            pltpu.HBM((TOK, FF_SHARE), BF16),
            pltpu.HBM((TOK, FF_SHARE), BF16),
            pltpu.HBM((PEERS, 48, WIDTH), BF16),
            jax.ShapeDtypeStruct((8, FF_SHARE), F32),
        ],
        compiler_params=params(50),
        cost_estimate=cost(10.5e9, 30e6, 3e6),
        name="middle_part",
    )(
        place,
        far(mixed),
        other,
        far(x),
        far(w_out),
        out_bias,
        gain,
        bias,
        *grads,
        far(w_fc1),
        fc1_bias,
        far(w_fc2),
    )


def ff_products_kernel(place, active_ref, grad_ref, w_back_ref, w_in_ref, low_ref, sent_ref, own_ref):
    second = lax.dot_general(grad_ref[...], w_in_ref[...], NT, preferred_element_type=F32)
    low_ref[...] = second.astype(BF16)
    product = jnp.dot(active_ref[...], w_back_ref[...], preferred_element_type=F32)

    @pl.when(pl.program_id(0) == 0)
    def _():
        sent_ref[...] = product.astype(BF16)

    @pl.when(pl.program_id(0) == 1)
    def _():
        own_ref[...] = product


def ff_products(place, active, grad_hidden, w_fc2, w_fc1):
    def tokens(columns):
        return pl.BlockSpec(
            (HALF, columns), lambda i, place: (jnp.where(i == 0, 1 - place[0], place[0]), 0)
        )

    return pl.pallas_call(
        ff_products_kernel,
        grid_spec=pltpu.PrefetchScalarGridSpec(
            num_scalar_prefetch=1,
            grid=(2,),
            in_specs=[
                tokens(FF_SHARE),
                tokens(FF_SHARE),
                pl.BlockSpec((FF_SHARE, WIDTH), lambda i, place: (place[0], 0)),
                pl.BlockSpec((WIDTH, FF_SHARE), lambda i, place: (0, place[0])),
            ],
            out_specs=[tokens(WIDTH), whole((HALF, WIDTH)), whole((HALF, WIDTH))],
        ),
        out_shape=[
            pltpu.HBM((TOK, WIDTH), BF16),
            pltpu.HBM((HALF, WIDTH), BF16),
            pltpu.HBM((HALF, WIDTH), F32),
        ],
        compiler_params=params(40),
        cost_estimate=cost(1e9, 4e6),
        name="ff_products",
    )(place, far(active), far(grad_hidden), far(w_fc2), far(w_fc1))


def attend_back_kernel(
    place,
    segments_ref,
    other_segments_ref,
    second_ref,
    other_ref,
    middle_ref,
    top_ref,
    mixed_ref,
    w_out_ref,
    gain_ref,
    in_sums_ref,
    x_hbm,
    first_hbm,
    w_hbm,
    q_ref,
    k_ref,
    v_ref,
    lse_ref,
    *refs,
):
    slots, (grad_middle_ref, own_ref, sent_ref), refs = refs[:8], refs[8:11], refs[11:]
    (
        late_ref,
        branch_ref,
        grad_mixed_ref,
        packed_ref,
        scores_ref,
        sums_ref,
        x_ref,
        first_ref,
        w_ref,
        arrived,
        left,
    ) = refs
    pair, core = pl.program_id(0), place[0]
    copies = [
        pltpu.make_async_copy(x_hbm, x_ref, arrived.at[0]),
        pltpu.make_async_copy(first_hbm, first_ref, arrived.at[1]),
    ]
    for kind in range(3):
        start = pl.multiple_of(kind * WIDTH + core * SHARE, 128)
        copies.append(
            pltpu.make_async_copy(
                w_hbm.at[:, pl.ds(start, SHARE)],
                w_ref.at[:, pl.ds(kind * SHARE, SHARE)],
                arrived.at[2 + kind],
            )
        )

    def half_rows(which, begin, end):
        return pl.ds(pl.multiple_of(which * HALF + begin, 16), end - begin)

    @pl.when(pair == 0)
    def _():
        for copy in copies:
            copy.start()
        sums = [0.0, 0.0, 0.0, 0.0]
        for which in (core, 1 - core):
            for begin, end in ((0, 256), (256, HALF)):
                rows = half_rows(which, begin, end)
                grad = second_ref[rows, :].astype(F32) + other_ref[rows, :].astype(F32)
                normed, inverse = norm_rows(middle_ref[rows, :])
                product = grad * normed
                scaled = grad * vector(gain_ref)
                top = top_ref[rows, :].astype(F32)
                grad_middle = top + inverse * (
                    scaled
                    - jnp.mean(scaled, axis=-1, keepdims=True)
                    - normed * jnp.mean(product * vector(gain_ref), axis=-1, keepdims=True)
                )
                if which is core:
                    grad_middle_ref[begin:end, :] = grad_middle
                branch = grad_middle.astype(BF16)
                branch_ref[rows, :] = branch
                grad_mixed_ref[rows, :] = lax.dot_general(
                    branch, w_out_ref[...], NT, preferred_element_type=F32
                ).astype(BF16)
                for i, values in enumerate((branch.astype(F32), product, grad, top)):
                    sums[i] += jnp.sum(values, axis=0, keepdims=True)
        for i in range(4):
            sums_ref[8 * i : 8 * i + 8, :] = jnp.broadcast_to(sums[i], (8, WIDTH))
        total = lax.dot_general(mixed_ref[...], branch_ref[...], TN, preferred_element_type=F32)
        total = total.astype(BF16)
        for a in range(8):
            for b in range(2):
                for s in range(3):
                    row = WIDTH + 16 * (2 * a + b)
                    late_ref[row : row + 16, SHARE * s : SHARE * (s + 1)] = total[
                        48 * a + 16 * s : 48 * a + 16 * s + 16, SHARE * b : SHARE * (b + 1)
                    ]

    attention_back(
        pair,
        small_comes_first(place, segments_ref, other_segments_ref),
        q_ref,
        k_ref,
        v_ref,
        grad_mixed_ref,
        mixed_ref,
        lse_ref,
        packed_ref,
        scores_ref,
    )

    @pl.when(pair == 2)
    def _():
        for copy in copies:
            copy.wait()
        late_ref[:WIDTH, : 3 * SHARE] = lax.dot_general(
            first_ref[...], packed_ref[...], TN, preferred_element_type=F32
        ).astype(BF16)
        gain, bias, packed = 0.0, 0.0, 0.0
        for which in (core, 1 - core):
            for begin, end in ((0, 256), (256, HALF)):
                rows = half_rows(which, begin, end)
                grad = packed_ref[rows, :]
                part = lax.dot_general(grad, w_ref[...], NT, preferred_element_type=F32)
                if which is core:
                    own_ref[begin:end, :] = part
                else:
                    sent_ref[begin:end, :] = part.astype(BF16)
                gain += jnp.sum(
                    part * norm_rows(x_ref[rows, :].astype(F32))[0], axis=0, keepdims=True
                )
                bias += jnp.sum(part, axis=0, keepdims=True)
                packed += jnp.sum(grad.astype(F32), axis=0, keepdims=True)
        pieces = [sums_ref[8 * i : 8 * i + 1, :] for i in range(3)]
        pieces += [gain, bias, sums_ref[24:25, :]]
        pieces += [packed[:, :SHARE], packed[:, 2 * SHARE :], in_sums_ref[:1, :]]
        late_ref[:, 3 * SHARE :] = jnp.zeros((16 * PEERS, 128), BF16)
        at = 0
        for piece in pieces:
            for tile in range(piece.shape[1] // 128):
                late_ref[16 * at : 16 * at + 16, 3 * SHARE :] = jnp.broadcast_to(
                    piece[:, 128 * tile : 128 * (tile + 1)], (16, 128)
                ).astype(BF16)
                at += 1
        parts = []
        for side in range(2):
            for hop in range(4):
                start = pl.multiple_of(256 * lax.rem(place[2 + side] + hop, 4), 256)
                parts.append(
                    pltpu.make_async_copy(
                        late_ref.at[pl.ds(start, 256), pl.ds(LATE_HALF * side, LATE_HALF)],
                        slots[4 * side + hop],
                        left.at[4 * side + hop],
                    )
                )
        for copy in parts:
            copy.start()
        for copy in parts:
            copy.wait()


def attend_back(
    place, segments, second, other, middle, top, mixed, w_out, gain, in_sums, x, first, w_qkv, heads
):
    def once(shape, index=lambda i, place: (0, 0)):
        return pl.BlockSpec(shape, index, pipeline_mode=pl.Buffered(1))

    tokens, half = once((TOK, WIDTH)), whole((HALF, WIDTH))
    return pl.pallas_call(
        attend_back_kernel,
        grid_spec=pltpu.PrefetchScalarGridSpec(
            num_scalar_prefetch=1,
            grid=(3,),
            in_specs=[
                SCALARS,
                SCALARS,
                tokens,
                tokens,
                tokens,
                tokens,
                once((TOK, SHARE)),
                once((SHARE, WIDTH), lambda i, place: (place[0], 0)),
                WHOLE,
                WHOLE,
                ANYWHERE,
                ANYWHERE,
                ANYWHERE,
            ]
            + [block()] * 4,
            out_specs=[ANYWHERE] * 8 + [half, half, half],
            scratch_shapes=[
                pltpu.VMEM((16 * PEERS, LATE), BF16),
                pltpu.VMEM((TOK, WIDTH), BF16),
                pltpu.VMEM((TOK, SHARE), BF16),
                pltpu.VMEM((TOK, 3 * SHARE), BF16),
                pltpu.VMEM((2, BIG_Q, BIG_K), BF16),
                pltpu.VMEM((32, WIDTH), F32),
                pltpu.VMEM((TOK, WIDTH), BF16),
                pltpu.VMEM((TOK, WIDTH), BF16),
                pltpu.VMEM((WIDTH, 3 * SHARE), BF16),
                pltpu.SemaphoreType.DMA((5,)),
                pltpu.SemaphoreType.DMA((8,)),
            ],
        ),
        out_shape=[pltpu.HBM((256, LATE_HALF), BF16)] * 8
        + [
            pltpu.HBM((HALF, WIDTH), F32),
            pltpu.HBM((HALF, WIDTH), F32),
            pltpu.HBM((HALF, WIDTH), BF16),
        ],
        compiler_params=params(54),
        cost_estimate=cost(1e9, 4e6),
        name="attend_back",
    )(
        place,
        *segments,
        far(second),
        other,
        far(middle),
        far(top),
        far(mixed),
        far(w_out),
        gain,
        in_sums,
        far(x),
        far(first),
        far(w_qkv),
        *(far(a) for a in heads),
    )


def sum_early_kernel(parts_ref, total_ref):
    total = parts_ref[0].astype(F32)
    for i in range(1, PEERS):
        total += parts_ref[i].astype(F32)
    total_ref[...] = total.astype(BF16)


def sum_early(parts, after):
    def kernel(parts_ref, *refs):
        sum_early_kernel(parts_ref, refs[-1])

    return pl.pallas_call(
        kernel,
        grid=(2,),
        in_specs=[pl.BlockSpec((PEERS, 48, SHARE), lambda i: (0, 0, i))] + [ANYWHERE] * len(after),
        out_specs=pl.BlockSpec((48, SHARE), lambda i: (0, i)),
        out_shape=pltpu.HBM(parts.shape[1:], BF16),
        compiler_params=params(16),
        cost_estimate=cost(0, 5e6),
        name="sum_early",
    )(far(parts), *after)


def small_call(kernel, name, arrays, shapes, place, scratch=(), after=()):
    count = 1 + len(arrays)

    def body(*refs):
        kernel(*refs[:count], *refs[count + len(after) :])

    return pl.pallas_call(
        body,
        in_specs=[SCALARS] + [WHOLE] * len(arrays) + [ANYWHERE] * len(after),
        out_specs=[WHOLE] * len(shapes),
        out_shape=[jax.ShapeDtypeStruct(shape, BF16) for shape in shapes],
        scratch_shapes=list(scratch),
        compiler_params=params(16),
        cost_estimate=cost(0, 2e6),
        name=name,
    )(place, *arrays, *after)


def total_of(refs):
    total = refs[0][...].astype(F32)
    for ref in refs[1:]:
        total += ref[...].astype(F32)
    return total.astype(BF16)


def turn(place, axis, hop, size):
    return pl.ds(pl.multiple_of(size * lax.rem(place[axis] + hop, 4), size), size)


def sum_first_kernel(place, *refs):
    scratch = refs[-1]
    for side in range(2):
        scratch[...] = total_of(refs[4 * side : 4 * side + 4])
        for hop in range(4):
            refs[8 + 4 * side + hop][...] = scratch[turn(place, 3 - side, hop, 64), :]


def sum_second_kernel(place, *refs):
    scratch = refs[-1]
    for side in range(2):
        columns = slice(LATE_HALF * side, LATE_HALF * (side + 1))
        scratch[:, columns] = total_of(refs[4 * side : 4 * side + 4])
    for hop in range(4):
        refs[8 + hop][...] = scratch[turn(place, 4, hop, 16), :]


def sum_third_kernel(place, *refs):
    refs[-1][...] = total_of(refs[:4])


def join_third_kernel(place, *refs):
    for hop in range(4):
        rows = turn(place, 4, 4 - hop, 16)
        for side in range(2):
            columns = slice(LATE_HALF * side, LATE_HALF * (side + 1))
            refs[4 + side][rows, :] = refs[hop][:, columns]


def join_second_kernel(place, *refs):
    for side in range(2):
        for hop in range(4):
            refs[8 + side][turn(place, 3 - side, 4 - hop, 64), :] = refs[4 * side + hop][...]


def join_first_kernel(place, *refs):
    for side in range(2):
        columns = slice(LATE_HALF * side, LATE_HALF * (side + 1))
        for hop in range(4):
            refs[8][turn(place, 2 + side, 4 - hop, 256), columns] = refs[4 * side + hop][...]


def around(parts, axis):
    return [parts[0]] + [
        lax.ppermute(parts[hop], axis, [(i, (i + hop) % 4) for i in range(4)]) for hop in (1, 2, 3)
    ]


def sum_late(parts, place, early, meanwhile, latest):
    depth = ("zh", "zl")
    parts = small_call(
        sum_first_kernel,
        "sum_first",
        parts,
        [(64, LATE_HALF)] * 8,
        place,
        [pltpu.VMEM((256, LATE_HALF), BF16)],
        (early,),
    )
    parts = around(parts[:4], "y") + around(parts[4:], "x")
    parts = small_call(
        sum_second_kernel,
        "sum_second",
        parts,
        [(16, LATE)] * 4,
        place,
        [pltpu.VMEM((64, LATE), BF16)],
        meanwhile,
    )
    (share,) = small_call(sum_third_kernel, "sum_third", around(parts, depth), [(16, LATE)], place)
    one, two = small_call(
        join_third_kernel, "join_third", around([share] * 4, depth), [(64, LATE_HALF)] * 2, place
    )
    parts = around([one] * 4, "y") + around([two] * 4, "x")
    one, two = small_call(
        join_second_kernel, "join_second", parts, [(256, LATE_HALF)] * 2, place, after=latest
    )
    return around([one] * 4, "x") + around([two] * 4, "y")


def join_late(parts, place):
    return small_call(join_first_kernel, "join_first", parts, [(16 * PEERS, LATE)], place)[0]


def widen_late_kernel(
    place,
    mine_ref,
    other_ref,
    mine_small_ref,
    other_small_ref,
    *refs,
):
    packed_ref, out_ref, shared_ref, half_ref = refs[-4:]
    step, first = pl.program_id(0), place[0] == 0

    def pick(side, mine_ref, other_ref, rows, columns):
        mine, other = mine_ref[rows, columns].astype(F32), other_ref[rows, columns].astype(F32)
        return jnp.where(first if side == 0 else jnp.logical_not(first), mine, other)

    @pl.when(step < 3)
    def _():
        for side in range(2):
            for kind in range(3):
                at = SHARE * (2 * kind + side)
                packed_ref[:, at : at + SHARE] = pick(
                    side, mine_ref, other_ref, slice(0, 256), slice(SHARE * kind, SHARE * (kind + 1))
                )

    @pl.when(step == 3)
    def _():
        for side in range(2):
            for a in range(8):
                for b in range(2):
                    row = 16 * (2 * a + b)
                    for s in range(3):
                        at = SHARE * side + 48 * a + 16 * s
                        out_ref[at : at + 16, SHARE * b : SHARE * (b + 1)] = pick(
                            side,
                            mine_ref,
                            other_ref,
                            slice(row, row + 16),
                            slice(SHARE * s, SHARE * (s + 1)),
                        )

    @pl.when(step == 0)
    def _():
        def piece(side, at):
            rows = slice(16 * at, 16 * at + 16)
            return pick(side, mine_small_ref, other_small_ref, rows, slice(0, 128))[:8]

        for tile in range(6):
            columns = slice(128 * tile, 128 * (tile + 1))
            for at in range(6):
                value = piece(0, 6 * at + tile)
                if at in (3, 4):
                    value += piece(1, 6 * at + tile)
                shared_ref[8 * at : 8 * at + 8, columns] = value
        for side in range(2):
            for tile in range(3):
                columns = slice(128 * (3 * side + tile), 128 * (3 * side + tile + 1))
                for kind in range(2):
                    half_ref[8 * kind : 8 * kind + 8, columns] = piece(side, 36 + 3 * kind + tile)
            for tile in range(12):
                columns = slice(128 * (12 * side + tile), 128 * (12 * side + tile + 1))
                half_ref[16:24, columns] = piece(side, 42 + tile)


def widen_late(place, mine, other, after):
    rows = pl.BlockSpec((256, LATE), lambda i, place: (i, 0))
    small = pl.BlockSpec((16 * PEERS, 128), lambda i, place: (0, 9))
    return pl.pallas_call(
        widen_late_kernel,
        grid_spec=pltpu.PrefetchScalarGridSpec(
            num_scalar_prefetch=1,
            grid=(4,),
            in_specs=[rows, rows, small, small] + [ANYWHERE] * len(after),
            out_specs=[
                pl.BlockSpec((256, 3 * WIDTH), lambda i, place: (jnp.minimum(i, 2), 0)),
                whole((WIDTH, WIDTH)),
                whole((48, WIDTH)),
                whole((24, 2 * FF_SHARE)),
            ],
        ),
        out_shape=[
            pltpu.HBM((WIDTH, 3 * WIDTH), F32),
            pltpu.HBM((WIDTH, WIDTH), F32),
            jax.ShapeDtypeStruct((48, WIDTH), F32),
            jax.ShapeDtypeStruct((24, 2 * FF_SHARE), F32),
        ],
        compiler_params=params(24),
        cost_estimate=cost(0, 15e6),
        name="widen_late",
    )(place, far(mine), far(other), far(mine), far(other), *(far(a) for a in after))


def widen_early_kernel(shares_ref, *refs):
    back_ref, in_ref = refs[-2:]
    for group in range(32):
        for half in range(2):
            back_ref[16 * group : 16 * group + 16, SHARE * half : SHARE * (half + 1)] = shares_ref[
                2 * group + half, 0, :, :SHARE
            ].astype(F32)
    for group in range(16):
        for tile in range(4):
            for third in range(3):
                row = 48 * group + 16 * third
                in_ref[row : row + 16, 128 * tile : 128 * (tile + 1)] = shares_ref[
                    4 * group + tile, 0, :, SHARE + 128 * third : SHARE + 128 * (third + 1)
                ].astype(F32)


def widen_early(shares, after):
    return pl.pallas_call(
        widen_early_kernel,
        grid=(2, 3),
        in_specs=[pl.BlockSpec((PEERS, 1, 16, WIDTH), lambda h, i: (0, h, i, 0))]
        + [ANYWHERE] * len(after),
        out_specs=[
            pl.BlockSpec((512, WIDTH), lambda h, i: (3 * h + i, 0)),
            pl.BlockSpec((WIDTH, 512), lambda h, i: (0, 3 * h + i)),
        ],
        out_shape=[
            pltpu.HBM((2 * FF_SHARE, WIDTH), F32),
            pltpu.HBM((WIDTH, 2 * FF_SHARE), F32),
        ],
        compiler_params=params(24),
        cost_estimate=cost(0, 28e6),
        name="widen_early",
    )(far(shares), *after)


def norm_back(grad_normed, normed, inverse):
    return inverse * (
        grad_normed
        - jnp.mean(grad_normed, axis=-1, keepdims=True)
        - normed * jnp.mean(grad_normed * normed, axis=-1, keepdims=True)
    )


def other_core(values):
    return lax.ppermute(values, "c", [(0, 1), (1, 0)])


def swap_home(values):
    return lax.ppermute(values, ("c", "zl"), [(1, 2), (2, 1)])


def from_host(values):
    return lax.ppermute(values, ("c", "zl"), [(0, 2), (3, 1)])


def from_guest(values):
    return lax.ppermute(values, ("c", "zl"), [(2, 0), (1, 3)])


def from_next(values):
    return lax.ppermute(values, ("c", "zl"), [(1, 0), (2, 3)])


def body(
    inputs,
    segments,
    cotangent,
    ln1_gain,
    ln1_bias,
    w_qkv,
    q_bias,
    v_bias,
    w_out,
    out_bias,
    ln2_gain,
    ln2_bias,
    w_fc1,
    fc1_bias,
    w_fc2,
    fc2_bias,
):
    core = lax.axis_index("c")
    home = core == lax.axis_index("zl")

    def half(array, which):
        return lax.dynamic_slice_in_dim(array, which * HALF, HALF, 0)

    tokens, top = inputs[0], cotangent[0]
    swapped = swap_home(tokens)
    rows = (tokens, swapped, from_host(tokens), from_guest(swapped))
    images = (segments, other_core(segments))
    depth = 2 * lax.axis_index("zh") + lax.axis_index("zl")
    place = [core, home, lax.axis_index("x"), lax.axis_index("y"), depth]
    place = jnp.stack([index.astype(jnp.int32) for index in place])

    sent = jnp.concatenate([top, swapped[: HALF - REAL]], axis=0)
    tops = (top, swap_home(sent), from_host(top), from_next(sent))

    x_all, first_in, query, key, value, mixed, lse = attend(
        place, images, rows, ln1_gain, ln1_bias, w_qkv, q_bias, v_bias
    )
    middle, grad_top, active, grad_hidden, early, in_sums = middle_part(
        place,
        mixed,
        other_core(mixed),
        x_all,
        w_out,
        out_bias,
        ln2_gain,
        ln2_bias,
        tops,
        w_fc1,
        fc1_bias,
        w_fc2,
    )
    second, product_sent, product = ff_products(place, active, grad_hidden, w_fc2, w_fc1)
    *late, grad_middle, first_part, first_sent = attend_back(
        place,
        images,
        second,
        other_core(second),
        middle,
        grad_top,
        mixed,
        w_out,
        ln2_gain,
        in_sums,
        x_all,
        first_in,
        w_qkv,
        (query, key, value, lse),
    )
    result = half(middle, core) + product + other_core(product_sent).astype(F32) + fc2_bias
    result = result.astype(BF16)
    output = jnp.where(home, result, swap_home(result))[None, :REAL]

    grad_first_in = first_part + other_core(first_sent).astype(F32)
    normed_one, inverse_one = norm_rows(half(x_all, core).astype(F32))
    grad_input = grad_middle + norm_back(grad_first_in * ln1_gain, normed_one, inverse_one)
    grad_input = grad_input.astype(BF16)
    input_grad = jnp.where(home, grad_input, swap_home(grad_input))[None, :REAL]

    late = around(late[:4], "x") + around(late[4:], "y")
    early = lax.all_to_all(early, CHIPS, 0, 0, tiled=True)
    early = sum_early(early, (*late[1:4], *late[5:], result))
    shares = lax.all_gather(early, CHIPS + ("c",)).reshape(PEERS, 2, 48, WIDTH)

    late = sum_late(late, place, early, (grad_input,), (output, input_grad))
    total_back, total_in = widen_early(shares, after=(late[1],))
    late = join_late(late, place)
    total_packed, total_out, shared, halves = widen_late(
        place, late, other_core(late), after=(total_back, total_in)
    )
    return (
        output,
        input_grad,
        shared[24],
        shared[32],
        total_packed,
        halves[0, :WIDTH],
        halves[8, :WIDTH],
        total_out,
        shared[0],
        shared[8],
        shared[16],
        total_in,
        halves[16],
        total_back,
        shared[40],
    )


def solution(mesh):
    fine = Mesh(mesh.devices.reshape(4, 4, 2, 2, 2), ("x", "y", "zh", "c", "zl"))
    tokens = P(ROWS, "zl", None)
    return jax.shard_map(
        body,
        mesh=fine,
        in_specs=(tokens, P(ROWS, None), tokens) + (P(),) * 13,
        out_specs=(tokens, tokens) + (P(),) * 13,
        check_vma=False,
    )
```

```python
import jax
import jax.numpy as jnp
from jax import lax
from jax.experimental import pallas as pl
from jax.experimental.pallas import tpu as pltpu
from jax.sharding import Mesh
from jax.sharding import PartitionSpec as P


HALF = 496
TOK = 2 * HALF
REAL = 490
PAIR = 128
BIG_Q, BIG_K, BIG_STEP = 800, 896, 160
WIDTH = 768
SMALL_Q, SMALL_K = 208, 256
OFF = -1e30
F32, BF16 = jnp.float32, jnp.bfloat16
PARTS = ((0, 256), (256, 512), (512, 768), (768, TOK))
NT = (((1,), (1,)), ((), ()))
TN = (((0,), (0,)), ((), ()))


def windows(small_first):
    big = (
        pl.multiple_of(small_first * 192, 32),
        pl.multiple_of(small_first * 96, 32),
        small_first * 196,
        790 + small_first * 196,
    )
    small = (
        pl.multiple_of((1 - small_first) * 784, 16),
        pl.multiple_of((1 - small_first) * 736, 32),
        (1 - small_first) * 790,
        196 + (1 - small_first) * 790,
    )
    return big, small


def in_image(start, count, first, end):
    rows = start + lax.broadcasted_iota(jnp.int32, (count, PAIR), 0)
    return (rows >= first) & (rows < end) & ((rows < REAL) | (rows >= HALF))


def lanes(count):
    return lax.broadcasted_iota(jnp.int32, (count, PAIR), 1)


def own(lane, head):
    return lane < 64 if head == 0 else lane >= 64


def norm_rows(values):
    center = values - jnp.mean(values, axis=-1, keepdims=True)
    inverse = lax.rsqrt(jnp.mean(center * center, axis=-1, keepdims=True) + 1e-06)
    return center * inverse, inverse


def assemble(place, own_ref, swapped_ref, host_ref, guest_ref, rows_ref):
    core, home = place[0], place[1] == 1
    for half, at_home, away in ((core, own_ref, swapped_ref), (1 - core, guest_ref, host_ref)):
        start = pl.multiple_of(half * HALF, 16)
        rows_ref[pl.ds(pl.multiple_of(start + 488, 8), 8), :] = jnp.zeros((8, WIDTH), F32)

        @pl.when(home)
        def _():
            rows_ref[pl.ds(start, REAL), :] = at_home[...][:REAL].astype(F32)

        @pl.when(jnp.logical_not(home))
        def _():
            rows_ref[pl.ds(start, REAL), :] = away[...][:REAL].astype(F32)


def small_comes_first(place, segments_ref, other_ref):
    mine = segments_ref[0, 196] != segments_ref[0, 0]
    other = other_ref[0, 196] != other_ref[0, 0]
    return jnp.where(place[1] == 1, mine.astype(jnp.int32), other.astype(jnp.int32))


def vector(ref, start=0, size=WIDTH):
    return ref[pl.ds(start, size)].reshape(1, size)


def attend_kernel(
    place,
    segments_ref,
    other_segments_ref,
    own_ref,
    swapped_ref,
    host_ref,
    guest_ref,
    gain_ref,
    bias_ref,
    wq_ref,
    wk_ref,
    wv_ref,
    q_bias_ref,
    v_bias_ref,
    x_hbm,
    first_hbm,
    q_ref,
    k_ref,
    v_ref,
    mixed_ref,
    lse_ref,
    x_ref,
    first_ref,
    rows_ref,
    left,
):
    pair = pl.program_id(0)
    copies = [
        pltpu.make_async_copy(x_ref, x_hbm, left.at[0]),
        pltpu.make_async_copy(first_ref, first_hbm, left.at[1]),
    ]

    @pl.when(pair == 0)
    def _():
        assemble(place, own_ref, swapped_ref, host_ref, guest_ref, rows_ref)
        for begin, end in PARTS:
            rows = slice(begin, end)
            values = rows_ref[rows, :]
            x_ref[rows, :] = values.astype(BF16)
            first = norm_rows(values)[0] * vector(gain_ref) + vector(bias_ref)
            first_ref[rows, :] = first.astype(BF16)
        for copy in copies:
            copy.start()

    weights = jnp.concatenate([wq_ref[...], wk_ref[...], wv_ref[...]], axis=1)
    start = pl.multiple_of((3 * place[0] + pair) * PAIR, PAIR)
    q_bias, v_bias = vector(q_bias_ref, start, PAIR), vector(v_bias_ref, start, PAIR)
    for begin, end in PARTS:
        rows = slice(begin, end)
        packed = jnp.dot(first_ref[rows, :], weights, preferred_element_type=F32)
        q_ref[rows, :] = (packed[:, :PAIR] + q_bias).astype(BF16)
        k_ref[rows, :] = packed[:, PAIR : 2 * PAIR].astype(BF16)
        v_ref[rows, :] = (packed[:, 2 * PAIR :] + v_bias).astype(BF16)

    small_first = small_comes_first(place, segments_ref, other_segments_ref)
    big, small = windows(small_first)

    def image(window, queries, step, keys, merge):
        q_start, k_start, first, end = window
        lane_k = lanes(keys)
        bias = jnp.where(in_image(k_start, keys, first, end), 0.0, OFF)
        k_all = k_ref[pl.ds(k_start, keys), :].astype(F32)
        v_all = v_ref[pl.ds(k_start, keys), :].astype(F32)
        k_heads, v_heads = [], []
        for head in range(2):
            spare = 64 - 64 * head
            k_heads.append(
                jnp.where(own(lane_k, head), k_all, jnp.where(lane_k == spare, bias, 0.0)).astype(BF16)
            )
            v_heads.append(
                jnp.where(own(lane_k, head), v_all, jnp.where(lane_k == spare, 1.0, 0.0)).astype(BF16)
            )
        lane = lanes(step)
        for part in range(queries // step):
            start = pl.multiple_of(q_start + part * step, 16)
            here = pl.ds(start, step)
            q_part = q_ref[here, :].astype(F32) * 0.125
            outs, sums = [], []
            for head in range(2):
                spare = 64 - 64 * head
                q_head = jnp.where(
                    own(lane, head), q_part, jnp.where(lane == spare, 1.0, 0.0)
                ).astype(BF16)
                scores = lax.dot_general(q_head, k_heads[head], NT, preferred_element_type=F32)
                top = jnp.max(scores, axis=1, keepdims=True)
                weights = jnp.exp(scores - top).astype(BF16)
                out = jnp.dot(weights, v_heads[head], preferred_element_type=F32)
                total = out[:, spare : spare + 1]
                outs.append(out * (1.0 / total))
                sums.append(top + jnp.log(total))
            mixed = jnp.where(lane < 64, outs[0], outs[1])
            lse = jnp.where(lane < 64, sums[1], sums[0])
            if merge:
                rows = start + lax.broadcasted_iota(jnp.int32, (step, PAIR), 0)
                keep = (rows >= small[2]) & ((rows < 196) | (small_first == 0))
                mixed = jnp.where(keep, mixed_ref[here, :].astype(F32), mixed)
                lse = jnp.where(keep, lse_ref[here, :], lse)
            mixed_ref[here, :] = mixed.astype(BF16)
            lse_ref[here, :] = lse

    image(small, SMALL_Q, SMALL_Q, SMALL_K, False)
    image(big, BIG_Q, BIG_Q, BIG_K, True)

    @pl.when(pair == 2)
    def _():
        for copy in copies:
            copy.wait()


WHOLE = pl.BlockSpec(memory_space=pltpu.VMEM)
SCALARS = pl.BlockSpec(memory_space=pltpu.SMEM)
ANYWHERE = pl.BlockSpec(memory_space=pl.ANY)


def params(mib):
    return pltpu.CompilerParams(vmem_limit_bytes=mib * 2**20)


def cost(flops, traffic, transcendentals=0):
    return pl.CostEstimate(
        flops=int(flops), bytes_accessed=int(traffic), transcendentals=int(transcendentals)
    )


def far(array):
    return pltpu.with_memory_space_constraint(array, pltpu.HBM)


def block():
    return pl.BlockSpec((TOK, PAIR), lambda i, place: (0, i))


def whole(shape):
    return pl.BlockSpec(shape, lambda i, place: (0,) * len(shape))


def once(shape, index=lambda i, place: (0, 0)):
    return pl.BlockSpec(shape, index, pipeline_mode=pl.Buffered(1))


def attend(place, segments, tokens, gain, bias, w_qkv, q_bias, v_bias):
    def weight(kind):
        return pl.BlockSpec((WIDTH, PAIR), lambda i, place: (0, 6 * kind + 3 * place[0] + i))

    heads = pltpu.HBM((TOK, 3 * PAIR), BF16)
    return pl.pallas_call(
        attend_kernel,
        grid_spec=pltpu.PrefetchScalarGridSpec(
            num_scalar_prefetch=1,
            grid=(3,),
            in_specs=[SCALARS, SCALARS]
            + [once((REAL, WIDTH))] * 4
            + [WHOLE, WHOLE, weight(0), weight(1), weight(2), WHOLE, WHOLE],
            out_specs=[ANYWHERE, ANYWHERE, block(), block(), block(), block(), block()],
            scratch_shapes=[
                pltpu.VMEM((TOK, WIDTH), BF16),
                pltpu.VMEM((TOK, WIDTH), BF16),
                pltpu.VMEM((TOK, WIDTH), F32),
                pltpu.SemaphoreType.DMA((2,)),
            ],
        ),
        out_shape=[
            pltpu.HBM((TOK, WIDTH), BF16),
            pltpu.HBM((TOK, WIDTH), BF16),
            heads,
            heads,
            heads,
            heads,
            pltpu.HBM((TOK, 3 * PAIR), F32),
        ],
        compiler_params=params(36),
        cost_estimate=cost(8e9, 15e6, 4e6),
        name="attend",
    )(
        place,
        *segments,
        *tokens,
        gain,
        bias,
        far(w_qkv),
        far(w_qkv),
        far(w_qkv),
        q_bias,
        v_bias,
    )


def split(values):
    high = values.astype(BF16).astype(F32)
    return high, values - high


def attention_back(pair, small_first, q_ref, k_ref, v_ref, grad_ref, mixed_ref, lse_ref, out_ref, scores_ref):
    big, small = windows(small_first)
    pair_lanes = pl.ds(pl.multiple_of(pair * PAIR, PAIR), PAIR)

    def lanes_of(kind):
        return pl.ds(pl.multiple_of((3 * kind + pair) * PAIR, PAIR), PAIR)

    def image(window, keys, step, queries, add):
        k_start, q_start, first, end = window
        here = pl.ds(q_start, queries)
        lane = lanes(queries)
        bias = jnp.where(in_image(q_start, queries, first, end), 0.0, OFF)
        q_all = q_ref[here, :].astype(F32) * 0.125
        q_low = q_all.astype(BF16)
        grad_low = grad_ref[here, pair_lanes]
        grad_all = grad_low.astype(F32)
        products = grad_all * mixed_ref[here, pair_lanes].astype(F32)
        lse_high, lse_rest = split(lse_ref[here, :])
        lse_mid, lse_low = split(lse_rest)
        q_heads, grad_heads = [], []
        for head in range(2):
            spare = 64 - 64 * head
            mine = own(lane, head)
            q_head = jnp.where(mine, q_all, 0.0)
            for at, extra in enumerate((1.0, -lse_high, -lse_mid, -lse_low, bias)):
                q_head = jnp.where(lane == spare + at, extra, q_head)
            q_heads.append(q_head.astype(BF16))
            row_term = jnp.sum(jnp.where(mine, products, 0.0), axis=1, keepdims=True)
            term_high, term_low = split(row_term)
            grad_head = jnp.where(mine, grad_all, 0.0)
            grad_head = jnp.where(lane == spare + 1, -term_high, grad_head)
            grad_head = jnp.where(lane == spare + 2, -term_low, grad_head)
            grad_heads.append(grad_head.astype(BF16))
        lane = lanes(step)
        for part in range(keys // step):
            start = pl.multiple_of(k_start + part * step, 16)
            rows = pl.ds(start, step)
            k_part = k_ref[rows, :].astype(F32)
            v_part = v_ref[rows, :].astype(F32)
            key_bias = jnp.where(in_image(start, step, first, end), 0.0, OFF)
            keys_grad, values_grad = [], []
            for head in range(2):
                spare = 64 - 64 * head
                mine = own(lane, head)
                ones = (lane >= spare + 1) & (lane <= spare + 4)
                k_head = jnp.where(mine, k_part, jnp.where(ones, 1.0, 0.0))
                k_head = jnp.where(lane == spare, key_bias, k_head).astype(BF16)
                v_head = jnp.where(mine, v_part, jnp.where(ones, 1.0, 0.0)).astype(BF16)
                probs = jnp.exp(
                    lax.dot_general(k_head, q_heads[head], NT, preferred_element_type=F32)
                )
                change = lax.dot_general(v_head, grad_heads[head], NT, preferred_element_type=F32)
                grad_scores = (probs * change).astype(BF16)
                values_grad.append(
                    jnp.dot(probs.astype(BF16), grad_low, preferred_element_type=F32)
                )
                keys_grad.append(jnp.dot(grad_scores, q_low, preferred_element_type=F32))
                scores_ref[head, part * step : (part + 1) * step, :queries] = grad_scores
            key_out = jnp.where(lane < 64, keys_grad[0], keys_grad[1]).astype(BF16)
            value_out = jnp.where(lane < 64, values_grad[0], values_grad[1]).astype(BF16)
            if add:
                key_out = key_out + out_ref[rows, lanes_of(1)]
                value_out = value_out + out_ref[rows, lanes_of(2)]
            out_ref[rows, lanes_of(1)] = key_out
            out_ref[rows, lanes_of(2)] = value_out
        k_all = k_ref[pl.ds(k_start, keys), :]
        turned = [
            lax.dot_general(k_all, scores_ref[head, :keys, :queries], TN, preferred_element_type=F32)
            for head in range(2)
        ]
        row = lax.broadcasted_iota(jnp.int32, (PAIR, queries), 0)
        query_out = jnp.transpose(jnp.where(row < 64, turned[0], turned[1]) * 0.125).astype(BF16)
        if add:
            query_out = query_out + out_ref[here, lanes_of(0)]
        out_ref[here, lanes_of(0)] = query_out

    out_ref[pl.ds(small[0], SMALL_Q), lanes_of(1)] = jnp.zeros((SMALL_Q, PAIR), BF16)
    out_ref[pl.ds(small[0], SMALL_Q), lanes_of(2)] = jnp.zeros((SMALL_Q, PAIR), BF16)
    out_ref[pl.ds(small[1], SMALL_K), lanes_of(0)] = jnp.zeros((SMALL_K, PAIR), BF16)
    image(big, BIG_Q, BIG_STEP, BIG_K, False)
    image(small, SMALL_Q, SMALL_Q, SMALL_K, True)


FF_SHARE = 1536
SUB = 256
SHARE = 384
PEERS = 64
LATE = 3 * SHARE + 128
LATE_HALF = LATE // 2
CHIPS = ("x", "y", "zh", "zl")
ROWS = ("x", "y", "zh", "c")

def middle_kernel(
    place,
    mixed_ref,
    other_ref,
    x_ref,
    w_out_ref,
    out_bias_ref,
    gain_ref,
    bias_ref,
    own_ref,
    swapped_ref,
    host_ref,
    guest_ref,
    w_in_ref,
    in_bias_ref,
    w_back_ref,
    middle_hbm,
    grad_hbm,
    active_ref,
    grad_back_ref,
    grad_in_ref,
    sums_ref,
    back_ref,
    middle_ref,
    grad_ref,
    grad_hidden_ref,
    second_ref,
    turned_ref,
    rows_ref,
    left,
):
    core, step = place[0], pl.program_id(0)
    copies = [
        pltpu.make_async_copy(middle_ref, middle_hbm, left.at[0]),
        pltpu.make_async_copy(grad_ref, grad_hbm, left.at[1]),
    ]

    @pl.when(step == 0)
    def _():
        mine = w_out_ref[pl.ds(pl.multiple_of(core * SHARE, 128), SHARE), :]
        other = w_out_ref[pl.ds(pl.multiple_of((1 - core) * SHARE, 128), SHARE), :]
        assemble(place, own_ref, swapped_ref, host_ref, guest_ref, rows_ref)
        grad_ref[...] = rows_ref[...].astype(BF16)
        for begin, end in PARTS:
            rows = slice(begin, end)
            branch = jnp.dot(mixed_ref[rows, :], mine, preferred_element_type=F32)
            branch += jnp.dot(other_ref[rows, :], other, preferred_element_type=F32)
            middle = x_ref[rows, :].astype(F32) + branch + vector(out_bias_ref)
            middle_ref[rows, :] = middle
            second = norm_rows(middle)[0] * vector(gain_ref) + vector(bias_ref)
            second_ref[rows, :] = second.astype(BF16)
        for copy in copies:
            copy.start()
        turned_ref[...] = jnp.transpose(second_ref[...])

    for sub in range(2):
        columns = slice(SUB * sub, SUB * (sub + 1))
        column_sums = 0.0
        start = pl.multiple_of(core * FF_SHARE + step * 512 + SUB * sub, SUB)
        in_bias = vector(in_bias_ref, start, SUB)
        for part in range(2):
            rows = slice(part * HALF, (part + 1) * HALF)
            hidden = jnp.dot(second_ref[rows, :], w_in_ref[:, columns], preferred_element_type=F32)
            hidden += in_bias
            grad_active = lax.dot_general(
                grad_ref[rows, :], w_back_ref[columns, :], NT, preferred_element_type=F32
            )
            below = 0.5 + 0.5 * lax.erf(hidden * 0.7071067811865476)
            active_ref[rows, columns] = (hidden * below).astype(BF16)
            slope = below + hidden * jnp.exp(hidden * hidden * -0.5) * 0.3989422804014327
            grad_hidden = (grad_active * slope).astype(BF16)
            grad_hidden_ref[rows, columns] = grad_hidden
            column_sums += jnp.sum(grad_hidden.astype(F32), axis=0, keepdims=True)
        sums_ref[:, columns] = jnp.broadcast_to(column_sums, (8, SUB))
        total = jnp.dot(
            turned_ref[...], grad_hidden_ref[:, columns], preferred_element_type=F32
        ).astype(BF16)
        grad_in_ref[:, columns] = total
        total = lax.dot_general(
            active_ref[:, columns], grad_ref[...], TN, preferred_element_type=F32
        ).astype(BF16)
        grad_back_ref[columns, :] = total

    back = lax.dot_general(
        grad_hidden_ref[...], w_in_ref[...], NT, preferred_element_type=F32
    )

    @pl.when(step == 0)
    def _():
        rows_ref[...] = back

    @pl.when(step == 1)
    def _():
        rows_ref[...] += back

    @pl.when(step == 2)
    def _():
        back_ref[...] = (rows_ref[...] + back).astype(BF16)
        for copy in copies:
            copy.wait()


def middle_part(
    place, mixed, other, x, w_out, out_bias, gain, bias, grads, w_fc1, fc1_bias, w_fc2
):
    tokens, ff_columns = whole((TOK, WIDTH)), pl.BlockSpec((TOK, 512), lambda i, place: (0, i))
    return pl.pallas_call(
        middle_kernel,
        grid_spec=pltpu.PrefetchScalarGridSpec(
            num_scalar_prefetch=1,
            grid=(3,),
            in_specs=[once(a.shape) for a in (mixed, other, x, w_out)]
            + [WHOLE] * 3
            + [once(a.shape) for a in grads]
            + [
                pl.BlockSpec((WIDTH, 512), lambda i, place: (0, place[0] * 3 + i)),
                WHOLE,
                pl.BlockSpec((512, WIDTH), lambda i, place: (place[0] * 3 + i, 0)),
            ],
            out_specs=[
                ANYWHERE,
                ANYWHERE,
                ff_columns,
                pl.BlockSpec((512, WIDTH), lambda i, place: (i, 0)),
                pl.BlockSpec((WIDTH, 512), lambda i, place: (0, i)),
                pl.BlockSpec((8, 512), lambda i, place: (0, i)),
                tokens,
            ],
            scratch_shapes=[
                pltpu.VMEM((TOK, WIDTH), F32),
                pltpu.VMEM((TOK, WIDTH), BF16),
                pltpu.VMEM((TOK, 512), BF16),
                pltpu.VMEM((TOK, WIDTH), BF16),
                pltpu.VMEM((WIDTH, TOK), BF16),
                pltpu.VMEM((TOK, WIDTH), F32),
                pltpu.SemaphoreType.DMA((2,)),
            ],
        ),
        out_shape=[
            pltpu.HBM((TOK, WIDTH), F32),
            pltpu.HBM((TOK, WIDTH), BF16),
            pltpu.HBM((TOK, FF_SHARE), BF16),
            pltpu.HBM((FF_SHARE, WIDTH), BF16),
            pltpu.HBM((WIDTH, FF_SHARE), BF16),
            jax.ShapeDtypeStruct((8, FF_SHARE), F32),
            pltpu.HBM((TOK, WIDTH), BF16),
        ],
        compiler_params=params(44),
        cost_estimate=cost(10.5e9, 30e6, 3e6),
        name="middle_part",
    )(
        place,
        far(mixed),
        other,
        far(x),
        far(w_out),
        out_bias,
        gain,
        bias,
        *grads,
        far(w_fc1),
        fc1_bias,
        far(w_fc2),
    )


def halves(columns, first):
    def index(i, place):
        return (jnp.where(i == first, place[0], 1 - place[0]), 0)

    return pl.BlockSpec((HALF, columns), index)


def product_kernel(place, active_ref, w_back_ref, *refs):
    sent_ref, own_ref = refs[-2:]
    product = jnp.dot(active_ref[...], w_back_ref[...], preferred_element_type=F32)

    @pl.when(pl.program_id(0) == 0)
    def _():
        sent_ref[...] = product.astype(BF16)

    @pl.when(pl.program_id(0) == 1)
    def _():
        own_ref[...] = product


def mlp_product(place, active, w_fc2, after):
    return pl.pallas_call(
        product_kernel,
        grid_spec=pltpu.PrefetchScalarGridSpec(
            num_scalar_prefetch=1,
            grid=(2,),
            in_specs=[
                halves(FF_SHARE, 1),
                pl.BlockSpec((FF_SHARE, WIDTH), lambda i, place: (place[0], 0)),
            ]
            + [ANYWHERE] * len(after),
            out_specs=[whole((HALF, WIDTH)), whole((HALF, WIDTH))],
        ),
        out_shape=[pltpu.HBM((HALF, WIDTH), BF16), pltpu.HBM((HALF, WIDTH), F32)],
        compiler_params=params(24),
        cost_estimate=cost(1, 1),
        name="mlp_product",
    )(place, far(active), far(w_fc2), *after)


def attend_back_kernel(
    place,
    segments_ref,
    other_segments_ref,
    second_ref,
    other_ref,
    middle_ref,
    top_ref,
    mixed_ref,
    w_out_ref,
    gain_ref,
    in_sums_ref,
    x_hbm,
    first_hbm,
    w_hbm,
    q_ref,
    k_ref,
    v_ref,
    lse_ref,
    *refs,
):
    slots, (grad_middle_ref, own_ref, sent_ref), refs = refs[:8], refs[8:11], refs[11:]
    (
        late_ref,
        branch_ref,
        grad_mixed_ref,
        packed_ref,
        scores_ref,
        sums_ref,
        x_ref,
        first_ref,
        w_ref,
        arrived,
        left,
    ) = refs
    pair, core = pl.program_id(0), place[0]
    copies = [
        pltpu.make_async_copy(x_hbm, x_ref, arrived.at[0]),
        pltpu.make_async_copy(first_hbm, first_ref, arrived.at[1]),
    ]
    for kind in range(3):
        start = pl.multiple_of(kind * WIDTH + core * SHARE, 128)
        copies.append(
            pltpu.make_async_copy(
                w_hbm.at[:, pl.ds(start, SHARE)],
                w_ref.at[:, pl.ds(kind * SHARE, SHARE)],
                arrived.at[2 + kind],
            )
        )

    def half_rows(which, begin, end):
        return pl.ds(pl.multiple_of(which * HALF + begin, 16), end - begin)

    @pl.when(pair == 0)
    def _():
        for copy in copies:
            copy.start()
        sums = [0.0, 0.0, 0.0, 0.0]
        for which in (core, 1 - core):
            for begin, end in ((0, 256), (256, HALF)):
                rows = half_rows(which, begin, end)
                grad = second_ref[rows, :].astype(F32) + other_ref[rows, :].astype(F32)
                normed, inverse = norm_rows(middle_ref[rows, :])
                product = grad * normed
                scaled = grad * vector(gain_ref)
                top = top_ref[rows, :].astype(F32)
                grad_middle = top + inverse * (
                    scaled
                    - jnp.mean(scaled, axis=-1, keepdims=True)
                    - normed * jnp.mean(product * vector(gain_ref), axis=-1, keepdims=True)
                )
                if which is core:
                    grad_middle_ref[begin:end, :] = grad_middle
                branch = grad_middle.astype(BF16)
                branch_ref[rows, :] = branch
                grad_mixed_ref[rows, :] = lax.dot_general(
                    branch, w_out_ref[...], NT, preferred_element_type=F32
                ).astype(BF16)
                for i, values in enumerate((branch.astype(F32), product, grad, top)):
                    sums[i] += jnp.sum(values, axis=0, keepdims=True)
        for i in range(4):
            sums_ref[8 * i : 8 * i + 8, :] = jnp.broadcast_to(sums[i], (8, WIDTH))
        total = lax.dot_general(mixed_ref[...], branch_ref[...], TN, preferred_element_type=F32)
        total = total.astype(BF16)
        for a in range(8):
            for b in range(2):
                for s in range(3):
                    row = WIDTH + 16 * (2 * a + b)
                    late_ref[row : row + 16, SHARE * s : SHARE * (s + 1)] = total[
                        48 * a + 16 * s : 48 * a + 16 * s + 16, SHARE * b : SHARE * (b + 1)
                    ]

    attention_back(
        pair,
        small_comes_first(place, segments_ref, other_segments_ref),
        q_ref,
        k_ref,
        v_ref,
        grad_mixed_ref,
        mixed_ref,
        lse_ref,
        packed_ref,
        scores_ref,
    )

    @pl.when(pair == 2)
    def _():
        for copy in copies:
            copy.wait()
        late_ref[:WIDTH, : 3 * SHARE] = lax.dot_general(
            first_ref[...], packed_ref[...], TN, preferred_element_type=F32
        ).astype(BF16)
        gain, bias, packed = 0.0, 0.0, 0.0
        for which in (core, 1 - core):
            for begin, end in ((0, 256), (256, HALF)):
                rows = half_rows(which, begin, end)
                grad = packed_ref[rows, :]
                part = lax.dot_general(grad, w_ref[...], NT, preferred_element_type=F32)
                if which is core:
                    own_ref[begin:end, :] = part
                else:
                    sent_ref[begin:end, :] = part.astype(BF16)
                gain += jnp.sum(
                    part * norm_rows(x_ref[rows, :].astype(F32))[0], axis=0, keepdims=True
                )
                bias += jnp.sum(part, axis=0, keepdims=True)
                packed += jnp.sum(grad.astype(F32), axis=0, keepdims=True)
        pieces = [sums_ref[8 * i : 8 * i + 1, :] for i in range(3)]
        pieces += [gain, bias, sums_ref[24:25, :]]
        pieces += [packed[:, :SHARE], packed[:, 2 * SHARE :], in_sums_ref[:1, :]]
        late_ref[:, 3 * SHARE :] = jnp.zeros((16 * PEERS, 128), BF16)
        at = 0
        for piece in pieces:
            for tile in range(piece.shape[1] // 128):
                late_ref[16 * at : 16 * at + 16, 3 * SHARE :] = jnp.broadcast_to(
                    piece[:, 128 * tile : 128 * (tile + 1)], (16, 128)
                ).astype(BF16)
                at += 1
        parts = []
        for side in range(2):
            for hop in range(4):
                start = pl.multiple_of(256 * lax.rem(place[2 + side] + hop, 4), 256)
                parts.append(
                    pltpu.make_async_copy(
                        late_ref.at[pl.ds(start, 256), pl.ds(LATE_HALF * side, LATE_HALF)],
                        slots[4 * side + hop],
                        left.at[4 * side + hop],
                    )
                )
        for copy in parts:
            copy.start()
        for copy in parts:
            copy.wait()


def attend_back(
    place, segments, second, other, middle, top, mixed, w_out, gain, in_sums, x, first, w_qkv, heads
):
    tokens, half = once((TOK, WIDTH)), whole((HALF, WIDTH))
    return pl.pallas_call(
        attend_back_kernel,
        grid_spec=pltpu.PrefetchScalarGridSpec(
            num_scalar_prefetch=1,
            grid=(3,),
            in_specs=[
                SCALARS,
                SCALARS,
                tokens,
                tokens,
                tokens,
                tokens,
                once((TOK, SHARE)),
                once((SHARE, WIDTH), lambda i, place: (place[0], 0)),
                WHOLE,
                WHOLE,
                ANYWHERE,
                ANYWHERE,
                ANYWHERE,
            ]
            + [block()] * 4,
            out_specs=[ANYWHERE] * 8 + [half, half, half],
            scratch_shapes=[
                pltpu.VMEM((16 * PEERS, LATE), BF16),
                pltpu.VMEM((TOK, WIDTH), BF16),
                pltpu.VMEM((TOK, SHARE), BF16),
                pltpu.VMEM((TOK, 3 * SHARE), BF16),
                pltpu.VMEM((2, BIG_Q, BIG_K), BF16),
                pltpu.VMEM((32, WIDTH), F32),
                pltpu.VMEM((TOK, WIDTH), BF16),
                pltpu.VMEM((TOK, WIDTH), BF16),
                pltpu.VMEM((WIDTH, 3 * SHARE), BF16),
                pltpu.SemaphoreType.DMA((5,)),
                pltpu.SemaphoreType.DMA((8,)),
            ],
        ),
        out_shape=[pltpu.HBM((256, LATE_HALF), BF16)] * 8
        + [
            pltpu.HBM((HALF, WIDTH), F32),
            pltpu.HBM((HALF, WIDTH), F32),
            pltpu.HBM((HALF, WIDTH), BF16),
        ],
        compiler_params=params(46),
        cost_estimate=cost(1, 1),
        name="attend_back",
    )(
        place,
        *segments,
        far(second),
        other,
        far(middle),
        far(top),
        far(mixed),
        far(w_out),
        gain,
        in_sums,
        far(x),
        far(first),
        far(w_qkv),
        *(far(a) for a in heads),
    )


def small_call(kernel, name, arrays, shapes, place, scratch=(), after=()):
    count = 1 + len(arrays)

    def body(*refs):
        kernel(*refs[:count], *refs[count + len(after) :])

    return pl.pallas_call(
        body,
        in_specs=[SCALARS] + [WHOLE] * len(arrays) + [ANYWHERE] * len(after),
        out_specs=[WHOLE] * len(shapes),
        out_shape=[jax.ShapeDtypeStruct(shape, BF16) for shape in shapes],
        scratch_shapes=list(scratch),
        compiler_params=params(16),
        cost_estimate=cost(1, 1),
        name=name,
    )(place, *arrays, *after)


def total_of(refs):
    total = refs[0][...].astype(F32)
    for ref in refs[1:]:
        total += ref[...].astype(F32)
    return total.astype(BF16)


def turn(place, axis, hop, size):
    return pl.ds(pl.multiple_of(size * lax.rem(place[axis] + hop, 4), size), size)


def sum_first_kernel(place, *refs):
    scratch = refs[-1]
    for side in range(2):
        scratch[...] = total_of(refs[4 * side : 4 * side + 4])
        for hop in range(4):
            refs[8 + 4 * side + hop][...] = scratch[turn(place, 3 - side, hop, 64), :]


def sum_second_kernel(place, *refs):
    scratch = refs[-1]
    for side in range(2):
        columns = slice(LATE_HALF * side, LATE_HALF * (side + 1))
        scratch[:, columns] = total_of(refs[4 * side : 4 * side + 4])
    for hop in range(4):
        refs[8 + hop][...] = scratch[turn(place, 4, hop, 16), :]


def sum_third_kernel(place, *refs):
    refs[-1][...] = total_of(refs[:4])


def join_third_kernel(place, *refs):
    for hop in range(4):
        rows = turn(place, 4, 4 - hop, 16)
        for side in range(2):
            columns = slice(LATE_HALF * side, LATE_HALF * (side + 1))
            refs[4 + side][rows, :] = refs[hop][:, columns]


def join_second_kernel(place, *refs):
    for side in range(2):
        for hop in range(4):
            refs[8 + side][turn(place, 3 - side, 4 - hop, 64), :] = refs[4 * side + hop][...]


def join_first_kernel(place, *refs):
    for side in range(2):
        columns = slice(LATE_HALF * side, LATE_HALF * (side + 1))
        for hop in range(4):
            refs[8][turn(place, 2 + side, 4 - hop, 256), columns] = refs[4 * side + hop][...]


def around(parts, axis):
    return [parts[0]] + [
        lax.ppermute(parts[hop], axis, [(i, (i + hop) % 4) for i in range(4)]) for hop in (1, 2, 3)
    ]


def sum_late(parts, place, first, second):
    depth = ("zh", "zl")
    parts = small_call(
        sum_first_kernel,
        "sum_first",
        parts,
        [(64, LATE_HALF)] * 8,
        place,
        [pltpu.VMEM((256, LATE_HALF), BF16)],
    )
    parts = around(parts[:4], "y") + around(parts[4:], "x")
    parts = small_call(
        sum_second_kernel,
        "sum_second",
        parts,
        [(16, LATE)] * 4,
        place,
        [pltpu.VMEM((64, LATE), BF16)],
        first,
    )
    (share,) = small_call(
        sum_third_kernel, "sum_third", around(parts, depth), [(16, LATE)], place
    )
    one, two = small_call(
        join_third_kernel, "join_third", around([share] * 4, depth), [(64, LATE_HALF)] * 2, place
    )
    parts = around([one] * 4, "y") + around([two] * 4, "x")
    one, two = small_call(
        join_second_kernel, "join_second", parts, [(256, LATE_HALF)] * 2, place, after=second
    )
    return around([one] * 4, "x") + around([two] * 4, "y")


def join_late(parts, place):
    return small_call(join_first_kernel, "join_first", parts, [(16 * PEERS, LATE)], place)[0]


def widen_mine_kernel(place, back_ref, in_ref, *refs):
    total_back_ref, total_in_ref = refs[-2:]
    total_back_ref[...] = back_ref[...].astype(F32)
    total_in_ref[...] = in_ref[...].astype(F32)


def widen_mine(place, early, after):
    return pl.pallas_call(
        widen_mine_kernel,
        grid_spec=pltpu.PrefetchScalarGridSpec(
            num_scalar_prefetch=1,
            grid=(3,),
            in_specs=[
                pl.BlockSpec((512, WIDTH), lambda i, place: (i, 0)),
                pl.BlockSpec((WIDTH, 512), lambda i, place: (0, i)),
            ]
            + [ANYWHERE] * len(after),
            out_specs=[
                pl.BlockSpec((512, WIDTH), lambda i, place: (3 * place[0] + i, 0)),
                pl.BlockSpec((WIDTH, 512), lambda i, place: (0, 3 * place[0] + i)),
            ],
        ),
        out_shape=[
            pltpu.HBM((2 * FF_SHARE, WIDTH), F32),
            pltpu.HBM((WIDTH, 2 * FF_SHARE), F32),
        ],
        compiler_params=params(24),
        cost_estimate=cost(0, 100e6),
        name="widen_mine",
    )(place, *(far(a) for a in early), *after)


def widen_kernel(
    place,
    back_ref,
    in_ref,
    same_back_ref,
    same_in_ref,
    mine_ref,
    other_ref,
    mine_small_ref,
    other_small_ref,
    total_back_ref,
    total_in_ref,
    packed_ref,
    out_ref,
    in_bias_ref,
    q_bias_ref,
    v_bias_ref,
    *vector_refs,
):
    step, first = pl.program_id(0), place[0] == 0
    total_back_ref[...] = back_ref[...].astype(F32)
    total_in_ref[...] = in_ref[...].astype(F32)

    def pick(side, mine_ref, other_ref, rows, columns):
        mine, other = mine_ref[rows, columns].astype(F32), other_ref[rows, columns].astype(F32)
        return jnp.where(first if side == 0 else jnp.logical_not(first), mine, other)

    @pl.when(step < 3)
    def _():
        for side in range(2):
            for kind in range(3):
                at = SHARE * (2 * kind + side)
                packed_ref[:, at : at + SHARE] = pick(
                    side, mine_ref, other_ref, slice(0, 256), slice(SHARE * kind, SHARE * (kind + 1))
                )

    @pl.when(step == 3)
    def _():
        for side in range(2):
            for a in range(8):
                for b in range(2):
                    row = 16 * (2 * a + b)
                    for s in range(3):
                        at = SHARE * side + 48 * a + 16 * s
                        out_ref[at : at + 16, SHARE * b : SHARE * (b + 1)] = pick(
                            side,
                            mine_ref,
                            other_ref,
                            slice(row, row + 16),
                            slice(SHARE * s, SHARE * (s + 1)),
                        )

    @pl.when(step == 0)
    def _():
        def piece(side, at):
            rows = slice(16 * at, 16 * at + 16)
            return pick(side, mine_small_ref, other_small_ref, rows, slice(0, 128))[:1]

        def put(ref, tile, value):
            ref[128 * tile : 128 * (tile + 1)] = value.reshape(128)

        for tile in range(6):
            for at in range(6):
                value = piece(0, 6 * at + tile)
                if at in (3, 4):
                    value += piece(1, 6 * at + tile)
                put(vector_refs[at], tile, value)
        for side in range(2):
            for tile in range(3):
                put(q_bias_ref, 3 * side + tile, piece(side, 36 + tile))
                put(v_bias_ref, 3 * side + tile, piece(side, 39 + tile))
            for tile in range(12):
                put(in_bias_ref, 12 * side + tile, piece(side, 42 + tile))


def widen(place, early, totals, late, late_other):
    rows = pl.BlockSpec((256, LATE), lambda i, place: (i, 0))
    small = pl.BlockSpec((16 * PEERS, 128), lambda i, place: (0, 9))
    vectors = [jax.ShapeDtypeStruct((2 * FF_SHARE,), F32)] + [jax.ShapeDtypeStruct((WIDTH,), F32)] * 8
    return pl.pallas_call(
        widen_kernel,
        grid_spec=pltpu.PrefetchScalarGridSpec(
            num_scalar_prefetch=1,
            grid=(4,),
            in_specs=[
                pl.BlockSpec((512, WIDTH), lambda i, place: (jnp.minimum(i, 2), 0)),
                pl.BlockSpec((WIDTH, 512), lambda i, place: (0, jnp.minimum(i, 2))),
                ANYWHERE,
                ANYWHERE,
                rows,
                rows,
                small,
                small,
            ],
            out_specs=[
                pl.BlockSpec((512, WIDTH), lambda i, place: (3 - 3 * place[0] + jnp.minimum(i, 2), 0)),
                pl.BlockSpec((WIDTH, 512), lambda i, place: (0, 3 - 3 * place[0] + jnp.minimum(i, 2))),
                pl.BlockSpec((256, 3 * WIDTH), lambda i, place: (jnp.minimum(i, 2), 0)),
                whole((WIDTH, WIDTH)),
            ]
            + [WHOLE] * 9,
        ),
        out_shape=[
            pltpu.HBM((2 * FF_SHARE, WIDTH), F32),
            pltpu.HBM((WIDTH, 2 * FF_SHARE), F32),
            pltpu.HBM((WIDTH, 3 * WIDTH), F32),
            pltpu.HBM((WIDTH, WIDTH), F32),
        ]
        + vectors,
        input_output_aliases={3: 0, 4: 1},
        compiler_params=params(32),
        cost_estimate=cost(0, 29e6),
        name="widen",
    )(place, *early, *(far(a) for a in (*totals, late, late_other, late, late_other)))


def norm_back(grad_normed, normed, inverse):
    return inverse * (
        grad_normed
        - jnp.mean(grad_normed, axis=-1, keepdims=True)
        - normed * jnp.mean(grad_normed * normed, axis=-1, keepdims=True)
    )


def other_core(values):
    return lax.ppermute(values, "c", [(0, 1), (1, 0)])


def swap_home(values):
    return lax.ppermute(values, ("c", "zl"), [(1, 2), (2, 1)])


def from_host(values):
    return lax.ppermute(values, ("c", "zl"), [(0, 2), (3, 1)])


def from_guest(values):
    return lax.ppermute(values, ("c", "zl"), [(2, 0), (1, 3)])


def from_next(values):
    return lax.ppermute(values, ("c", "zl"), [(1, 0), (2, 3)])


def body(
    inputs,
    segments,
    cotangent,
    ln1_gain,
    ln1_bias,
    w_qkv,
    q_bias,
    v_bias,
    w_out,
    out_bias,
    ln2_gain,
    ln2_bias,
    w_fc1,
    fc1_bias,
    w_fc2,
    fc2_bias,
):
    core = lax.axis_index("c")
    home = core == lax.axis_index("zl")

    def half(array, which):
        return lax.dynamic_slice_in_dim(array, which * HALF, HALF, 0)

    tokens, top = inputs[0], cotangent[0]
    swapped = swap_home(tokens)
    rows = (tokens, swapped, from_host(tokens), from_guest(swapped))
    images = (segments, other_core(segments))
    depth = 2 * lax.axis_index("zh") + lax.axis_index("zl")
    place = [core, home, lax.axis_index("x"), lax.axis_index("y"), depth]
    place = jnp.stack([index.astype(jnp.int32) for index in place])

    sent = jnp.concatenate([top, swapped[: HALF - REAL]], axis=0)
    tops = (top, swap_home(sent), from_host(top), from_next(sent))

    x_all, first_in, query, key, value, mixed, lse = attend(
        place, images, rows, ln1_gain, ln1_bias, w_qkv, q_bias, v_bias
    )
    middle, grad_top, active, grad_back, grad_in, in_sums, second = middle_part(
        place,
        mixed,
        other_core(mixed),
        x_all,
        w_out,
        out_bias,
        ln2_gain,
        ln2_bias,
        tops,
        w_fc1,
        fc1_bias,
        w_fc2,
    )
    early = lax.psum((grad_back, grad_in), CHIPS)
    *late, grad_middle, first_part, first_sent = attend_back(
        place,
        images,
        second,
        other_core(second),
        middle,
        grad_top,
        mixed,
        w_out,
        ln2_gain,
        in_sums,
        x_all,
        first_in,
        w_qkv,
        (query, key, value, lse),
    )
    late = around(late[:4], "x") + around(late[4:], "y")
    product_sent, product = mlp_product(place, active, w_fc2, (late[5],))
    result = half(middle, core) + product + other_core(product_sent).astype(F32) + fc2_bias
    result = result.astype(BF16)
    output = jnp.where(home, result, swap_home(result))[None, :REAL]

    grad_first_in = first_part + other_core(first_sent).astype(F32)
    normed_one, inverse_one = norm_rows(half(x_all, core).astype(F32))
    grad_input = grad_middle + norm_back(grad_first_in * ln1_gain, normed_one, inverse_one)
    grad_input = grad_input.astype(BF16)
    input_grad = jnp.where(home, grad_input, swap_home(grad_input))[None, :REAL]

    late = sum_late(late, place, (result, grad_input), (output, input_grad))
    totals = widen_mine(place, early, (late[1],))
    early_other = [other_core(a) for a in early]
    late = join_late(late, place)
    total_back, total_in, total_packed, total_out, in_bias, total_q_bias, total_v_bias, *vectors = widen(
        place, early_other, totals, late, other_core(late)
    )
    return (
        output,
        input_grad,
        vectors[3],
        vectors[4],
        total_packed,
        total_q_bias,
        total_v_bias,
        total_out,
        vectors[0],
        vectors[1],
        vectors[2],
        total_in,
        in_bias,
        total_back,
        vectors[5],
    )


def solution(mesh):
    fine = Mesh(mesh.devices.reshape(4, 4, 2, 2, 2), ("x", "y", "zh", "c", "zl"))
    tokens = P(ROWS, "zl", None)
    return jax.shard_map(
        body,
        mesh=fine,
        in_specs=(tokens, P(ROWS, None), tokens) + (P(),) * 13,
        out_specs=(tokens, tokens) + (P(),) * 13,
        check_vma=False,
    )
```

```python
import jax
import jax.numpy as jnp
from jax import lax
from jax.experimental import pallas as pl
from jax.experimental.pallas import tpu as pltpu
from jax.sharding import Mesh
from jax.sharding import PartitionSpec as P


HALF = 496
TOK = 2 * HALF
REAL = 490
PAIR = 128
BIG_Q, BIG_K, BIG_STEP = 800, 896, 160
WIDTH = 768
SMALL_Q, SMALL_K = 208, 256
OFF = -1e30
F32, BF16 = jnp.float32, jnp.bfloat16
PARTS = ((0, 256), (256, 512), (512, 768), (768, TOK))
NT = (((1,), (1,)), ((), ()))
TN = (((0,), (0,)), ((), ()))


def windows(small_first):
    big = (
        pl.multiple_of(small_first * 192, 32),
        pl.multiple_of(small_first * 96, 32),
        small_first * 196,
        790 + small_first * 196,
    )
    small = (
        pl.multiple_of((1 - small_first) * 784, 16),
        pl.multiple_of((1 - small_first) * 736, 32),
        (1 - small_first) * 790,
        196 + (1 - small_first) * 790,
    )
    return big, small


def in_image(start, count, first, end):
    rows = start + lax.broadcasted_iota(jnp.int32, (count, PAIR), 0)
    return (rows >= first) & (rows < end) & ((rows < REAL) | (rows >= HALF))


def lanes(count):
    return lax.broadcasted_iota(jnp.int32, (count, PAIR), 1)


def own(lane, head):
    return lane < 64 if head == 0 else lane >= 64


def norm_rows(values):
    center = values - jnp.mean(values, axis=-1, keepdims=True)
    inverse = lax.rsqrt(jnp.mean(center * center, axis=-1, keepdims=True) + 1e-06)
    return center * inverse, inverse


def assemble(place, own_ref, swapped_ref, host_ref, guest_ref, rows_ref):
    core, home = place[0], place[1] == 1
    for half, at_home, away in ((core, own_ref, swapped_ref), (1 - core, guest_ref, host_ref)):
        start = pl.multiple_of(half * HALF, 16)
        rows_ref[pl.ds(pl.multiple_of(start + 488, 8), 8), :] = jnp.zeros((8, WIDTH), F32)

        @pl.when(home)
        def _():
            rows_ref[pl.ds(start, REAL), :] = at_home[...][:REAL].astype(F32)

        @pl.when(jnp.logical_not(home))
        def _():
            rows_ref[pl.ds(start, REAL), :] = away[...][:REAL].astype(F32)


def small_comes_first(place, segments_ref, other_ref):
    mine = segments_ref[0, 196] != segments_ref[0, 0]
    other = other_ref[0, 196] != other_ref[0, 0]
    return jnp.where(place[1] == 1, mine.astype(jnp.int32), other.astype(jnp.int32))


def vector(ref, start=0, size=WIDTH):
    return ref[pl.ds(start, size)].reshape(1, size)


def attend_kernel(
    place,
    segments_ref,
    other_segments_ref,
    own_ref,
    swapped_ref,
    host_ref,
    guest_ref,
    gain_ref,
    bias_ref,
    wq_ref,
    wk_ref,
    wv_ref,
    q_bias_ref,
    v_bias_ref,
    x_hbm,
    first_hbm,
    q_ref,
    k_ref,
    v_ref,
    mixed_ref,
    lse_ref,
    x_ref,
    first_ref,
    rows_ref,
    left,
):
    pair = pl.program_id(0)
    copies = [
        pltpu.make_async_copy(x_ref, x_hbm, left.at[0]),
        pltpu.make_async_copy(first_ref, first_hbm, left.at[1]),
    ]

    @pl.when(pair == 0)
    def _():
        assemble(place, own_ref, swapped_ref, host_ref, guest_ref, rows_ref)
        for begin, end in PARTS:
            rows = slice(begin, end)
            values = rows_ref[rows, :]
            x_ref[rows, :] = values.astype(BF16)
            first = norm_rows(values)[0] * vector(gain_ref) + vector(bias_ref)
            first_ref[rows, :] = first.astype(BF16)
        for copy in copies:
            copy.start()

    weights = jnp.concatenate([wq_ref[...], wk_ref[...], wv_ref[...]], axis=1)
    start = pl.multiple_of((3 * place[0] + pair) * PAIR, PAIR)
    q_bias, v_bias = vector(q_bias_ref, start, PAIR), vector(v_bias_ref, start, PAIR)
    for begin, end in PARTS:
        rows = slice(begin, end)
        packed = jnp.dot(first_ref[rows, :], weights, preferred_element_type=F32)
        q_ref[rows, :] = (packed[:, :PAIR] + q_bias).astype(BF16)
        k_ref[rows, :] = packed[:, PAIR : 2 * PAIR].astype(BF16)
        v_ref[rows, :] = (packed[:, 2 * PAIR :] + v_bias).astype(BF16)

    small_first = small_comes_first(place, segments_ref, other_segments_ref)
    big, small = windows(small_first)

    def image(window, queries, step, keys, merge):
        q_start, k_start, first, end = window
        lane_k = lanes(keys)
        bias = jnp.where(in_image(k_start, keys, first, end), 0.0, OFF)
        k_all = k_ref[pl.ds(k_start, keys), :].astype(F32)
        v_all = v_ref[pl.ds(k_start, keys), :].astype(F32)
        k_heads, v_heads = [], []
        for head in range(2):
            spare = 64 - 64 * head
            k_heads.append(
                jnp.where(own(lane_k, head), k_all, jnp.where(lane_k == spare, bias, 0.0)).astype(BF16)
            )
            v_heads.append(
                jnp.where(own(lane_k, head), v_all, jnp.where(lane_k == spare, 1.0, 0.0)).astype(BF16)
            )
        lane = lanes(step)
        for part in range(queries // step):
            start = pl.multiple_of(q_start + part * step, 16)
            here = pl.ds(start, step)
            q_part = q_ref[here, :].astype(F32) * 0.125
            outs, sums = [], []
            for head in range(2):
                spare = 64 - 64 * head
                q_head = jnp.where(
                    own(lane, head), q_part, jnp.where(lane == spare, 1.0, 0.0)
                ).astype(BF16)
                scores = lax.dot_general(q_head, k_heads[head], NT, preferred_element_type=F32)
                top = jnp.max(scores, axis=1, keepdims=True)
                weights = jnp.exp(scores - top).astype(BF16)
                out = jnp.dot(weights, v_heads[head], preferred_element_type=F32)
                total = out[:, spare : spare + 1]
                outs.append(out * (1.0 / total))
                sums.append(top + jnp.log(total))
            mixed = jnp.where(lane < 64, outs[0], outs[1])
            lse = jnp.where(lane < 64, sums[1], sums[0])
            if merge:
                rows = start + lax.broadcasted_iota(jnp.int32, (step, PAIR), 0)
                keep = (rows >= small[2]) & ((rows < 196) | (small_first == 0))
                mixed = jnp.where(keep, mixed_ref[here, :].astype(F32), mixed)
                lse = jnp.where(keep, lse_ref[here, :], lse)
            mixed_ref[here, :] = mixed.astype(BF16)
            lse_ref[here, :] = lse

    image(small, SMALL_Q, SMALL_Q, SMALL_K, False)
    image(big, BIG_Q, BIG_Q, BIG_K, True)

    @pl.when(pair == 2)
    def _():
        for copy in copies:
            copy.wait()


WHOLE = pl.BlockSpec(memory_space=pltpu.VMEM)
SCALARS = pl.BlockSpec(memory_space=pltpu.SMEM)
ANYWHERE = pl.BlockSpec(memory_space=pl.ANY)


def params(mib):
    return pltpu.CompilerParams(vmem_limit_bytes=mib * 2**20)


def cost(flops, traffic, transcendentals=0):
    return pl.CostEstimate(
        flops=int(flops), bytes_accessed=int(traffic), transcendentals=int(transcendentals)
    )


def far(array):
    return pltpu.with_memory_space_constraint(array, pltpu.HBM)


def block():
    return pl.BlockSpec((TOK, PAIR), lambda i, place: (0, i))


def whole(shape):
    return pl.BlockSpec(shape, lambda i, place: (0,) * len(shape))


def once(shape, index=lambda i, place: (0, 0)):
    return pl.BlockSpec(shape, index, pipeline_mode=pl.Buffered(1))


def attend(place, segments, tokens, gain, bias, w_qkv, q_bias, v_bias):
    def weight(kind):
        return pl.BlockSpec((WIDTH, PAIR), lambda i, place: (0, 6 * kind + 3 * place[0] + i))

    heads = pltpu.HBM((TOK, 3 * PAIR), BF16)
    return pl.pallas_call(
        attend_kernel,
        grid_spec=pltpu.PrefetchScalarGridSpec(
            num_scalar_prefetch=1,
            grid=(3,),
            in_specs=[SCALARS, SCALARS]
            + [once((REAL, WIDTH))] * 4
            + [WHOLE, WHOLE, weight(0), weight(1), weight(2), WHOLE, WHOLE],
            out_specs=[ANYWHERE, ANYWHERE, block(), block(), block(), block(), block()],
            scratch_shapes=[
                pltpu.VMEM((TOK, WIDTH), BF16),
                pltpu.VMEM((TOK, WIDTH), BF16),
                pltpu.VMEM((TOK, WIDTH), F32),
                pltpu.SemaphoreType.DMA((2,)),
            ],
        ),
        out_shape=[
            pltpu.HBM((TOK, WIDTH), BF16),
            pltpu.HBM((TOK, WIDTH), BF16),
            heads,
            heads,
            heads,
            heads,
            pltpu.HBM((TOK, 3 * PAIR), F32),
        ],
        compiler_params=params(36),
        cost_estimate=cost(8e9, 15e6, 4e6),
        name="attend",
    )(
        place,
        *segments,
        *tokens,
        gain,
        bias,
        far(w_qkv),
        far(w_qkv),
        far(w_qkv),
        q_bias,
        v_bias,
    )


def split(values):
    high = values.astype(BF16).astype(F32)
    return high, values - high


def attention_back(pair, small_first, q_ref, k_ref, v_ref, grad_ref, mixed_ref, lse_ref, out_ref, scores_ref):
    big, small = windows(small_first)
    pair_lanes = pl.ds(pl.multiple_of(pair * PAIR, PAIR), PAIR)

    def lanes_of(kind):
        return pl.ds(pl.multiple_of((3 * kind + pair) * PAIR, PAIR), PAIR)

    def image(window, keys, step, queries, add):
        k_start, q_start, first, end = window
        here = pl.ds(q_start, queries)
        lane = lanes(queries)
        bias = jnp.where(in_image(q_start, queries, first, end), 0.0, OFF)
        q_all = q_ref[here, :].astype(F32) * 0.125
        q_low = q_all.astype(BF16)
        grad_low = grad_ref[here, pair_lanes]
        grad_all = grad_low.astype(F32)
        products = grad_all * mixed_ref[here, pair_lanes].astype(F32)
        lse_high, lse_rest = split(lse_ref[here, :])
        lse_mid, lse_low = split(lse_rest)
        q_heads, grad_heads = [], []
        for head in range(2):
            spare = 64 - 64 * head
            mine = own(lane, head)
            q_head = jnp.where(mine, q_all, 0.0)
            for at, extra in enumerate((1.0, -lse_high, -lse_mid, -lse_low, bias)):
                q_head = jnp.where(lane == spare + at, extra, q_head)
            q_heads.append(q_head.astype(BF16))
            row_term = jnp.sum(jnp.where(mine, products, 0.0), axis=1, keepdims=True)
            term_high, term_low = split(row_term)
            grad_head = jnp.where(mine, grad_all, 0.0)
            grad_head = jnp.where(lane == spare + 1, -term_high, grad_head)
            grad_head = jnp.where(lane == spare + 2, -term_low, grad_head)
            grad_heads.append(grad_head.astype(BF16))
        lane = lanes(step)
        for part in range(keys // step):
            start = pl.multiple_of(k_start + part * step, 16)
            rows = pl.ds(start, step)
            k_part = k_ref[rows, :].astype(F32)
            v_part = v_ref[rows, :].astype(F32)
            key_bias = jnp.where(in_image(start, step, first, end), 0.0, OFF)
            keys_grad, values_grad = [], []
            for head in range(2):
                spare = 64 - 64 * head
                mine = own(lane, head)
                ones = (lane >= spare + 1) & (lane <= spare + 4)
                k_head = jnp.where(mine, k_part, jnp.where(ones, 1.0, 0.0))
                k_head = jnp.where(lane == spare, key_bias, k_head).astype(BF16)
                v_head = jnp.where(mine, v_part, jnp.where(ones, 1.0, 0.0)).astype(BF16)
                probs = jnp.exp(
                    lax.dot_general(k_head, q_heads[head], NT, preferred_element_type=F32)
                )
                change = lax.dot_general(v_head, grad_heads[head], NT, preferred_element_type=F32)
                grad_scores = (probs * change).astype(BF16)
                values_grad.append(
                    jnp.dot(probs.astype(BF16), grad_low, preferred_element_type=F32)
                )
                keys_grad.append(jnp.dot(grad_scores, q_low, preferred_element_type=F32))
                scores_ref[head, part * step : (part + 1) * step, :queries] = grad_scores
            key_out = jnp.where(lane < 64, keys_grad[0], keys_grad[1]).astype(BF16)
            value_out = jnp.where(lane < 64, values_grad[0], values_grad[1]).astype(BF16)
            if add:
                key_out = key_out + out_ref[rows, lanes_of(1)]
                value_out = value_out + out_ref[rows, lanes_of(2)]
            out_ref[rows, lanes_of(1)] = key_out
            out_ref[rows, lanes_of(2)] = value_out
        k_all = k_ref[pl.ds(k_start, keys), :]
        turned = [
            lax.dot_general(k_all, scores_ref[head, :keys, :queries], TN, preferred_element_type=F32)
            for head in range(2)
        ]
        row = lax.broadcasted_iota(jnp.int32, (PAIR, queries), 0)
        query_out = jnp.transpose(jnp.where(row < 64, turned[0], turned[1]) * 0.125).astype(BF16)
        if add:
            query_out = query_out + out_ref[here, lanes_of(0)]
        out_ref[here, lanes_of(0)] = query_out

    out_ref[pl.ds(small[0], SMALL_Q), lanes_of(1)] = jnp.zeros((SMALL_Q, PAIR), BF16)
    out_ref[pl.ds(small[0], SMALL_Q), lanes_of(2)] = jnp.zeros((SMALL_Q, PAIR), BF16)
    out_ref[pl.ds(small[1], SMALL_K), lanes_of(0)] = jnp.zeros((SMALL_K, PAIR), BF16)
    image(big, BIG_Q, BIG_STEP, BIG_K, False)
    image(small, SMALL_Q, SMALL_Q, SMALL_K, True)


FF_SHARE = 1536
SUB = 256
SHARE = 384
PEERS = 64
LATE = 3 * SHARE + 128
LATE_HALF = LATE // 2
CHIPS = ("x", "y", "zh", "zl")
ROWS = ("x", "y", "zh", "c")

def middle_kernel(
    place,
    mixed_ref,
    other_ref,
    x_ref,
    w_out_ref,
    out_bias_ref,
    gain_ref,
    bias_ref,
    own_ref,
    swapped_ref,
    host_ref,
    guest_ref,
    w_in_ref,
    in_bias_ref,
    w_back_ref,
    middle_hbm,
    grad_hbm,
    active_ref,
    grad_back_ref,
    grad_in_ref,
    sums_ref,
    back_ref,
    middle_ref,
    grad_ref,
    grad_hidden_ref,
    second_ref,
    turned_ref,
    rows_ref,
    left,
):
    core, step = place[0], pl.program_id(0)
    copies = [
        pltpu.make_async_copy(middle_ref, middle_hbm, left.at[0]),
        pltpu.make_async_copy(grad_ref, grad_hbm, left.at[1]),
    ]

    @pl.when(step == 0)
    def _():
        mine = w_out_ref[pl.ds(pl.multiple_of(core * SHARE, 128), SHARE), :]
        other = w_out_ref[pl.ds(pl.multiple_of((1 - core) * SHARE, 128), SHARE), :]
        assemble(place, own_ref, swapped_ref, host_ref, guest_ref, rows_ref)
        grad_ref[...] = rows_ref[...].astype(BF16)
        for begin, end in PARTS:
            rows = slice(begin, end)
            branch = jnp.dot(mixed_ref[rows, :], mine, preferred_element_type=F32)
            branch += jnp.dot(other_ref[rows, :], other, preferred_element_type=F32)
            middle = x_ref[rows, :].astype(F32) + branch + vector(out_bias_ref)
            middle_ref[rows, :] = middle
            second = norm_rows(middle)[0] * vector(gain_ref) + vector(bias_ref)
            second_ref[rows, :] = second.astype(BF16)
        for copy in copies:
            copy.start()
        turned_ref[...] = jnp.transpose(second_ref[...])

    for sub in range(2):
        columns = slice(SUB * sub, SUB * (sub + 1))
        column_sums = 0.0
        start = pl.multiple_of(core * FF_SHARE + step * 512 + SUB * sub, SUB)
        in_bias = vector(in_bias_ref, start, SUB)
        for begin, end in PARTS:
            rows = slice(begin, end)
            hidden = jnp.dot(second_ref[rows, :], w_in_ref[:, columns], preferred_element_type=F32)
            hidden += in_bias
            grad_active = lax.dot_general(
                grad_ref[rows, :], w_back_ref[columns, :], NT, preferred_element_type=F32
            )
            below = 0.5 + 0.5 * lax.erf(hidden * 0.7071067811865476)
            active_ref[rows, columns] = (hidden * below).astype(BF16)
            slope = below + hidden * jnp.exp(hidden * hidden * -0.5) * 0.3989422804014327
            grad_hidden = (grad_active * slope).astype(BF16)
            grad_hidden_ref[rows, columns] = grad_hidden
            column_sums += jnp.sum(grad_hidden.astype(F32), axis=0, keepdims=True)
        sums_ref[:, columns] = jnp.broadcast_to(column_sums, (8, SUB))
        total = jnp.dot(
            turned_ref[...], grad_hidden_ref[:, columns], preferred_element_type=F32
        ).astype(BF16)
        grad_in_ref[:, columns] = total
        total = lax.dot_general(
            active_ref[:, columns], grad_ref[...], TN, preferred_element_type=F32
        ).astype(BF16)
        grad_back_ref[columns, :] = total

    back = lax.dot_general(
        grad_hidden_ref[...], w_in_ref[...], NT, preferred_element_type=F32
    )

    @pl.when(step == 0)
    def _():
        rows_ref[...] = back

    @pl.when(step == 1)
    def _():
        rows_ref[...] += back

    @pl.when(step == 2)
    def _():
        back_ref[...] = (rows_ref[...] + back).astype(BF16)
        for copy in copies:
            copy.wait()


def middle_part(
    place, mixed, other, x, w_out, out_bias, gain, bias, grads, w_fc1, fc1_bias, w_fc2
):
    tokens, ff_columns = whole((TOK, WIDTH)), pl.BlockSpec((TOK, 512), lambda i, place: (0, i))
    return pl.pallas_call(
        middle_kernel,
        grid_spec=pltpu.PrefetchScalarGridSpec(
            num_scalar_prefetch=1,
            grid=(3,),
            in_specs=[once(a.shape) for a in (mixed, other, x, w_out)]
            + [WHOLE] * 3
            + [once(a.shape) for a in grads]
            + [
                pl.BlockSpec((WIDTH, 512), lambda i, place: (0, place[0] * 3 + i)),
                WHOLE,
                pl.BlockSpec((512, WIDTH), lambda i, place: (place[0] * 3 + i, 0)),
            ],
            out_specs=[
                ANYWHERE,
                ANYWHERE,
                ff_columns,
                pl.BlockSpec((512, WIDTH), lambda i, place: (i, 0)),
                pl.BlockSpec((WIDTH, 512), lambda i, place: (0, i)),
                pl.BlockSpec((8, 512), lambda i, place: (0, i)),
                tokens,
            ],
            scratch_shapes=[
                pltpu.VMEM((TOK, WIDTH), F32),
                pltpu.VMEM((TOK, WIDTH), BF16),
                pltpu.VMEM((TOK, 512), BF16),
                pltpu.VMEM((TOK, WIDTH), BF16),
                pltpu.VMEM((WIDTH, TOK), BF16),
                pltpu.VMEM((TOK, WIDTH), F32),
                pltpu.SemaphoreType.DMA((2,)),
            ],
        ),
        out_shape=[
            pltpu.HBM((TOK, WIDTH), F32),
            pltpu.HBM((TOK, WIDTH), BF16),
            pltpu.HBM((TOK, FF_SHARE), BF16),
            pltpu.HBM((FF_SHARE, WIDTH), BF16),
            pltpu.HBM((WIDTH, FF_SHARE), BF16),
            jax.ShapeDtypeStruct((8, FF_SHARE), F32),
            pltpu.HBM((TOK, WIDTH), BF16),
        ],
        compiler_params=params(44),
        cost_estimate=cost(10.5e9, 30e6, 3e6),
        name="middle_part",
    )(
        place,
        far(mixed),
        other,
        far(x),
        far(w_out),
        out_bias,
        gain,
        bias,
        *grads,
        far(w_fc1),
        fc1_bias,
        far(w_fc2),
    )


def halves(columns, first):
    def index(i, place):
        return (jnp.where(i == first, place[0], 1 - place[0]), 0)

    return pl.BlockSpec((HALF, columns), index)


def product_kernel(place, active_ref, w_back_ref, *refs):
    sent_ref, own_ref = refs[-2:]
    product = jnp.dot(active_ref[...], w_back_ref[...], preferred_element_type=F32)

    @pl.when(pl.program_id(0) == 0)
    def _():
        sent_ref[...] = product.astype(BF16)

    @pl.when(pl.program_id(0) == 1)
    def _():
        own_ref[...] = product


def mlp_product(place, active, w_fc2, after):
    return pl.pallas_call(
        product_kernel,
        grid_spec=pltpu.PrefetchScalarGridSpec(
            num_scalar_prefetch=1,
            grid=(2,),
            in_specs=[
                halves(FF_SHARE, 1),
                pl.BlockSpec((FF_SHARE, WIDTH), lambda i, place: (place[0], 0)),
            ]
            + [ANYWHERE] * len(after),
            out_specs=[whole((HALF, WIDTH)), whole((HALF, WIDTH))],
        ),
        out_shape=[pltpu.HBM((HALF, WIDTH), BF16), pltpu.HBM((HALF, WIDTH), F32)],
        compiler_params=params(24),
        cost_estimate=cost(1, 1),
        name="mlp_product",
    )(place, far(active), far(w_fc2), *after)


def attend_back_kernel(
    place,
    segments_ref,
    other_segments_ref,
    second_ref,
    other_ref,
    middle_ref,
    top_ref,
    mixed_ref,
    w_out_ref,
    gain_ref,
    in_sums_ref,
    x_hbm,
    first_hbm,
    w_hbm,
    q_ref,
    k_ref,
    v_ref,
    lse_ref,
    *refs,
):
    slots, (grad_middle_ref, own_ref, sent_ref), refs = refs[:8], refs[8:11], refs[11:]
    (
        late_ref,
        branch_ref,
        grad_mixed_ref,
        packed_ref,
        scores_ref,
        sums_ref,
        x_ref,
        first_ref,
        w_ref,
        arrived,
        left,
    ) = refs
    pair, core = pl.program_id(0), place[0]
    copies = [
        pltpu.make_async_copy(x_hbm, x_ref, arrived.at[0]),
        pltpu.make_async_copy(first_hbm, first_ref, arrived.at[1]),
    ]
    for kind in range(3):
        start = pl.multiple_of(kind * WIDTH + core * SHARE, 128)
        copies.append(
            pltpu.make_async_copy(
                w_hbm.at[:, pl.ds(start, SHARE)],
                w_ref.at[:, pl.ds(kind * SHARE, SHARE)],
                arrived.at[2 + kind],
            )
        )

    def half_rows(which, begin, end):
        return pl.ds(pl.multiple_of(which * HALF + begin, 16), end - begin)

    @pl.when(pair == 0)
    def _():
        for copy in copies:
            copy.start()
        sums = [0.0, 0.0, 0.0, 0.0]
        for which in (core, 1 - core):
            for begin, end in ((0, 256), (256, HALF)):
                rows = half_rows(which, begin, end)
                grad = second_ref[rows, :].astype(F32) + other_ref[rows, :].astype(F32)
                normed, inverse = norm_rows(middle_ref[rows, :])
                product = grad * normed
                scaled = grad * vector(gain_ref)
                top = top_ref[rows, :].astype(F32)
                grad_middle = top + inverse * (
                    scaled
                    - jnp.mean(scaled, axis=-1, keepdims=True)
                    - normed * jnp.mean(product * vector(gain_ref), axis=-1, keepdims=True)
                )
                if which is core:
                    grad_middle_ref[begin:end, :] = grad_middle
                branch = grad_middle.astype(BF16)
                branch_ref[rows, :] = branch
                grad_mixed_ref[rows, :] = lax.dot_general(
                    branch, w_out_ref[...], NT, preferred_element_type=F32
                ).astype(BF16)
                for i, values in enumerate((branch.astype(F32), product, grad, top)):
                    sums[i] += jnp.sum(values, axis=0, keepdims=True)
        for i in range(4):
            sums_ref[8 * i : 8 * i + 8, :] = jnp.broadcast_to(sums[i], (8, WIDTH))
        total = lax.dot_general(mixed_ref[...], branch_ref[...], TN, preferred_element_type=F32)
        total = total.astype(BF16)
        for a in range(8):
            for b in range(2):
                for s in range(3):
                    row = WIDTH + 16 * (2 * a + b)
                    late_ref[row : row + 16, SHARE * s : SHARE * (s + 1)] = total[
                        48 * a + 16 * s : 48 * a + 16 * s + 16, SHARE * b : SHARE * (b + 1)
                    ]

    attention_back(
        pair,
        small_comes_first(place, segments_ref, other_segments_ref),
        q_ref,
        k_ref,
        v_ref,
        grad_mixed_ref,
        mixed_ref,
        lse_ref,
        packed_ref,
        scores_ref,
    )

    @pl.when(pair == 2)
    def _():
        for copy in copies:
            copy.wait()
        late_ref[:WIDTH, : 3 * SHARE] = lax.dot_general(
            first_ref[...], packed_ref[...], TN, preferred_element_type=F32
        ).astype(BF16)
        gain, bias, packed = 0.0, 0.0, 0.0
        for which in (core, 1 - core):
            for begin, end in ((0, 256), (256, HALF)):
                rows = half_rows(which, begin, end)
                grad = packed_ref[rows, :]
                part = lax.dot_general(grad, w_ref[...], NT, preferred_element_type=F32)
                if which is core:
                    own_ref[begin:end, :] = part
                else:
                    sent_ref[begin:end, :] = part.astype(BF16)
                gain += jnp.sum(
                    part * norm_rows(x_ref[rows, :].astype(F32))[0], axis=0, keepdims=True
                )
                bias += jnp.sum(part, axis=0, keepdims=True)
                packed += jnp.sum(grad.astype(F32), axis=0, keepdims=True)
        pieces = [sums_ref[8 * i : 8 * i + 1, :] for i in range(3)]
        pieces += [gain, bias, sums_ref[24:25, :]]
        pieces += [packed[:, :SHARE], packed[:, 2 * SHARE :], in_sums_ref[:1, :]]
        late_ref[:, 3 * SHARE :] = jnp.zeros((16 * PEERS, 128), BF16)
        at = 0
        for piece in pieces:
            for tile in range(piece.shape[1] // 128):
                late_ref[16 * at : 16 * at + 16, 3 * SHARE :] = jnp.broadcast_to(
                    piece[:, 128 * tile : 128 * (tile + 1)], (16, 128)
                ).astype(BF16)
                at += 1
        parts = []
        for side in range(2):
            for hop in range(4):
                start = pl.multiple_of(256 * lax.rem(place[2 + side] + hop, 4), 256)
                parts.append(
                    pltpu.make_async_copy(
                        late_ref.at[pl.ds(start, 256), pl.ds(LATE_HALF * side, LATE_HALF)],
                        slots[4 * side + hop],
                        left.at[4 * side + hop],
                    )
                )
        for copy in parts:
            copy.start()
        for copy in parts:
            copy.wait()


def attend_back(
    place, segments, second, other, middle, top, mixed, w_out, gain, in_sums, x, first, w_qkv, heads
):
    tokens, half = once((TOK, WIDTH)), whole((HALF, WIDTH))
    return pl.pallas_call(
        attend_back_kernel,
        grid_spec=pltpu.PrefetchScalarGridSpec(
            num_scalar_prefetch=1,
            grid=(3,),
            in_specs=[
                SCALARS,
                SCALARS,
                tokens,
                tokens,
                tokens,
                tokens,
                once((TOK, SHARE)),
                once((SHARE, WIDTH), lambda i, place: (place[0], 0)),
                WHOLE,
                WHOLE,
                ANYWHERE,
                ANYWHERE,
                ANYWHERE,
            ]
            + [block()] * 4,
            out_specs=[ANYWHERE] * 8 + [half, half, half],
            scratch_shapes=[
                pltpu.VMEM((16 * PEERS, LATE), BF16),
                pltpu.VMEM((TOK, WIDTH), BF16),
                pltpu.VMEM((TOK, SHARE), BF16),
                pltpu.VMEM((TOK, 3 * SHARE), BF16),
                pltpu.VMEM((2, BIG_Q, BIG_K), BF16),
                pltpu.VMEM((32, WIDTH), F32),
                pltpu.VMEM((TOK, WIDTH), BF16),
                pltpu.VMEM((TOK, WIDTH), BF16),
                pltpu.VMEM((WIDTH, 3 * SHARE), BF16),
                pltpu.SemaphoreType.DMA((5,)),
                pltpu.SemaphoreType.DMA((8,)),
            ],
        ),
        out_shape=[pltpu.HBM((256, LATE_HALF), BF16)] * 8
        + [
            pltpu.HBM((HALF, WIDTH), F32),
            pltpu.HBM((HALF, WIDTH), F32),
            pltpu.HBM((HALF, WIDTH), BF16),
        ],
        compiler_params=params(46),
        cost_estimate=cost(1, 1),
        name="attend_back",
    )(
        place,
        *segments,
        far(second),
        other,
        far(middle),
        far(top),
        far(mixed),
        far(w_out),
        gain,
        in_sums,
        far(x),
        far(first),
        far(w_qkv),
        *(far(a) for a in heads),
    )


def small_call(kernel, name, arrays, shapes, place, scratch=(), after=()):
    count = 1 + len(arrays)

    def body(*refs):
        kernel(*refs[:count], *refs[count + len(after) :])

    return pl.pallas_call(
        body,
        in_specs=[SCALARS] + [WHOLE] * len(arrays) + [ANYWHERE] * len(after),
        out_specs=[WHOLE] * len(shapes),
        out_shape=[jax.ShapeDtypeStruct(shape, BF16) for shape in shapes],
        scratch_shapes=list(scratch),
        compiler_params=params(16),
        cost_estimate=cost(1, 1),
        name=name,
    )(place, *arrays, *after)


def total_of(refs):
    total = refs[0][...].astype(F32)
    for ref in refs[1:]:
        total += ref[...].astype(F32)
    return total.astype(BF16)


def turn(place, axis, hop, size):
    return pl.ds(pl.multiple_of(size * lax.rem(place[axis] + hop, 4), size), size)


def sum_first_kernel(place, *refs):
    scratch = refs[-1]
    for side in range(2):
        scratch[...] = total_of(refs[4 * side : 4 * side + 4])
        for hop in range(4):
            refs[8 + 4 * side + hop][...] = scratch[turn(place, 3 - side, hop, 64), :]


def sum_second_kernel(place, *refs):
    scratch = refs[-1]
    for side in range(2):
        columns = slice(LATE_HALF * side, LATE_HALF * (side + 1))
        scratch[:, columns] = total_of(refs[4 * side : 4 * side + 4])
    for hop in range(4):
        refs[8 + hop][...] = scratch[turn(place, 4, hop, 16), :]


def sum_third_kernel(place, *refs):
    refs[-1][...] = total_of(refs[:4])


def join_third_kernel(place, *refs):
    for hop in range(4):
        rows = turn(place, 4, 4 - hop, 16)
        for side in range(2):
            columns = slice(LATE_HALF * side, LATE_HALF * (side + 1))
            refs[4 + side][rows, :] = refs[hop][:, columns]


def join_second_kernel(place, *refs):
    for side in range(2):
        for hop in range(4):
            refs[8 + side][turn(place, 3 - side, 4 - hop, 64), :] = refs[4 * side + hop][...]


def join_first_kernel(place, *refs):
    for side in range(2):
        columns = slice(LATE_HALF * side, LATE_HALF * (side + 1))
        for hop in range(4):
            refs[8][turn(place, 2 + side, 4 - hop, 256), columns] = refs[4 * side + hop][...]


def around(parts, axis):
    return [parts[0]] + [
        lax.ppermute(parts[hop], axis, [(i, (i + hop) % 4) for i in range(4)]) for hop in (1, 2, 3)
    ]


def sum_late(parts, place, first, second):
    depth = ("zh", "zl")
    parts = small_call(
        sum_first_kernel,
        "sum_first",
        parts,
        [(64, LATE_HALF)] * 8,
        place,
        [pltpu.VMEM((256, LATE_HALF), BF16)],
    )
    parts = around(parts[:4], "y") + around(parts[4:], "x")
    parts = small_call(
        sum_second_kernel,
        "sum_second",
        parts,
        [(16, LATE)] * 4,
        place,
        [pltpu.VMEM((64, LATE), BF16)],
        first,
    )
    (share,) = small_call(
        sum_third_kernel, "sum_third", around(parts, depth), [(16, LATE)], place
    )
    one, two = small_call(
        join_third_kernel, "join_third", around([share] * 4, depth), [(64, LATE_HALF)] * 2, place
    )
    parts = around([one] * 4, "y") + around([two] * 4, "x")
    one, two = small_call(
        join_second_kernel, "join_second", parts, [(256, LATE_HALF)] * 2, place, after=second
    )
    return around([one] * 4, "x") + around([two] * 4, "y")


def join_late(parts, place):
    return small_call(join_first_kernel, "join_first", parts, [(16 * PEERS, LATE)], place)[0]


def widen_kernel(
    place,
    back_ref,
    in_ref,
    mine_ref,
    other_ref,
    mine_small_ref,
    other_small_ref,
    total_back_ref,
    total_in_ref,
    packed_ref,
    out_ref,
    in_bias_ref,
    q_bias_ref,
    v_bias_ref,
    *vector_refs,
):
    step, first = pl.program_id(0), place[0] == 0
    total_back_ref[...] = back_ref[...].astype(F32)
    total_in_ref[...] = in_ref[...].astype(F32)

    def pick(side, mine_ref, other_ref, rows, columns):
        mine, other = mine_ref[rows, columns].astype(F32), other_ref[rows, columns].astype(F32)
        return jnp.where(first if side == 0 else jnp.logical_not(first), mine, other)

    @pl.when(step < 3)
    def _():
        for side in range(2):
            for kind in range(3):
                at = SHARE * (2 * kind + side)
                packed_ref[:, at : at + SHARE] = pick(
                    side, mine_ref, other_ref, slice(0, 256), slice(SHARE * kind, SHARE * (kind + 1))
                )

    @pl.when(step == 3)
    def _():
        for side in range(2):
            for a in range(8):
                for b in range(2):
                    row = 16 * (2 * a + b)
                    for s in range(3):
                        at = SHARE * side + 48 * a + 16 * s
                        out_ref[at : at + 16, SHARE * b : SHARE * (b + 1)] = pick(
                            side,
                            mine_ref,
                            other_ref,
                            slice(row, row + 16),
                            slice(SHARE * s, SHARE * (s + 1)),
                        )

    @pl.when(step == 0)
    def _():
        def piece(side, at):
            rows = slice(16 * at, 16 * at + 16)
            return pick(side, mine_small_ref, other_small_ref, rows, slice(0, 128))[:1]

        def put(ref, tile, value):
            ref[128 * tile : 128 * (tile + 1)] = value.reshape(128)

        for tile in range(6):
            for at in range(6):
                value = piece(0, 6 * at + tile)
                if at in (3, 4):
                    value += piece(1, 6 * at + tile)
                put(vector_refs[at], tile, value)
        for side in range(2):
            for tile in range(3):
                put(q_bias_ref, 3 * side + tile, piece(side, 36 + tile))
                put(v_bias_ref, 3 * side + tile, piece(side, 39 + tile))
            for tile in range(12):
                put(in_bias_ref, 12 * side + tile, piece(side, 42 + tile))


def widen(place, early, late, late_other):
    rows = pl.BlockSpec((256, LATE), lambda i, place: (i, 0))
    small = pl.BlockSpec((16 * PEERS, 128), lambda i, place: (0, 9))
    vectors = [jax.ShapeDtypeStruct((2 * FF_SHARE,), F32)] + [jax.ShapeDtypeStruct((WIDTH,), F32)] * 8
    return pl.pallas_call(
        widen_kernel,
        grid_spec=pltpu.PrefetchScalarGridSpec(
            num_scalar_prefetch=1,
            grid=(4,),
            in_specs=[
                pl.BlockSpec((512, WIDTH), lambda i, place: (jnp.minimum(i, 2), 0)),
                pl.BlockSpec((WIDTH, 512), lambda i, place: (0, jnp.minimum(i, 2))),
                rows,
                rows,
                small,
                small,
            ],
            out_specs=[
                pl.BlockSpec((512, WIDTH), lambda i, place: (3 * place[0] + jnp.minimum(i, 2), 0)),
                pl.BlockSpec((WIDTH, 512), lambda i, place: (0, 3 * place[0] + jnp.minimum(i, 2))),
                pl.BlockSpec((256, 3 * WIDTH), lambda i, place: (jnp.minimum(i, 2), 0)),
                whole((WIDTH, WIDTH)),
            ]
            + [WHOLE] * 9,
        ),
        out_shape=[
            pltpu.HBM((2 * FF_SHARE, WIDTH), F32),
            pltpu.HBM((WIDTH, 2 * FF_SHARE), F32),
            pltpu.HBM((WIDTH, 3 * WIDTH), F32),
            pltpu.HBM((WIDTH, WIDTH), F32),
        ]
        + vectors,
        compiler_params=params(32),
        cost_estimate=cost(0, 100e6),
        name="widen",
    )(place, *(far(a) for a in (*early, late, late_other, late, late_other)))


def widen_rest_kernel(place, back_ref, in_ref, same_back_ref, same_in_ref, total_back_ref, total_in_ref):
    total_back_ref[...] = back_ref[...].astype(F32)
    total_in_ref[...] = in_ref[...].astype(F32)


def widen_rest(place, early, totals):
    return pl.pallas_call(
        widen_rest_kernel,
        grid_spec=pltpu.PrefetchScalarGridSpec(
            num_scalar_prefetch=1,
            grid=(3,),
            in_specs=[
                pl.BlockSpec((512, WIDTH), lambda i, place: (i, 0)),
                pl.BlockSpec((WIDTH, 512), lambda i, place: (0, i)),
                ANYWHERE,
                ANYWHERE,
            ],
            out_specs=[
                pl.BlockSpec((512, WIDTH), lambda i, place: (3 - 3 * place[0] + i, 0)),
                pl.BlockSpec((WIDTH, 512), lambda i, place: (0, 3 - 3 * place[0] + i)),
            ],
        ),
        out_shape=[
            pltpu.HBM((2 * FF_SHARE, WIDTH), F32),
            pltpu.HBM((WIDTH, 2 * FF_SHARE), F32),
        ],
        input_output_aliases={3: 0, 4: 1},
        compiler_params=params(24),
        cost_estimate=cost(0, 14e6),
        name="widen_rest",
    )(place, *early, *(far(a) for a in totals))


def norm_back(grad_normed, normed, inverse):
    return inverse * (
        grad_normed
        - jnp.mean(grad_normed, axis=-1, keepdims=True)
        - normed * jnp.mean(grad_normed * normed, axis=-1, keepdims=True)
    )


def other_core(values):
    return lax.ppermute(values, "c", [(0, 1), (1, 0)])


def swap_home(values):
    return lax.ppermute(values, ("c", "zl"), [(1, 2), (2, 1)])


def from_host(values):
    return lax.ppermute(values, ("c", "zl"), [(0, 2), (3, 1)])


def from_guest(values):
    return lax.ppermute(values, ("c", "zl"), [(2, 0), (1, 3)])


def from_next(values):
    return lax.ppermute(values, ("c", "zl"), [(1, 0), (2, 3)])


def body(
    inputs,
    segments,
    cotangent,
    ln1_gain,
    ln1_bias,
    w_qkv,
    q_bias,
    v_bias,
    w_out,
    out_bias,
    ln2_gain,
    ln2_bias,
    w_fc1,
    fc1_bias,
    w_fc2,
    fc2_bias,
):
    core = lax.axis_index("c")
    home = core == lax.axis_index("zl")

    def half(array, which):
        return lax.dynamic_slice_in_dim(array, which * HALF, HALF, 0)

    tokens, top = inputs[0], cotangent[0]
    swapped = swap_home(tokens)
    rows = (tokens, swapped, from_host(tokens), from_guest(swapped))
    images = (segments, other_core(segments))
    depth = 2 * lax.axis_index("zh") + lax.axis_index("zl")
    place = [core, home, lax.axis_index("x"), lax.axis_index("y"), depth]
    place = jnp.stack([index.astype(jnp.int32) for index in place])

    sent = jnp.concatenate([top, swapped[: HALF - REAL]], axis=0)
    tops = (top, swap_home(sent), from_host(top), from_next(sent))

    x_all, first_in, query, key, value, mixed, lse = attend(
        place, images, rows, ln1_gain, ln1_bias, w_qkv, q_bias, v_bias
    )
    middle, grad_top, active, grad_back, grad_in, in_sums, second = middle_part(
        place,
        mixed,
        other_core(mixed),
        x_all,
        w_out,
        out_bias,
        ln2_gain,
        ln2_bias,
        tops,
        w_fc1,
        fc1_bias,
        w_fc2,
    )
    early = lax.psum((grad_back, grad_in), CHIPS)
    *late, grad_middle, first_part, first_sent = attend_back(
        place,
        images,
        second,
        other_core(second),
        middle,
        grad_top,
        mixed,
        w_out,
        ln2_gain,
        in_sums,
        x_all,
        first_in,
        w_qkv,
        (query, key, value, lse),
    )
    late = around(late[:4], "x") + around(late[4:], "y")
    product_sent, product = mlp_product(place, active, w_fc2, (late[5],))
    result = half(middle, core) + product + other_core(product_sent).astype(F32) + fc2_bias
    result = result.astype(BF16)
    output = jnp.where(home, result, swap_home(result))[None, :REAL]

    grad_first_in = first_part + other_core(first_sent).astype(F32)
    normed_one, inverse_one = norm_rows(half(x_all, core).astype(F32))
    grad_input = grad_middle + norm_back(grad_first_in * ln1_gain, normed_one, inverse_one)
    grad_input = grad_input.astype(BF16)
    input_grad = jnp.where(home, grad_input, swap_home(grad_input))[None, :REAL]

    late = sum_late(late, place, (result, grad_input), (output, input_grad))
    early_other = [other_core(a) for a in early]
    late = join_late(late, place)
    total_back, total_in, total_packed, total_out, in_bias, total_q_bias, total_v_bias, *vectors = widen(
        place, early, late, other_core(late)
    )
    total_back, total_in = widen_rest(place, early_other, (total_back, total_in))
    return (
        output,
        input_grad,
        vectors[3],
        vectors[4],
        total_packed,
        total_q_bias,
        total_v_bias,
        total_out,
        vectors[0],
        vectors[1],
        vectors[2],
        total_in,
        in_bias,
        total_back,
        vectors[5],
    )


def solution(mesh):
    fine = Mesh(mesh.devices.reshape(4, 4, 2, 2, 2), ("x", "y", "zh", "c", "zl"))
    tokens = P(ROWS, "zl", None)
    return jax.shard_map(
        body,
        mesh=fine,
        in_specs=(tokens, P(ROWS, None), tokens) + (P(),) * 13,
        out_specs=(tokens, tokens) + (P(),) * 13,
        check_vma=False,
    )
```

```python
import jax
import jax.numpy as jnp
from jax import lax
from jax.experimental import pallas as pl
from jax.experimental.pallas import tpu as pltpu
from jax.sharding import Mesh
from jax.sharding import PartitionSpec as P


HALF = 496
TOK = 2 * HALF
REAL = 490
PAIR = 128
BIG_Q, BIG_K, BIG_STEP = 800, 896, 160
WIDTH = 768
SMALL_Q, SMALL_K = 208, 256
OFF = -1e30
F32, BF16 = jnp.float32, jnp.bfloat16
PARTS = ((0, 256), (256, 512), (512, 768), (768, TOK))
NT = (((1,), (1,)), ((), ()))
TN = (((0,), (0,)), ((), ()))


def windows(small_first):
    big = (
        pl.multiple_of(small_first * 192, 32),
        pl.multiple_of(small_first * 96, 32),
        small_first * 196,
        790 + small_first * 196,
    )
    small = (
        pl.multiple_of((1 - small_first) * 784, 16),
        pl.multiple_of((1 - small_first) * 736, 32),
        (1 - small_first) * 790,
        196 + (1 - small_first) * 790,
    )
    return big, small


def in_image(start, count, first, end):
    rows = start + lax.broadcasted_iota(jnp.int32, (count, PAIR), 0)
    return (rows >= first) & (rows < end) & ((rows < REAL) | (rows >= HALF))


def lanes(count):
    return lax.broadcasted_iota(jnp.int32, (count, PAIR), 1)


def own(lane, head):
    return lane < 64 if head == 0 else lane >= 64


def norm_rows(values):
    center = values - jnp.mean(values, axis=-1, keepdims=True)
    inverse = lax.rsqrt(jnp.mean(center * center, axis=-1, keepdims=True) + 1e-06)
    return center * inverse, inverse


def assemble(place, own_ref, swapped_ref, host_ref, guest_ref, rows_ref):
    core, home = place[0], place[1] == 1
    for half, at_home, away in ((core, own_ref, swapped_ref), (1 - core, guest_ref, host_ref)):
        start = pl.multiple_of(half * HALF, 16)
        rows_ref[pl.ds(pl.multiple_of(start + 488, 8), 8), :] = jnp.zeros((8, WIDTH), F32)

        @pl.when(home)
        def _():
            rows_ref[pl.ds(start, REAL), :] = at_home[...][:REAL].astype(F32)

        @pl.when(jnp.logical_not(home))
        def _():
            rows_ref[pl.ds(start, REAL), :] = away[...][:REAL].astype(F32)


def small_comes_first(place, segments_ref, other_ref):
    mine = segments_ref[0, 196] != segments_ref[0, 0]
    other = other_ref[0, 196] != other_ref[0, 0]
    return jnp.where(place[1] == 1, mine.astype(jnp.int32), other.astype(jnp.int32))


def vector(ref, start=0, size=WIDTH):
    return ref[pl.ds(start, size)].reshape(1, size)


def attend_kernel(
    place,
    segments_ref,
    other_segments_ref,
    own_ref,
    swapped_ref,
    host_ref,
    guest_ref,
    gain_ref,
    bias_ref,
    wq_ref,
    wk_ref,
    wv_ref,
    q_bias_ref,
    v_bias_ref,
    x_hbm,
    first_hbm,
    q_ref,
    k_ref,
    v_ref,
    mixed_ref,
    lse_ref,
    x_ref,
    first_ref,
    rows_ref,
    left,
):
    pair = pl.program_id(0)
    copies = [
        pltpu.make_async_copy(x_ref, x_hbm, left.at[0]),
        pltpu.make_async_copy(first_ref, first_hbm, left.at[1]),
    ]

    @pl.when(pair == 0)
    def _():
        assemble(place, own_ref, swapped_ref, host_ref, guest_ref, rows_ref)
        for begin, end in PARTS:
            rows = slice(begin, end)
            values = rows_ref[rows, :]
            x_ref[rows, :] = values.astype(BF16)
            first = norm_rows(values)[0] * vector(gain_ref) + vector(bias_ref)
            first_ref[rows, :] = first.astype(BF16)
        for copy in copies:
            copy.start()

    weights = jnp.concatenate([wq_ref[...], wk_ref[...], wv_ref[...]], axis=1)
    start = pl.multiple_of((3 * place[0] + pair) * PAIR, PAIR)
    q_bias, v_bias = vector(q_bias_ref, start, PAIR), vector(v_bias_ref, start, PAIR)
    for begin, end in PARTS:
        rows = slice(begin, end)
        packed = jnp.dot(first_ref[rows, :], weights, preferred_element_type=F32)
        q_ref[rows, :] = (packed[:, :PAIR] + q_bias).astype(BF16)
        k_ref[rows, :] = packed[:, PAIR : 2 * PAIR].astype(BF16)
        v_ref[rows, :] = (packed[:, 2 * PAIR :] + v_bias).astype(BF16)

    small_first = small_comes_first(place, segments_ref, other_segments_ref)
    big, small = windows(small_first)

    def image(window, queries, step, keys, merge):
        q_start, k_start, first, end = window
        lane_k = lanes(keys)
        bias = jnp.where(in_image(k_start, keys, first, end), 0.0, OFF)
        k_all = k_ref[pl.ds(k_start, keys), :].astype(F32)
        v_all = v_ref[pl.ds(k_start, keys), :].astype(F32)
        k_heads, v_heads = [], []
        for head in range(2):
            spare = 64 - 64 * head
            k_heads.append(
                jnp.where(own(lane_k, head), k_all, jnp.where(lane_k == spare, bias, 0.0)).astype(BF16)
            )
            v_heads.append(
                jnp.where(own(lane_k, head), v_all, jnp.where(lane_k == spare, 1.0, 0.0)).astype(BF16)
            )
        lane = lanes(step)
        for part in range(queries // step):
            start = pl.multiple_of(q_start + part * step, 16)
            here = pl.ds(start, step)
            q_part = q_ref[here, :].astype(F32) * 0.125
            outs, sums = [], []
            for head in range(2):
                spare = 64 - 64 * head
                q_head = jnp.where(
                    own(lane, head), q_part, jnp.where(lane == spare, 1.0, 0.0)
                ).astype(BF16)
                scores = lax.dot_general(q_head, k_heads[head], NT, preferred_element_type=F32)
                top = jnp.max(scores, axis=1, keepdims=True)
                weights = jnp.exp(scores - top).astype(BF16)
                out = jnp.dot(weights, v_heads[head], preferred_element_type=F32)
                total = out[:, spare : spare + 1]
                outs.append(out * (1.0 / total))
                sums.append(top + jnp.log(total))
            mixed = jnp.where(lane < 64, outs[0], outs[1])
            lse = jnp.where(lane < 64, sums[1], sums[0])
            if merge:
                rows = start + lax.broadcasted_iota(jnp.int32, (step, PAIR), 0)
                keep = (rows >= small[2]) & ((rows < 196) | (small_first == 0))
                mixed = jnp.where(keep, mixed_ref[here, :].astype(F32), mixed)
                lse = jnp.where(keep, lse_ref[here, :], lse)
            mixed_ref[here, :] = mixed.astype(BF16)
            lse_ref[here, :] = lse

    image(small, SMALL_Q, SMALL_Q, SMALL_K, False)
    image(big, BIG_Q, BIG_Q, BIG_K, True)

    @pl.when(pair == 2)
    def _():
        for copy in copies:
            copy.wait()


WHOLE = pl.BlockSpec(memory_space=pltpu.VMEM)
SCALARS = pl.BlockSpec(memory_space=pltpu.SMEM)
ANYWHERE = pl.BlockSpec(memory_space=pl.ANY)


def params(mib):
    return pltpu.CompilerParams(vmem_limit_bytes=mib * 2**20)


def cost(flops, traffic, transcendentals=0):
    return pl.CostEstimate(
        flops=int(flops), bytes_accessed=int(traffic), transcendentals=int(transcendentals)
    )


def far(array):
    return pltpu.with_memory_space_constraint(array, pltpu.HBM)


def block():
    return pl.BlockSpec((TOK, PAIR), lambda i, place: (0, i))


def whole(shape):
    return pl.BlockSpec(shape, lambda i, place: (0,) * len(shape))


def once(shape, index=lambda i, place: (0, 0)):
    return pl.BlockSpec(shape, index, pipeline_mode=pl.Buffered(1))


def attend(place, segments, tokens, gain, bias, w_qkv, q_bias, v_bias):
    def weight(kind):
        return pl.BlockSpec((WIDTH, PAIR), lambda i, place: (0, 6 * kind + 3 * place[0] + i))

    heads = pltpu.HBM((TOK, 3 * PAIR), BF16)
    return pl.pallas_call(
        attend_kernel,
        grid_spec=pltpu.PrefetchScalarGridSpec(
            num_scalar_prefetch=1,
            grid=(3,),
            in_specs=[SCALARS, SCALARS]
            + [once((REAL, WIDTH))] * 4
            + [WHOLE, WHOLE, weight(0), weight(1), weight(2), WHOLE, WHOLE],
            out_specs=[ANYWHERE, ANYWHERE, block(), block(), block(), block(), block()],
            scratch_shapes=[
                pltpu.VMEM((TOK, WIDTH), BF16),
                pltpu.VMEM((TOK, WIDTH), BF16),
                pltpu.VMEM((TOK, WIDTH), F32),
                pltpu.SemaphoreType.DMA((2,)),
            ],
        ),
        out_shape=[
            pltpu.HBM((TOK, WIDTH), BF16),
            pltpu.HBM((TOK, WIDTH), BF16),
            heads,
            heads,
            heads,
            heads,
            pltpu.HBM((TOK, 3 * PAIR), F32),
        ],
        compiler_params=params(36),
        cost_estimate=cost(8e9, 15e6, 4e6),
        name="attend",
    )(
        place,
        *segments,
        *tokens,
        gain,
        bias,
        far(w_qkv),
        far(w_qkv),
        far(w_qkv),
        q_bias,
        v_bias,
    )


def split(values):
    high = values.astype(BF16).astype(F32)
    return high, values - high


def attention_back(pair, small_first, q_ref, k_ref, v_ref, grad_ref, mixed_ref, lse_ref, out_ref, scores_ref):
    big, small = windows(small_first)
    pair_lanes = pl.ds(pl.multiple_of(pair * PAIR, PAIR), PAIR)

    def lanes_of(kind):
        return pl.ds(pl.multiple_of((3 * kind + pair) * PAIR, PAIR), PAIR)

    def image(window, keys, step, queries, add):
        k_start, q_start, first, end = window
        here = pl.ds(q_start, queries)
        lane = lanes(queries)
        bias = jnp.where(in_image(q_start, queries, first, end), 0.0, OFF)
        q_all = q_ref[here, :].astype(F32) * 0.125
        q_low = q_all.astype(BF16)
        grad_low = grad_ref[here, pair_lanes]
        grad_all = grad_low.astype(F32)
        products = grad_all * mixed_ref[here, pair_lanes].astype(F32)
        lse_high, lse_rest = split(lse_ref[here, :])
        lse_mid, lse_low = split(lse_rest)
        q_heads, grad_heads = [], []
        for head in range(2):
            spare = 64 - 64 * head
            mine = own(lane, head)
            q_head = jnp.where(mine, q_all, 0.0)
            for at, extra in enumerate((1.0, -lse_high, -lse_mid, -lse_low, bias)):
                q_head = jnp.where(lane == spare + at, extra, q_head)
            q_heads.append(q_head.astype(BF16))
            row_term = jnp.sum(jnp.where(mine, products, 0.0), axis=1, keepdims=True)
            term_high, term_low = split(row_term)
            grad_head = jnp.where(mine, grad_all, 0.0)
            grad_head = jnp.where(lane == spare + 1, -term_high, grad_head)
            grad_head = jnp.where(lane == spare + 2, -term_low, grad_head)
            grad_heads.append(grad_head.astype(BF16))
        lane = lanes(step)
        for part in range(keys // step):
            start = pl.multiple_of(k_start + part * step, 16)
            rows = pl.ds(start, step)
            k_part = k_ref[rows, :].astype(F32)
            v_part = v_ref[rows, :].astype(F32)
            key_bias = jnp.where(in_image(start, step, first, end), 0.0, OFF)
            keys_grad, values_grad = [], []
            for head in range(2):
                spare = 64 - 64 * head
                mine = own(lane, head)
                ones = (lane >= spare + 1) & (lane <= spare + 4)
                k_head = jnp.where(mine, k_part, jnp.where(ones, 1.0, 0.0))
                k_head = jnp.where(lane == spare, key_bias, k_head).astype(BF16)
                v_head = jnp.where(mine, v_part, jnp.where(ones, 1.0, 0.0)).astype(BF16)
                probs = jnp.exp(
                    lax.dot_general(k_head, q_heads[head], NT, preferred_element_type=F32)
                )
                change = lax.dot_general(v_head, grad_heads[head], NT, preferred_element_type=F32)
                grad_scores = (probs * change).astype(BF16)
                values_grad.append(
                    jnp.dot(probs.astype(BF16), grad_low, preferred_element_type=F32)
                )
                keys_grad.append(jnp.dot(grad_scores, q_low, preferred_element_type=F32))
                scores_ref[head, part * step : (part + 1) * step, :queries] = grad_scores
            key_out = jnp.where(lane < 64, keys_grad[0], keys_grad[1]).astype(BF16)
            value_out = jnp.where(lane < 64, values_grad[0], values_grad[1]).astype(BF16)
            if add:
                key_out = key_out + out_ref[rows, lanes_of(1)]
                value_out = value_out + out_ref[rows, lanes_of(2)]
            out_ref[rows, lanes_of(1)] = key_out
            out_ref[rows, lanes_of(2)] = value_out
        k_all = k_ref[pl.ds(k_start, keys), :]
        turned = [
            lax.dot_general(k_all, scores_ref[head, :keys, :queries], TN, preferred_element_type=F32)
            for head in range(2)
        ]
        row = lax.broadcasted_iota(jnp.int32, (PAIR, queries), 0)
        query_out = jnp.transpose(jnp.where(row < 64, turned[0], turned[1]) * 0.125).astype(BF16)
        if add:
            query_out = query_out + out_ref[here, lanes_of(0)]
        out_ref[here, lanes_of(0)] = query_out

    out_ref[pl.ds(small[0], SMALL_Q), lanes_of(1)] = jnp.zeros((SMALL_Q, PAIR), BF16)
    out_ref[pl.ds(small[0], SMALL_Q), lanes_of(2)] = jnp.zeros((SMALL_Q, PAIR), BF16)
    out_ref[pl.ds(small[1], SMALL_K), lanes_of(0)] = jnp.zeros((SMALL_K, PAIR), BF16)
    image(big, BIG_Q, BIG_STEP, BIG_K, False)
    image(small, SMALL_Q, SMALL_Q, SMALL_K, True)


FF_SHARE = 1536
SUB = 256
SHARE = 384
PEERS = 64
LATE = 3 * SHARE + 128
LATE_HALF = LATE // 2
CHIPS = ("x", "y", "zh", "zl")
ROWS = ("x", "y", "zh", "c")

def middle_kernel(
    place,
    mixed_ref,
    other_ref,
    x_ref,
    w_out_ref,
    out_bias_ref,
    gain_ref,
    bias_ref,
    own_ref,
    swapped_ref,
    host_ref,
    guest_ref,
    w_in_ref,
    in_bias_ref,
    w_back_ref,
    middle_hbm,
    grad_hbm,
    active_ref,
    grad_back_ref,
    grad_in_ref,
    sums_ref,
    back_ref,
    middle_ref,
    grad_ref,
    grad_hidden_ref,
    second_ref,
    turned_ref,
    rows_ref,
    left,
):
    core, step = place[0], pl.program_id(0)
    copies = [
        pltpu.make_async_copy(middle_ref, middle_hbm, left.at[0]),
        pltpu.make_async_copy(grad_ref, grad_hbm, left.at[1]),
    ]

    @pl.when(step == 0)
    def _():
        mine = w_out_ref[pl.ds(pl.multiple_of(core * SHARE, 128), SHARE), :]
        other = w_out_ref[pl.ds(pl.multiple_of((1 - core) * SHARE, 128), SHARE), :]
        assemble(place, own_ref, swapped_ref, host_ref, guest_ref, rows_ref)
        grad_ref[...] = rows_ref[...].astype(BF16)
        for begin, end in PARTS:
            rows = slice(begin, end)
            branch = jnp.dot(mixed_ref[rows, :], mine, preferred_element_type=F32)
            branch += jnp.dot(other_ref[rows, :], other, preferred_element_type=F32)
            middle = x_ref[rows, :].astype(F32) + branch + vector(out_bias_ref)
            middle_ref[rows, :] = middle
            second = norm_rows(middle)[0] * vector(gain_ref) + vector(bias_ref)
            second_ref[rows, :] = second.astype(BF16)
        for copy in copies:
            copy.start()
        turned_ref[...] = jnp.transpose(second_ref[...])

    for sub in range(2):
        columns = slice(SUB * sub, SUB * (sub + 1))
        column_sums = 0.0
        start = pl.multiple_of(core * FF_SHARE + step * 512 + SUB * sub, SUB)
        in_bias = vector(in_bias_ref, start, SUB)
        for begin, end in PARTS:
            rows = slice(begin, end)
            hidden = jnp.dot(second_ref[rows, :], w_in_ref[:, columns], preferred_element_type=F32)
            hidden += in_bias
            grad_active = lax.dot_general(
                grad_ref[rows, :], w_back_ref[columns, :], NT, preferred_element_type=F32
            )
            below = 0.5 + 0.5 * lax.erf(hidden * 0.7071067811865476)
            active_ref[rows, columns] = (hidden * below).astype(BF16)
            slope = below + hidden * jnp.exp(hidden * hidden * -0.5) * 0.3989422804014327
            grad_hidden = (grad_active * slope).astype(BF16)
            grad_hidden_ref[rows, columns] = grad_hidden
            column_sums += jnp.sum(grad_hidden.astype(F32), axis=0, keepdims=True)
        sums_ref[:, columns] = jnp.broadcast_to(column_sums, (8, SUB))
        total = jnp.dot(
            turned_ref[...], grad_hidden_ref[:, columns], preferred_element_type=F32
        ).astype(BF16)
        grad_in_ref[:, columns] = total
        total = lax.dot_general(
            active_ref[:, columns], grad_ref[...], TN, preferred_element_type=F32
        ).astype(BF16)
        grad_back_ref[columns, :] = total

    back = lax.dot_general(
        grad_hidden_ref[...], w_in_ref[...], NT, preferred_element_type=F32
    )

    @pl.when(step == 0)
    def _():
        rows_ref[...] = back

    @pl.when(step == 1)
    def _():
        rows_ref[...] += back

    @pl.when(step == 2)
    def _():
        back_ref[...] = (rows_ref[...] + back).astype(BF16)
        for copy in copies:
            copy.wait()


def middle_part(
    place, mixed, other, x, w_out, out_bias, gain, bias, grads, w_fc1, fc1_bias, w_fc2
):
    tokens, ff_columns = whole((TOK, WIDTH)), pl.BlockSpec((TOK, 512), lambda i, place: (0, i))
    return pl.pallas_call(
        middle_kernel,
        grid_spec=pltpu.PrefetchScalarGridSpec(
            num_scalar_prefetch=1,
            grid=(3,),
            in_specs=[once(a.shape) for a in (mixed, other, x, w_out)]
            + [WHOLE] * 3
            + [once(a.shape) for a in grads]
            + [
                pl.BlockSpec((WIDTH, 512), lambda i, place: (0, place[0] * 3 + i)),
                WHOLE,
                pl.BlockSpec((512, WIDTH), lambda i, place: (place[0] * 3 + i, 0)),
            ],
            out_specs=[
                ANYWHERE,
                ANYWHERE,
                ff_columns,
                pl.BlockSpec((512, WIDTH), lambda i, place: (i, 0)),
                pl.BlockSpec((WIDTH, 512), lambda i, place: (0, i)),
                pl.BlockSpec((8, 512), lambda i, place: (0, i)),
                tokens,
            ],
            scratch_shapes=[
                pltpu.VMEM((TOK, WIDTH), F32),
                pltpu.VMEM((TOK, WIDTH), BF16),
                pltpu.VMEM((TOK, 512), BF16),
                pltpu.VMEM((TOK, WIDTH), BF16),
                pltpu.VMEM((WIDTH, TOK), BF16),
                pltpu.VMEM((TOK, WIDTH), F32),
                pltpu.SemaphoreType.DMA((2,)),
            ],
        ),
        out_shape=[
            pltpu.HBM((TOK, WIDTH), F32),
            pltpu.HBM((TOK, WIDTH), BF16),
            pltpu.HBM((TOK, FF_SHARE), BF16),
            pltpu.HBM((FF_SHARE, WIDTH), BF16),
            pltpu.HBM((WIDTH, FF_SHARE), BF16),
            jax.ShapeDtypeStruct((8, FF_SHARE), F32),
            pltpu.HBM((TOK, WIDTH), BF16),
        ],
        compiler_params=params(44),
        cost_estimate=cost(10.5e9, 30e6, 3e6),
        name="middle_part",
    )(
        place,
        far(mixed),
        other,
        far(x),
        far(w_out),
        out_bias,
        gain,
        bias,
        *grads,
        far(w_fc1),
        fc1_bias,
        far(w_fc2),
    )


def halves(columns, first):
    def index(i, place):
        return (jnp.where(i == first, place[0], 1 - place[0]), 0)

    return pl.BlockSpec((HALF, columns), index)


def product_kernel(place, active_ref, w_back_ref, *refs):
    sent_ref, own_ref = refs[-2:]
    product = jnp.dot(active_ref[...], w_back_ref[...], preferred_element_type=F32)

    @pl.when(pl.program_id(0) == 0)
    def _():
        sent_ref[...] = product.astype(BF16)

    @pl.when(pl.program_id(0) == 1)
    def _():
        own_ref[...] = product


def mlp_product(place, active, w_fc2, after):
    return pl.pallas_call(
        product_kernel,
        grid_spec=pltpu.PrefetchScalarGridSpec(
            num_scalar_prefetch=1,
            grid=(2,),
            in_specs=[
                halves(FF_SHARE, 1),
                pl.BlockSpec((FF_SHARE, WIDTH), lambda i, place: (place[0], 0)),
            ]
            + [ANYWHERE] * len(after),
            out_specs=[whole((HALF, WIDTH)), whole((HALF, WIDTH))],
        ),
        out_shape=[pltpu.HBM((HALF, WIDTH), BF16), pltpu.HBM((HALF, WIDTH), F32)],
        compiler_params=params(24),
        cost_estimate=cost(1, 1),
        name="mlp_product",
    )(place, far(active), far(w_fc2), *after)


def attend_back_kernel(
    place,
    segments_ref,
    other_segments_ref,
    second_ref,
    other_ref,
    middle_ref,
    top_ref,
    mixed_ref,
    w_out_ref,
    gain_ref,
    in_sums_ref,
    x_hbm,
    first_hbm,
    w_hbm,
    q_ref,
    k_ref,
    v_ref,
    lse_ref,
    *refs,
):
    slots, (grad_middle_ref, own_ref, sent_ref), refs = refs[:8], refs[8:11], refs[11:]
    (
        late_ref,
        branch_ref,
        grad_mixed_ref,
        packed_ref,
        scores_ref,
        sums_ref,
        x_ref,
        first_ref,
        w_ref,
        arrived,
        left,
    ) = refs
    pair, core = pl.program_id(0), place[0]
    copies = [
        pltpu.make_async_copy(x_hbm, x_ref, arrived.at[0]),
        pltpu.make_async_copy(first_hbm, first_ref, arrived.at[1]),
    ]
    for kind in range(3):
        start = pl.multiple_of(kind * WIDTH + core * SHARE, 128)
        copies.append(
            pltpu.make_async_copy(
                w_hbm.at[:, pl.ds(start, SHARE)],
                w_ref.at[:, pl.ds(kind * SHARE, SHARE)],
                arrived.at[2 + kind],
            )
        )

    def half_rows(which, begin, end):
        return pl.ds(pl.multiple_of(which * HALF + begin, 16), end - begin)

    @pl.when(pair == 0)
    def _():
        for copy in copies:
            copy.start()
        sums = [0.0, 0.0, 0.0, 0.0]
        for which in (core, 1 - core):
            for begin, end in ((0, 256), (256, HALF)):
                rows = half_rows(which, begin, end)
                grad = second_ref[rows, :].astype(F32) + other_ref[rows, :].astype(F32)
                normed, inverse = norm_rows(middle_ref[rows, :])
                product = grad * normed
                scaled = grad * vector(gain_ref)
                top = top_ref[rows, :].astype(F32)
                grad_middle = top + inverse * (
                    scaled
                    - jnp.mean(scaled, axis=-1, keepdims=True)
                    - normed * jnp.mean(product * vector(gain_ref), axis=-1, keepdims=True)
                )
                if which is core:
                    grad_middle_ref[begin:end, :] = grad_middle
                branch = grad_middle.astype(BF16)
                branch_ref[rows, :] = branch
                grad_mixed_ref[rows, :] = lax.dot_general(
                    branch, w_out_ref[...], NT, preferred_element_type=F32
                ).astype(BF16)
                for i, values in enumerate((branch.astype(F32), product, grad, top)):
                    sums[i] += jnp.sum(values, axis=0, keepdims=True)
        for i in range(4):
            sums_ref[8 * i : 8 * i + 8, :] = jnp.broadcast_to(sums[i], (8, WIDTH))
        total = lax.dot_general(mixed_ref[...], branch_ref[...], TN, preferred_element_type=F32)
        total = total.astype(BF16)
        for a in range(8):
            for b in range(2):
                for s in range(3):
                    row = WIDTH + 16 * (2 * a + b)
                    late_ref[row : row + 16, SHARE * s : SHARE * (s + 1)] = total[
                        48 * a + 16 * s : 48 * a + 16 * s + 16, SHARE * b : SHARE * (b + 1)
                    ]

    attention_back(
        pair,
        small_comes_first(place, segments_ref, other_segments_ref),
        q_ref,
        k_ref,
        v_ref,
        grad_mixed_ref,
        mixed_ref,
        lse_ref,
        packed_ref,
        scores_ref,
    )

    @pl.when(pair == 2)
    def _():
        for copy in copies:
            copy.wait()
        late_ref[:WIDTH, : 3 * SHARE] = lax.dot_general(
            first_ref[...], packed_ref[...], TN, preferred_element_type=F32
        ).astype(BF16)
        gain, bias, packed = 0.0, 0.0, 0.0
        for which in (core, 1 - core):
            for begin, end in ((0, 256), (256, HALF)):
                rows = half_rows(which, begin, end)
                grad = packed_ref[rows, :]
                part = lax.dot_general(grad, w_ref[...], NT, preferred_element_type=F32)
                if which is core:
                    own_ref[begin:end, :] = part
                else:
                    sent_ref[begin:end, :] = part.astype(BF16)
                gain += jnp.sum(
                    part * norm_rows(x_ref[rows, :].astype(F32))[0], axis=0, keepdims=True
                )
                bias += jnp.sum(part, axis=0, keepdims=True)
                packed += jnp.sum(grad.astype(F32), axis=0, keepdims=True)
        pieces = [sums_ref[8 * i : 8 * i + 1, :] for i in range(3)]
        pieces += [gain, bias, sums_ref[24:25, :]]
        pieces += [packed[:, :SHARE], packed[:, 2 * SHARE :], in_sums_ref[:1, :]]
        late_ref[:, 3 * SHARE :] = jnp.zeros((16 * PEERS, 128), BF16)
        at = 0
        for piece in pieces:
            for tile in range(piece.shape[1] // 128):
                late_ref[16 * at : 16 * at + 16, 3 * SHARE :] = jnp.broadcast_to(
                    piece[:, 128 * tile : 128 * (tile + 1)], (16, 128)
                ).astype(BF16)
                at += 1
        parts = []
        for side in range(2):
            for hop in range(4):
                start = pl.multiple_of(256 * lax.rem(place[2 + side] + hop, 4), 256)
                parts.append(
                    pltpu.make_async_copy(
                        late_ref.at[pl.ds(start, 256), pl.ds(LATE_HALF * side, LATE_HALF)],
                        slots[4 * side + hop],
                        left.at[4 * side + hop],
                    )
                )
        for copy in parts:
            copy.start()
        for copy in parts:
            copy.wait()


def attend_back(
    place, segments, second, other, middle, top, mixed, w_out, gain, in_sums, x, first, w_qkv, heads
):
    tokens, half = once((TOK, WIDTH)), whole((HALF, WIDTH))
    return pl.pallas_call(
        attend_back_kernel,
        grid_spec=pltpu.PrefetchScalarGridSpec(
            num_scalar_prefetch=1,
            grid=(3,),
            in_specs=[
                SCALARS,
                SCALARS,
                tokens,
                tokens,
                tokens,
                tokens,
                once((TOK, SHARE)),
                once((SHARE, WIDTH), lambda i, place: (place[0], 0)),
                WHOLE,
                WHOLE,
                ANYWHERE,
                ANYWHERE,
                ANYWHERE,
            ]
            + [block()] * 4,
            out_specs=[ANYWHERE] * 8 + [half, half, half],
            scratch_shapes=[
                pltpu.VMEM((16 * PEERS, LATE), BF16),
                pltpu.VMEM((TOK, WIDTH), BF16),
                pltpu.VMEM((TOK, SHARE), BF16),
                pltpu.VMEM((TOK, 3 * SHARE), BF16),
                pltpu.VMEM((2, BIG_Q, BIG_K), BF16),
                pltpu.VMEM((32, WIDTH), F32),
                pltpu.VMEM((TOK, WIDTH), BF16),
                pltpu.VMEM((TOK, WIDTH), BF16),
                pltpu.VMEM((WIDTH, 3 * SHARE), BF16),
                pltpu.SemaphoreType.DMA((5,)),
                pltpu.SemaphoreType.DMA((8,)),
            ],
        ),
        out_shape=[pltpu.HBM((256, LATE_HALF), BF16)] * 8
        + [
            pltpu.HBM((HALF, WIDTH), F32),
            pltpu.HBM((HALF, WIDTH), F32),
            pltpu.HBM((HALF, WIDTH), BF16),
        ],
        compiler_params=params(46),
        cost_estimate=cost(1, 1),
        name="attend_back",
    )(
        place,
        *segments,
        far(second),
        other,
        far(middle),
        far(top),
        far(mixed),
        far(w_out),
        gain,
        in_sums,
        far(x),
        far(first),
        far(w_qkv),
        *(far(a) for a in heads),
    )


def small_call(kernel, name, arrays, shapes, place, scratch=(), after=()):
    count = 1 + len(arrays)

    def body(*refs):
        kernel(*refs[:count], *refs[count + len(after) :])

    return pl.pallas_call(
        body,
        in_specs=[SCALARS] + [WHOLE] * len(arrays) + [ANYWHERE] * len(after),
        out_specs=[WHOLE] * len(shapes),
        out_shape=[jax.ShapeDtypeStruct(shape, BF16) for shape in shapes],
        scratch_shapes=list(scratch),
        compiler_params=params(16),
        cost_estimate=cost(1, 1),
        name=name,
    )(place, *arrays, *after)


def total_of(refs):
    total = refs[0][...].astype(F32)
    for ref in refs[1:]:
        total += ref[...].astype(F32)
    return total.astype(BF16)


def turn(place, axis, hop, size):
    return pl.ds(pl.multiple_of(size * lax.rem(place[axis] + hop, 4), size), size)


def sum_first_kernel(place, *refs):
    scratch = refs[-1]
    for side in range(2):
        scratch[...] = total_of(refs[4 * side : 4 * side + 4])
        for hop in range(4):
            refs[8 + 4 * side + hop][...] = scratch[turn(place, 3 - side, hop, 64), :]


def sum_second_kernel(place, *refs):
    scratch = refs[-1]
    for side in range(2):
        columns = slice(LATE_HALF * side, LATE_HALF * (side + 1))
        scratch[:, columns] = total_of(refs[4 * side : 4 * side + 4])
    for hop in range(4):
        refs[8 + hop][...] = scratch[turn(place, 4, hop, 16), :]


def sum_third_kernel(place, *refs):
    refs[-1][...] = total_of(refs[:4])


def join_third_kernel(place, *refs):
    for hop in range(4):
        rows = turn(place, 4, 4 - hop, 16)
        for side in range(2):
            columns = slice(LATE_HALF * side, LATE_HALF * (side + 1))
            refs[4 + side][rows, :] = refs[hop][:, columns]


def join_second_kernel(place, *refs):
    for side in range(2):
        for hop in range(4):
            refs[8 + side][turn(place, 3 - side, 4 - hop, 64), :] = refs[4 * side + hop][...]


def join_first_kernel(place, *refs):
    for side in range(2):
        columns = slice(LATE_HALF * side, LATE_HALF * (side + 1))
        for hop in range(4):
            refs[8][turn(place, 2 + side, 4 - hop, 256), columns] = refs[4 * side + hop][...]


def around(parts, axis):
    return [parts[0]] + [
        lax.ppermute(parts[hop], axis, [(i, (i + hop) % 4) for i in range(4)]) for hop in (1, 2, 3)
    ]


def sum_late(parts, place, first, second):
    depth = ("zh", "zl")
    parts = small_call(
        sum_first_kernel,
        "sum_first",
        parts,
        [(64, LATE_HALF)] * 8,
        place,
        [pltpu.VMEM((256, LATE_HALF), BF16)],
    )
    parts = around(parts[:4], "y") + around(parts[4:], "x")
    parts = small_call(
        sum_second_kernel,
        "sum_second",
        parts,
        [(16, LATE)] * 4,
        place,
        [pltpu.VMEM((64, LATE), BF16)],
        first,
    )
    (share,) = small_call(
        sum_third_kernel, "sum_third", around(parts, depth), [(16, LATE)], place
    )
    one, two = small_call(
        join_third_kernel, "join_third", around([share] * 4, depth), [(64, LATE_HALF)] * 2, place
    )
    parts = around([one] * 4, "y") + around([two] * 4, "x")
    one, two = small_call(
        join_second_kernel, "join_second", parts, [(256, LATE_HALF)] * 2, place, after=second
    )
    return around([one] * 4, "x") + around([two] * 4, "y")


def join_late(parts, place):
    return small_call(join_first_kernel, "join_first", parts, [(16 * PEERS, LATE)], place)[0]


def wait_kernel(*refs):
    pass


def later(array, after):
    return pl.pallas_call(
        wait_kernel,
        in_specs=[ANYWHERE, ANYWHERE],
        out_specs=ANYWHERE,
        out_shape=pltpu.HBM(array.shape, array.dtype),
        input_output_aliases={0: 0},
        cost_estimate=cost(1, 1),
        name="later",
    )(far(array), far(after))


def widen_kernel(
    place,
    back_ref,
    in_ref,
    mine_ref,
    other_ref,
    mine_small_ref,
    other_small_ref,
    total_back_ref,
    total_in_ref,
    packed_ref,
    out_ref,
    in_bias_ref,
    q_bias_ref,
    v_bias_ref,
    *vector_refs,
):
    step, first = pl.program_id(0), place[0] == 0
    total_back_ref[...] = back_ref[...].astype(F32)
    total_in_ref[...] = in_ref[...].astype(F32)

    def pick(side, mine_ref, other_ref, rows, columns):
        mine, other = mine_ref[rows, columns].astype(F32), other_ref[rows, columns].astype(F32)
        return jnp.where(first if side == 0 else jnp.logical_not(first), mine, other)

    @pl.when(step < 3)
    def _():
        for side in range(2):
            for kind in range(3):
                at = SHARE * (2 * kind + side)
                packed_ref[:, at : at + SHARE] = pick(
                    side, mine_ref, other_ref, slice(0, 256), slice(SHARE * kind, SHARE * (kind + 1))
                )

    @pl.when(step == 3)
    def _():
        for side in range(2):
            for a in range(8):
                for b in range(2):
                    row = 16 * (2 * a + b)
                    for s in range(3):
                        at = SHARE * side + 48 * a + 16 * s
                        out_ref[at : at + 16, SHARE * b : SHARE * (b + 1)] = pick(
                            side,
                            mine_ref,
                            other_ref,
                            slice(row, row + 16),
                            slice(SHARE * s, SHARE * (s + 1)),
                        )

    @pl.when(step == 0)
    def _():
        def piece(side, at):
            rows = slice(16 * at, 16 * at + 16)
            return pick(side, mine_small_ref, other_small_ref, rows, slice(0, 128))[:1]

        def put(ref, tile, value):
            ref[128 * tile : 128 * (tile + 1)] = value.reshape(128)

        for tile in range(6):
            for at in range(6):
                value = piece(0, 6 * at + tile)
                if at in (3, 4):
                    value += piece(1, 6 * at + tile)
                put(vector_refs[at], tile, value)
        for side in range(2):
            for tile in range(3):
                put(q_bias_ref, 3 * side + tile, piece(side, 36 + tile))
                put(v_bias_ref, 3 * side + tile, piece(side, 39 + tile))
            for tile in range(12):
                put(in_bias_ref, 12 * side + tile, piece(side, 42 + tile))


def widen(place, early, late, late_other):
    rows = pl.BlockSpec((256, LATE), lambda i, place: (i, 0))
    small = pl.BlockSpec((16 * PEERS, 128), lambda i, place: (0, 9))
    vectors = [jax.ShapeDtypeStruct((2 * FF_SHARE,), F32)] + [jax.ShapeDtypeStruct((WIDTH,), F32)] * 8
    return pl.pallas_call(
        widen_kernel,
        grid_spec=pltpu.PrefetchScalarGridSpec(
            num_scalar_prefetch=1,
            grid=(4,),
            in_specs=[
                pl.BlockSpec((512, WIDTH), lambda i, place: (jnp.minimum(i, 2), 0)),
                pl.BlockSpec((WIDTH, 512), lambda i, place: (0, jnp.minimum(i, 2))),
                rows,
                rows,
                small,
                small,
            ],
            out_specs=[
                pl.BlockSpec((512, WIDTH), lambda i, place: (3 * place[0] + jnp.minimum(i, 2), 0)),
                pl.BlockSpec((WIDTH, 512), lambda i, place: (0, 3 * place[0] + jnp.minimum(i, 2))),
                pl.BlockSpec((256, 3 * WIDTH), lambda i, place: (jnp.minimum(i, 2), 0)),
                whole((WIDTH, WIDTH)),
            ]
            + [WHOLE] * 9,
        ),
        out_shape=[
            pltpu.HBM((2 * FF_SHARE, WIDTH), F32),
            pltpu.HBM((WIDTH, 2 * FF_SHARE), F32),
            pltpu.HBM((WIDTH, 3 * WIDTH), F32),
            pltpu.HBM((WIDTH, WIDTH), F32),
        ]
        + vectors,
        compiler_params=params(32),
        cost_estimate=cost(0, 100e6),
        name="widen",
    )(place, *(far(a) for a in (*early, late, late_other, late, late_other)))


def widen_rest_kernel(place, back_ref, in_ref, same_back_ref, same_in_ref, total_back_ref, total_in_ref):
    total_back_ref[...] = back_ref[...].astype(F32)
    total_in_ref[...] = in_ref[...].astype(F32)


def widen_rest(place, early, totals):
    return pl.pallas_call(
        widen_rest_kernel,
        grid_spec=pltpu.PrefetchScalarGridSpec(
            num_scalar_prefetch=1,
            grid=(3,),
            in_specs=[
                pl.BlockSpec((512, WIDTH), lambda i, place: (i, 0)),
                pl.BlockSpec((WIDTH, 512), lambda i, place: (0, i)),
                ANYWHERE,
                ANYWHERE,
            ],
            out_specs=[
                pl.BlockSpec((512, WIDTH), lambda i, place: (3 - 3 * place[0] + i, 0)),
                pl.BlockSpec((WIDTH, 512), lambda i, place: (0, 3 - 3 * place[0] + i)),
            ],
        ),
        out_shape=[
            pltpu.HBM((2 * FF_SHARE, WIDTH), F32),
            pltpu.HBM((WIDTH, 2 * FF_SHARE), F32),
        ],
        input_output_aliases={3: 0, 4: 1},
        compiler_params=params(24),
        cost_estimate=cost(0, 14e6),
        name="widen_rest",
    )(place, *early, *(far(a) for a in totals))


def norm_back(grad_normed, normed, inverse):
    return inverse * (
        grad_normed
        - jnp.mean(grad_normed, axis=-1, keepdims=True)
        - normed * jnp.mean(grad_normed * normed, axis=-1, keepdims=True)
    )


def other_core(values):
    return lax.ppermute(values, "c", [(0, 1), (1, 0)])


def swap_home(values):
    return lax.ppermute(values, ("c", "zl"), [(1, 2), (2, 1)])


def from_host(values):
    return lax.ppermute(values, ("c", "zl"), [(0, 2), (3, 1)])


def from_guest(values):
    return lax.ppermute(values, ("c", "zl"), [(2, 0), (1, 3)])


def body(
    inputs,
    segments,
    cotangent,
    ln1_gain,
    ln1_bias,
    w_qkv,
    q_bias,
    v_bias,
    w_out,
    out_bias,
    ln2_gain,
    ln2_bias,
    w_fc1,
    fc1_bias,
    w_fc2,
    fc2_bias,
):
    core = lax.axis_index("c")
    home = core == lax.axis_index("zl")

    def half(array, which):
        return lax.dynamic_slice_in_dim(array, which * HALF, HALF, 0)

    tokens, top = inputs[0], cotangent[0]
    swapped = swap_home(tokens)
    rows = (tokens, swapped, from_host(tokens), from_guest(swapped))
    images = (segments, other_core(segments))
    depth = 2 * lax.axis_index("zh") + lax.axis_index("zl")
    place = [core, home, lax.axis_index("x"), lax.axis_index("y"), depth]
    place = jnp.stack([index.astype(jnp.int32) for index in place])

    sent = jnp.concatenate([top, swapped[: HALF - REAL]], axis=0)
    top_swapped = swap_home(sent)

    x_all, first_in, query, key, value, mixed, lse = attend(
        place, images, rows, ln1_gain, ln1_bias, w_qkv, q_bias, v_bias
    )
    top_swapped = later(top_swapped, mixed)
    tops = (top, top_swapped, from_host(top), from_guest(top_swapped))
    middle, grad_top, active, grad_back, grad_in, in_sums, second = middle_part(
        place,
        mixed,
        other_core(mixed),
        x_all,
        w_out,
        out_bias,
        ln2_gain,
        ln2_bias,
        tops,
        w_fc1,
        fc1_bias,
        w_fc2,
    )
    early = lax.psum((grad_back, grad_in), CHIPS)
    *late, grad_middle, first_part, first_sent = attend_back(
        place,
        images,
        second,
        other_core(second),
        middle,
        grad_top,
        mixed,
        w_out,
        ln2_gain,
        in_sums,
        x_all,
        first_in,
        w_qkv,
        (query, key, value, lse),
    )
    late = around(late[:4], "x") + around(late[4:], "y")
    product_sent, product = mlp_product(place, active, w_fc2, (late[5],))
    result = half(middle, core) + product + other_core(product_sent).astype(F32) + fc2_bias
    result = result.astype(BF16)
    output = jnp.where(home, result, swap_home(result))[None, :REAL]

    grad_first_in = first_part + other_core(first_sent).astype(F32)
    normed_one, inverse_one = norm_rows(half(x_all, core).astype(F32))
    grad_input = grad_middle + norm_back(grad_first_in * ln1_gain, normed_one, inverse_one)
    grad_input = grad_input.astype(BF16)
    input_grad = jnp.where(home, grad_input, swap_home(grad_input))[None, :REAL]

    late = sum_late(late, place, (result, grad_input), (output, input_grad))
    early_other = [other_core(a) for a in early]
    late = join_late(late, place)
    total_back, total_in, total_packed, total_out, in_bias, total_q_bias, total_v_bias, *vectors = widen(
        place, early, late, other_core(late)
    )
    total_back, total_in = widen_rest(place, early_other, (total_back, total_in))
    return (
        output,
        input_grad,
        vectors[3],
        vectors[4],
        total_packed,
        total_q_bias,
        total_v_bias,
        total_out,
        vectors[0],
        vectors[1],
        vectors[2],
        total_in,
        in_bias,
        total_back,
        vectors[5],
    )


def solution(mesh):
    fine = Mesh(mesh.devices.reshape(4, 4, 2, 2, 2), ("x", "y", "zh", "c", "zl"))
    tokens = P(ROWS, "zl", None)
    return jax.shard_map(
        body,
        mesh=fine,
        in_specs=(tokens, P(ROWS, None), tokens) + (P(),) * 13,
        out_specs=(tokens, tokens) + (P(),) * 13,
        check_vma=False,
    )
```
